32 devices in a mesh: rep: 4 (over x, core), shard: 8 (over z, y).
Axes of the slice: x: 2, y: 2, z: 4, core: 2. Of those that a mesh axis runs over, the one named last changes fastest.
Arguments:
- tokens_in: bfloat16 [64, 1024, 768], P(('rep', 'shard')), may hold values from -6 to 6
- cotangent: bfloat16 [64, 1024, 768], P(('rep', 'shard')), may hold values from -6 to 6
- segment_ids: int32 [64, 1024], P(('rep', 'shard')), may hold values from 0 to 1023, as said below
- block_map: int32 [64, 2, 8], P(('rep', 'shard')), may hold values from 0 to 1, as said below
- timesteps: int32 [64], P(('rep', 'shard')), may hold values from 0 to 1023
- step_table: bfloat16 [1024, 768], P('shard'), may hold values from -6 to 6
- ln1_gain: bfloat16 [768], P('shard'), may hold values from 0.5 to 1.5
- ln1_bias: bfloat16 [768], P('shard'), may hold values from -3 to 3
- w_query: bfloat16 [768, 768], P('shard'), may hold values from -0.21875 to 0.21875
- b_query: bfloat16 [768], P('shard'), may hold values from -3 to 3
- w_key: bfloat16 [768, 768], P('shard'), may hold values from -0.21875 to 0.21875
- w_value: bfloat16 [768, 768], P('shard'), may hold values from -0.21875 to 0.21875
- b_value: bfloat16 [768], P('shard'), may hold values from -3 to 3
- w_out: bfloat16 [768, 768], P('shard'), may hold values from -0.875 to 0.875
- b_out: bfloat16 [768], P('shard'), may hold values from -3 to 3
- ln2_gain: bfloat16 [768], P('shard'), may hold values from 0.5 to 1.5
- ln2_bias: bfloat16 [768], P('shard'), may hold values from -3 to 3
- w_up: bfloat16 [768, 3072], P('shard'), may hold values from -0.21875 to 0.21875
- b_up: bfloat16 [3072], P('shard'), may hold values from -3 to 3
- w_down: bfloat16 [3072, 768], P('shard'), may hold values from -0.109375 to 0.109375
- b_down: bfloat16 [768], P('shard'), may hold values from -3 to 3
Outputs:
- output: bfloat16 [64, 1024, 768], P(('rep', 'shard'))
- grad_input: bfloat16 [64, 1024, 768], P(('rep', 'shard'))
- grad_step_table: float32 [1024, 768], P('shard')
- grad_ln1_gain: float32 [768], P('shard')
- grad_ln1_bias: float32 [768], P('shard')
- grad_w_query: float32 [768, 768], P('shard')
- grad_b_query: float32 [768], P('shard')
- grad_w_key: float32 [768, 768], P('shard')
- grad_w_value: float32 [768, 768], P('shard')
- grad_b_value: float32 [768], P('shard')
- grad_w_out: float32 [768, 768], P('shard')
- grad_b_out: float32 [768], P('shard')
- grad_ln2_gain: float32 [768], P('shard')
- grad_ln2_bias: float32 [768], P('shard')
- grad_w_up: float32 [768, 3072], P('shard')
- grad_b_up: float32 [3072], P('shard')
- grad_w_down: float32 [3072, 768], P('shard')
- grad_b_down: float32 [768], P('shard')
The draws below stay inside these ranges and needn't reach their ends.
Inputs may be any that keep to these rules, and one draw needn't show every extreme that they name: `segment_ids`: in each sequence the ids start at 0 and never fall; a document is a run of positions with one id. block_map[s, i, j] is 1 exactly where query block i (rows i * 512 onward) and key block j (rows j * 128 onward) of sequence s hold tokens of a common document.
All inputs are finite; a program needn't handle non-finite values.
Results may differ from the reference program's by a relative error of at most 0.013.
Values may be sent and summed in bfloat16 or wider, within the bound.
No kernel may reach another device: no remote copies, remote signals or barrier semaphores. Data moves between devices by JAX's collectives and lax.ppermute only.
A program may use at most 320 MiB of HBM per device.

```python
import jax
import jax.numpy as jnp
from jax import lax

D = 768
HEADS = 12
HD = 64
FF = 3072
NSTEPS = 1024
SEQ = 1024
QBLK = 512
KBLK = 128
NSEQS = 64
NQB = 2
NKB = 8


def document_ids(key):
    base_key = jax.random.fold_in(key, 7)
    rate_key, flag_key = jax.random.split(base_key)
    pick_key = jax.random.fold_in(base_key, 11)
    rates = jax.random.randint(rate_key, (NSEQS, 1), 2, 10)
    chosen = jax.random.randint(pick_key, (), 0, NSEQS)
    rows = lax.broadcasted_iota(jnp.int32, (NSEQS, 1), 0)
    rates = jnp.where(rows == chosen, 0, rates)
    noise = jax.random.randint(flag_key, (NSEQS, SEQ), 0, 1 << 12)
    flags = jnp.remainder(noise, jnp.left_shift(jnp.ones_like(rates), rates)) == 0
    flags = flags & (lax.broadcasted_iota(jnp.int32, (NSEQS, SEQ), 1) > 0)
    return jnp.cumsum(flags.astype(jnp.int32), axis=1).astype(jnp.int32)


def draw_segment_ids(key, part):
    return document_ids(key)


def draw_block_map(key, part):
    ident = document_ids(key)
    query_first = ident.reshape(NSEQS, NQB, QBLK)[:, :, 0]
    query_last = ident.reshape(NSEQS, NQB, QBLK)[:, :, QBLK - 1]
    key_first = ident.reshape(NSEQS, NKB, KBLK)[:, :, 0]
    key_last = ident.reshape(NSEQS, NKB, KBLK)[:, :, KBLK - 1]
    linked = (query_first[:, :, None] <= key_last[:, None, :]) & (key_first[:, None, :] <= query_last[:, :, None])
    return linked.astype(jnp.int32)


def with_ends(drawn, own_key, low, high):
    spot = [jax.random.randint(jax.random.fold_in(own_key, axis), (), 0, length) for axis, length in enumerate(drawn.shape)]
    widest = drawn.shape.index(max(drawn.shape))
    next_to = spot[:widest] + [(spot[widest] + 1) % drawn.shape[widest]] + spot[widest + 1:]
    return drawn.at[tuple(spot)].set(low).at[tuple(next_to)].set(high)


def block_scale(stream_key, extent, cuts, least, top_value):
    loudness = 1.0
    for dim, shards_of in cuts:
        draws = jax.random.uniform(jax.random.fold_in(jax.random.fold_in(stream_key, 6), dim), (shards_of,), jnp.float32, least / len(cuts), top_value / len(cuts))
        loudness = loudness * jnp.repeat(jnp.exp(draws), extent[dim] // shards_of).reshape((-1,) + (1,) * (len(extent) - 1 - dim))
    return loudness


def bell_draw(stream_key, dims, spread, most, cuts=(), dtype=jnp.bfloat16):
    gain = block_scale(stream_key, dims, cuts, -0.22, 0.18) if cuts else 1.0
    entries = jax.random.normal(stream_key, dims, jnp.float32) * spread * gain
    return jnp.minimum(jnp.maximum(entries, -most), most).astype(dtype)


def setup_inputs(seed: int = 0) -> dict:
    splits = jax.random.split(jax.random.key(seed), 22)
    return {
        "tokens_in": bell_draw(splits[0], (NSEQS, SEQ, D), 1.0, 6.0, ((0, 32),)),
        "cotangent": bell_draw(splits[1], (NSEQS, SEQ, D), 1.0, 6.0, ((0, 32),)),
        "segment_ids": draw_segment_ids(jax.random.fold_in(splits[21], 71), 0),
        "block_map": draw_block_map(jax.random.fold_in(splits[21], 71), 0),
        "timesteps": with_ends(jax.random.randint(splits[4], (NSEQS,), 0, NSTEPS), jax.random.fold_in(splits[4], 1), 0, NSTEPS - 1).astype(jnp.int32),
        "step_table": bell_draw(splits[5], (NSTEPS, D), 1.0, 6.0, ((0, 8),)),
        "ln1_gain": jnp.clip(1.0 + 0.1 * jax.random.normal(splits[6], (D,), jnp.float32), 0.5, 1.5).astype(jnp.bfloat16),
        "ln1_bias": bell_draw(splits[7], (D,), 0.3, 3.0, ((0, 8),)),
        "w_query": bell_draw(splits[8], (D, D), D ** -0.5, 0.21875, ((0, 8),)),
        "b_query": bell_draw(splits[9], (D,), 0.5, 3.0, ((0, 8),)),
        "w_key": bell_draw(splits[10], (D, D), D ** -0.5, 0.21875, ((0, 8),)),
        "w_value": bell_draw(splits[11], (D, D), D ** -0.5, 0.21875, ((0, 8),)),
        "b_value": bell_draw(splits[12], (D,), 0.5, 3.0, ((0, 8),)),
        "w_out": bell_draw(splits[13], (D, D), (D // 16) ** -0.5, 0.875, ((0, 8),)),
        "b_out": bell_draw(splits[14], (D,), 0.5, 3.0, ((0, 8),)),
        "ln2_gain": jnp.clip(1.0 + 0.1 * jax.random.normal(splits[15], (D,), jnp.float32), 0.5, 1.5).astype(jnp.bfloat16),
        "ln2_bias": bell_draw(splits[16], (D,), 0.3, 3.0, ((0, 8),)),
        "w_up": bell_draw(splits[17], (D, FF), D ** -0.5, 0.21875, ((0, 8),)),
        "b_up": bell_draw(splits[18], (FF,), 0.5, 3.0, ((0, 8),)),
        "w_down": bell_draw(splits[19], (FF, D), FF ** -0.5, 0.109375, ((0, 8),)),
        "b_down": bell_draw(splits[20], (D,), 0.5, 3.0, ((0, 8),)),
    }


@jax.custom_vjp
def low(v):
    return lax.optimization_barrier(v.astype(jnp.bfloat16)).astype(jnp.float32)

@jax.custom_vjp
def low_back(v):
    return v

def low_keep(v):
    return (low(v), None)

def low_pass(kept, grad):
    return (grad,)

def back_keep(v):
    return (v, None)

def back_low(kept, grad):
    return (low(grad),)
low.defvjp(low_keep, low_pass)
low_back.defvjp(back_keep, back_low)
epsilon = 1e-05
highest = lax.Precision.HIGHEST

def gelu_exact(values):
    return jax.nn.gelu(values, approximate=False)

def normalize(values, gain_row, shift_row):
    center = values - lax.optimization_barrier(jnp.mean(values, axis=-1, keepdims=True))
    inv_dev = lax.rsqrt(lax.optimization_barrier(jnp.mean(center * center, axis=-1, keepdims=True)) + epsilon)
    return center * inv_dev * gain_row + shift_row

def product(left, right):
    return jnp.dot(left, right, precision=highest, preferred_element_type=jnp.float32)

def attend(query_rows, key_rows, value_rows, seg_row, map_row):
    seq_len = query_rows.shape[0]
    query_heads = query_rows.reshape(seq_len // QBLK, QBLK, HEADS, HD)
    key_heads = key_rows.reshape(seq_len, HEADS, HD)
    value_heads = value_rows.reshape(seq_len, HEADS, HD)
    seg_blocks = seg_row.reshape(seq_len // QBLK, QBLK)
    allowed = jnp.repeat(map_row, KBLK, axis=1)

    def one_block(inputs):
        query_block, seg_block, allowed_row = inputs
        raw_scores = low_back(jnp.einsum('qhd,khd->hqk', query_block, key_heads, precision=highest) * HD ** (-0.5))
        key_mask = (seg_block[:, None] == seg_row[None, :]) & (allowed_row[None, :] == 1)
        masked = jnp.where(key_mask[None], raw_scores, -1e+30)
        row_top = lax.optimization_barrier(jnp.max(masked, axis=-1, keepdims=True))
        row_total = lax.optimization_barrier(jnp.sum(jnp.where(key_mask[None], jnp.exp(masked - row_top), 0.0), axis=-1, keepdims=True))
        log_total = row_top + jnp.log(row_total)
        attn_prob = low(jnp.where(key_mask[None], jnp.exp(masked - log_total), 0.0))
        return jnp.einsum('hqk,khd->qhd', attn_prob, value_heads, precision=highest)
    mixed = lax.map(jax.checkpoint(one_block), (query_heads, seg_blocks, allowed))
    return mixed.reshape(seq_len, HEADS * HD)

def sequence(weights, tokens_row, seg_row, map_row, time_step):
    step_table, ln1_gain, ln1_bias, w_query, b_query, w_key, w_value, b_value, w_out, b_out, ln2_gain, ln2_bias, w_up, b_up, w_down, b_down = weights
    base = tokens_row + step_table[time_step][None, :]
    hidden1 = low(normalize(base, ln1_gain, ln1_bias))
    query_rows = low_back(low(product(hidden1, w_query) + b_query))
    key_rows = low_back(low(product(hidden1, w_key)))
    value_rows = low_back(low(product(hidden1, w_value) + b_value))
    mixed = low_back(low(attend(query_rows, key_rows, value_rows, seg_row, map_row)))
    middle = base + low_back(product(mixed, w_out) + b_out)
    hidden2 = low(normalize(middle, ln2_gain, ln2_bias))
    up_rows = low_back(product(hidden2, w_up) + b_up)
    active = low(gelu_exact(up_rows))
    return middle + low_back(product(active, w_down) + b_down)

def forward(weights, tokens, segment_ids, block_map, timesteps):

    def visit(running, inputs):
        return (running, jax.checkpoint(sequence)(weights, inputs[0], inputs[1], inputs[2], inputs[3]))
    unused, outputs = lax.scan(visit, jnp.zeros((), jnp.float32), (tokens, segment_ids, block_map, timesteps))
    return outputs

def reference(tokens_in, cotangent, segment_ids, block_map, timesteps, step_table, ln1_gain, ln1_bias, w_query, b_query, w_key, w_value, b_value, w_out, b_out, ln2_gain, ln2_bias, w_up, b_up, w_down, b_down):
    weights = tuple((member.astype(jnp.float32) for member in (step_table, ln1_gain, ln1_bias, w_query, b_query, w_key, w_value, b_value, w_out, b_out, ln2_gain, ln2_bias, w_up, b_up, w_down, b_down)))

    def bound(weight_set, token_set):
        return forward(weight_set, token_set, segment_ids, block_map, timesteps)
    outputs, pullback = jax.vjp(bound, weights, tokens_in.astype(jnp.float32))
    grads, grad_tokens = pullback(cotangent.astype(jnp.float32))
    return (outputs.astype(jnp.bfloat16), grad_tokens.astype(jnp.bfloat16), grads[0], grads[1], grads[2], grads[3], grads[4], grads[5], grads[6], grads[7], grads[8], grads[9], grads[10], grads[11], grads[12], grads[13], grads[14], grads[15])
```

```python
import jax
import jax.numpy as jnp
from jax import lax
from jax.experimental import pallas as pl
from jax.experimental.pallas import tpu as pltpu
from jax.sharding import Mesh, PartitionSpec as P

HEADS = 12
HD = 64
QT = 256
KT = 256
RT = 512
FC = 512
EPS = 1e-05
NEG = -1e30
f32 = jnp.float32
bf16 = jnp.bfloat16
VMEM_BYTES = 60 * 1000 * 1024


def dg(x, y, cx, cy):
    return lax.dot_general(x, y, (((cx,), (cy,)), ((), ())), preferred_element_type=f32)


def normalize(values):
    center = values - jnp.mean(values, axis=-1, keepdims=True)
    inv_dev = lax.rsqrt(jnp.mean(center * center, axis=-1, keepdims=True) + EPS)
    return center * inv_dev, inv_dev


def norm_back(grad_hidden, normed, inv_dev, gain_row):
    grad_normed = grad_hidden * gain_row
    return inv_dev * (
        grad_normed
        - jnp.mean(grad_normed, axis=-1, keepdims=True)
        - normed * jnp.mean(grad_normed * normed, axis=-1, keepdims=True)
    )


def col_sum(values):
    return jnp.sum(values, axis=0, keepdims=True)


def gelu_parts(x):
    density = jnp.exp(-0.5 * x * x)
    t = 1.0 / (1.0 + 0.2316418882 * jnp.abs(x))
    poly = t * (0.127414796 + t * (-0.142248368 + t * (0.7107068705 + t * (-0.7265760135 + t * 0.5307027145))))
    tail = density * poly
    cdf = jnp.where(x >= 0.0, 1.0 - tail, tail)
    return x * cdf, cdf + x * (density * 0.3989422804014327)


def place_halves(mine, other, full, core, sems):
    half = mine.shape[1]
    at = pl.multiple_of(core * half, 128)
    rest = pl.multiple_of((1 - core) * half, 128)
    return (
        pltpu.make_async_copy(mine, full.at[:, pl.ds(at, half)], sems.at[0]),
        pltpu.make_async_copy(other, full.at[:, pl.ds(rest, half)], sems.at[1]),
    )


def params(**kw):
    return pltpu.CompilerParams(vmem_limit_bytes=VMEM_BYTES, **kw)


def qkv_kernel(core_ref, tok_ref, row_ref, vec_ref, bias_ref, mine_ref, other_ref,
               q_ref, k_ref, v_ref, qT_ref, kT_ref, vT_ref, w_ref, sems):
    @pl.when((pl.program_id(0) == 0) & (pl.program_id(1) == 0))
    def _():
        copies = place_halves(mine_ref, other_ref, w_ref, core_ref[0], sems)
        for c in copies:
            c.start()
        for c in copies:
            c.wait()

    width = tok_ref.shape[2]
    base = tok_ref[0].astype(f32) + row_ref[0]
    normed, unused = normalize(base)
    hidden = (normed * vec_ref[0:1, :] + vec_ref[1:2, :]).astype(bf16)
    scale = HD ** (-0.5)
    for n, (out, outT) in enumerate(((q_ref, qT_ref), (k_ref, kT_ref), (v_ref, vT_ref))):
        cols = slice(n * width, (n + 1) * width)
        rows = (dg(hidden, w_ref[:, cols], 1, 0) + bias_ref[:, cols]).astype(bf16)
        scaled = (rows.astype(f32) * scale).astype(bf16)
        out[0] = scaled if n == 0 else rows
        outT[0] = (rows if n == 2 else scaled).T


def qkv_call(core, tokens, trow, vec, bias, mine, other):
    B, S, D = tokens.shape
    row = pl.BlockSpec((1, RT, D), lambda b, i: (b, i, 0))
    col = pl.BlockSpec((1, D, RT), lambda b, i: (b, 0, i))
    anyspec = pl.BlockSpec(memory_space=pl.ANY)
    return pl.pallas_call(
        qkv_kernel,
        grid=(B, S // RT),
        in_specs=[
            pl.BlockSpec(memory_space=pltpu.SMEM),
            row,
            pl.BlockSpec((1, 1, D), lambda b, i: (b, 0, 0)),
            pl.BlockSpec(vec.shape, lambda b, i: (0, 0)),
            pl.BlockSpec(bias.shape, lambda b, i: (0, 0)),
            anyspec,
            anyspec,
        ],
        out_specs=[row, row, row, col, col, col],
        out_shape=[jax.ShapeDtypeStruct((B, S, D), bf16)] * 3 + [jax.ShapeDtypeStruct((B, D, S), bf16)] * 3,
        scratch_shapes=[pltpu.VMEM((D, 3 * D), bf16), pltpu.SemaphoreType.DMA((2,))],
        compiler_params=params(),
        name="norm_qkv",
    )(core, tokens, trow, vec, bias, mine, other)

def head_mask(h, rows):
    lane=lax.broadcasted_iota(jnp.int32,(rows,256),1)
    return (lane//64)==h

def fwd_kernel(lo_ref, hi_ref, q_ref, k_ref, vT_ref, segk_ref, segq_ref, mixed_ref, mixedT_ref, lse_ref, acc, mrow, lrow):
    b=pl.program_id(0); i=pl.program_id(1)
    nq=pl.num_programs(1)
    lo=lo_ref[b*nq+i]; hi=hi_ref[b*nq+i]
    segq=segq_ref[0]
    acc[...]=jnp.zeros_like(acc)
    mrow[...]=jnp.full_like(mrow,NEG); lrow[...]=jnp.zeros_like(lrow)
    def body(c,carry):
        c0=pl.multiple_of(c*KT,KT)
        segk=segk_ref[0,pl.ds(c0,KT),:]
        same=jnp.concatenate([segk,segk],axis=1)==segq
        bias=jnp.where(same,0.0,NEG)
        def scores(quad):
            k4=k_ref[0,pl.ds(c0,KT),quad*256:(quad+1)*256]
            km=jnp.concatenate([jnp.where(head_mask(j,KT),k4,jnp.zeros_like(k4)) for j in range(4)],axis=0)
            return dg(km,q_ref[0,:,quad*256:(quad+1)*256],1,1)
        s_next=scores(0)
        for quad in range(HEADS//4):
            s4=s_next
            if quad+1<HEADS//4: s_next=scores(quad+1)
            for j in range(4):
                h=quad*4+j
                s=s4[j*KT:(j+1)*KT]+bias
                m_old=mrow[h:h+1,:]
                m_new=jnp.maximum(m_old,jnp.max(s,axis=0,keepdims=True))
                p=jnp.exp(s-m_new)
                alpha=jnp.exp(m_old-m_new)
                mrow[h:h+1,:]=m_new
                lrow[h:h+1,:]=lrow[h:h+1,:]*alpha+jnp.sum(p,axis=0,keepdims=True)
                o=dg(vT_ref[0,h*HD:(h+1)*HD,pl.ds(c0,KT)],p.astype(bf16),1,0)
                acc[h*HD:(h+1)*HD,:]=acc[h*HD:(h+1)*HD,:]*alpha+o
        return carry
    lax.fori_loop(lo,hi,body,0)
    inv=1.0/lrow[...]
    lse_ref[0]=mrow[...]+jnp.log(lrow[...])
    for h in range(HEADS):
        o=acc[h*HD:(h+1)*HD,:]*inv[h:h+1,:]
        mixedT_ref[0,h*HD:(h+1)*HD,:]=o
    mixed_ref[0]=mixedT_ref[0].astype(bf16).T

def attn_fwd(lo,hi,q,k,vT,segk,segq):
    B,S,D=q.shape; nq=S//QT
    return pl.pallas_call(fwd_kernel,
      grid_spec=pltpu.PrefetchScalarGridSpec(num_scalar_prefetch=2, grid=(B,nq),
        in_specs=[pl.BlockSpec((1,QT,D),lambda b,i,*_:(b,i,0)),
                  pl.BlockSpec((1,S,D),lambda b,i,*_:(b,0,0)),
                  pl.BlockSpec((1,D,S),lambda b,i,*_:(b,0,0)),
                  pl.BlockSpec((1,S,128),lambda b,i,*_:(b,0,0)),
                  pl.BlockSpec((1,1,QT),lambda b,i,*_:(b,0,i))],
        out_specs=[pl.BlockSpec((1,QT,D),lambda b,i,*_:(b,i,0)),
                   pl.BlockSpec((1,D,QT),lambda b,i,*_:(b,0,i)),
                   pl.BlockSpec((1,HEADS,QT),lambda b,i,*_:(b,0,i))],
        scratch_shapes=[pltpu.VMEM((D,QT),f32),pltpu.VMEM((HEADS,QT),f32),pltpu.VMEM((HEADS,QT),f32)]),
      out_shape=[jax.ShapeDtypeStruct((B,S,D),bf16),jax.ShapeDtypeStruct((B,D,S),f32),jax.ShapeDtypeStruct((B,HEADS,S),f32)],
      compiler_params=params(),
      name="attn_fwd")(lo,hi,q,k,vT,segk,segq)

def bwd_kernel(lo_ref, hi_ref, q_ref, qT_ref, k_ref, kT_ref, v_ref, do_ref, doT_ref, oT_ref, lse_ref, segk_ref, segq_ref,
               dq_ref, dk_ref, dv_ref, dqT, dkT, dvT, dlt):
    b=pl.program_id(0); i=pl.program_id(1)
    nq=pl.num_programs(1)
    lo=lo_ref[b*nq+i]; hi=hi_ref[b*nq+i]
    segq=segq_ref[0]
    @pl.when(i==0)
    def _():
        dkT[...]=jnp.zeros_like(dkT); dvT[...]=jnp.zeros_like(dvT)
    dqT[...]=jnp.zeros_like(dqT)
    for h in range(HEADS):
        sl=slice(h*HD,(h+1)*HD)
        dlt[h:h+1,:]=jnp.sum(doT_ref[0,sl,:]*oT_ref[0,sl,:],axis=0,keepdims=True)
    def body(c,carry):
        c0=pl.multiple_of(c*KT,KT)
        segk=segk_ref[0,pl.ds(c0,KT),:]
        same=jnp.concatenate([segk,segk],axis=1)==segq
        bias=jnp.where(same,0.0,NEG)
        def two(quad):
            ql=slice(quad*256,(quad+1)*256)
            k4=k_ref[0,pl.ds(c0,KT),ql]; v4=v_ref[0,pl.ds(c0,KT),ql]
            km=jnp.concatenate([jnp.where(head_mask(j,KT),k4,jnp.zeros_like(k4)) for j in range(4)],axis=0)
            vm=jnp.concatenate([jnp.where(head_mask(j,KT),v4,jnp.zeros_like(v4)) for j in range(4)],axis=0)
            return dg(km,q_ref[0,:,ql],1,1), dg(vm,do_ref[0,:,ql],1,1)
        nxt=two(0)
        for quad in range(HEADS//4):
            s4,dp4=nxt
            if quad+1<HEADS//4: nxt=two(quad+1)
            for j in range(4):
                h=quad*4+j; sl=slice(h*HD,(h+1)*HD)
                p=jnp.exp(s4[j*KT:(j+1)*KT]+bias-lse_ref[0,h:h+1,:])
                ds=(p*(dp4[j*KT:(j+1)*KT]-dlt[h:h+1,:])).astype(bf16)
                pb=p.astype(bf16)
                dvT[sl,pl.ds(c0,KT)]+=dg(doT_ref[0,sl,:],pb,1,1)
                dkT[sl,pl.ds(c0,KT)]+=dg(qT_ref[0,sl,:],ds,1,1)
                dqT[sl,:]+=dg(kT_ref[0,sl,pl.ds(c0,KT)],ds,1,0)
        return carry
    lax.fori_loop(lo,hi,body,0)
    dq_ref[0]=dqT[...].astype(bf16).T
    @pl.when(i==nq-1)
    def _():
        dk_ref[0]=dkT[...].astype(bf16).T
        dv_ref[0]=dvT[...].astype(bf16).T

def attn_bwd(lo,hi,q,qT,k,kT,v,do,doT,oT,lse,segk,segq):
    B,S,D=q.shape; nq=S//QT
    row=pl.BlockSpec((1,QT,D),lambda b,i,*_:(b,i,0))
    col=pl.BlockSpec((1,D,QT),lambda b,i,*_:(b,0,i))
    full=pl.BlockSpec((1,S,D),lambda b,i,*_:(b,0,0))
    fullT=pl.BlockSpec((1,D,S),lambda b,i,*_:(b,0,0))
    return pl.pallas_call(bwd_kernel,
      grid_spec=pltpu.PrefetchScalarGridSpec(num_scalar_prefetch=2, grid=(B,nq),
        in_specs=[row,col,full,fullT,full,row,col,col,
                  pl.BlockSpec((1,HEADS,QT),lambda b,i,*_:(b,0,i)),
                  pl.BlockSpec((1,S,128),lambda b,i,*_:(b,0,0)),
                  pl.BlockSpec((1,1,QT),lambda b,i,*_:(b,0,i))],
        out_specs=[row,full,full],
        scratch_shapes=[pltpu.VMEM((D,QT),f32),pltpu.VMEM((D,S),f32),pltpu.VMEM((D,S),f32),pltpu.VMEM((HEADS,QT),f32)]),
      out_shape=[jax.ShapeDtypeStruct((B,S,D),bf16)]*3,
      compiler_params=params(),
      name="attn_bwd")(lo,hi,q,qT,k,kT,v,do,doT,oT,lse,segk,segq)


def mlp_kernel(core_ref, tok_ref, row_ref, cot_ref, mix_ref, vec_ref, bup_ref,
               ou_mine, ou_other, d_mine, d_other,
               out_ref, gmid_ref, gmix_ref, gmixT_ref, vecg_ref, bupg_ref,
               ou_keep, ou_send, d_keep, d_send,
               wout, wup, wdown, aout, aup, adown, acc, gh2, hid, sems):
    i = pl.program_id(0)
    core = core_ref[0]
    D = tok_ref.shape[2]
    FF = wup.shape[1]
    hd, hf = D // 2, FF // 2
    at = (core, 1 - core)

    def weight_copies(out, refs_ou, refs_d):
        made = []
        for n in range(2):
            cd = pl.multiple_of(at[n] * hd, 128)
            cf = pl.multiple_of(at[n] * hf, 128)
            pairs = (
                (refs_ou[n].at[:, pl.ds(0, hd)], wout.at[:, pl.ds(cd, hd)]),
                (refs_ou[n].at[:, pl.ds(hd, hf)], wup.at[:, pl.ds(cf, hf)]),
                (refs_d[n], wdown.at[:, pl.ds(cd, hd)]),
            )
            for m, (hbm, vmem) in enumerate(pairs):
                src, dst = (vmem, hbm) if out else (hbm, vmem)
                made.append(pltpu.make_async_copy(src, dst, sems.at[n * 3 + m]))
        return made

    @pl.when(i == 0)
    def _():
        copies = weight_copies(False, (ou_mine, ou_other), (d_mine, d_other))
        for c in copies:
            c.start()
        aout[...] = jnp.zeros_like(aout)
        aup[...] = jnp.zeros_like(aup)
        adown[...] = jnp.zeros_like(adown)
        vecg_ref[...] = jnp.zeros_like(vecg_ref)
        bupg_ref[...] = jnp.zeros_like(bupg_ref)
        for c in copies:
            c.wait()

    base = tok_ref[0].astype(f32) + row_ref[0]
    middle = base + dg(mix_ref[0], wout[...], 1, 0) + vec_ref[0:1, :]
    normed, inv = normalize(middle)
    hid[...] = (normed * vec_ref[1:2, :] + vec_ref[2:3, :]).astype(bf16)
    acc[...] = middle + vec_ref[3:4, :]
    gh2[...] = jnp.zeros_like(gh2)
    cot = cot_ref[0]

    def chunk(j, carry):
        c0 = pl.multiple_of(j * FC, FC)
        cols = pl.ds(c0, FC)
        up = dg(hid[...], wup[:, cols], 1, 0) + bup_ref[:, cols]
        ga = dg(cot, wdown[cols, :], 1, 1)
        active, slope = gelu_parts(up)
        active = active.astype(bf16)
        gu = (ga * slope).astype(bf16)
        acc[...] += dg(active, wdown[cols, :], 1, 0)
        adown[cols, :] += dg(active, cot, 0, 0)
        gh2[...] += dg(gu, wup[:, cols], 1, 1)
        aup[:, cols] += dg(hid[...], gu, 0, 0)
        bupg_ref[:, cols] += col_sum(gu.astype(f32))
        return carry

    lax.fori_loop(0, FF // FC, chunk, 0)
    out_ref[0] = acc[...].astype(bf16)
    grad_hidden = gh2[...]
    base = tok_ref[0].astype(f32) + row_ref[0]
    middle = base + dg(mix_ref[0], wout[...], 1, 0) + vec_ref[0:1, :]
    normed, inv = normalize(middle)
    cotf = cot.astype(f32)
    gmid = cotf + norm_back(grad_hidden, normed, inv, vec_ref[1:2, :])
    gmid_ref[0] = gmid
    branch = gmid.astype(bf16)
    vecg_ref[0:1, :] += col_sum(branch.astype(f32))
    vecg_ref[1:2, :] += col_sum(grad_hidden * normed)
    vecg_ref[2:3, :] += col_sum(grad_hidden)
    vecg_ref[3:4, :] += col_sum(cotf)
    aout[...] += dg(mix_ref[0], branch, 0, 0)
    gmix = dg(branch, wout[...], 1, 1).astype(bf16)
    gmix_ref[0] = gmix
    gmixT_ref[0] = gmix.T

    @pl.when(i == pl.num_programs(0) - 1)
    def _():
        wout[...] = aout[...].astype(bf16)
        wup[...] = aup[...].astype(bf16)
        wdown[...] = adown[...].astype(bf16)
        copies = weight_copies(True, (ou_keep, ou_send), (d_keep, d_send))
        for c in copies:
            c.start()
        for c in copies:
            c.wait()


def mlp_call(core, tokens, trow, cot, mixed, vec, bup, ou_mine, ou_other, d_mine, d_other):
    B, S, D = tokens.shape
    FF = bup.shape[1]
    per = S // RT
    row = pl.BlockSpec((1, RT, D), lambda i: (i // per, i % per, 0))
    col = pl.BlockSpec((1, D, RT), lambda i: (i // per, 0, i % per))
    whole = lambda shape: pl.BlockSpec(shape, lambda i: (0,) * len(shape))
    anyspec = pl.BlockSpec(memory_space=pl.ANY)
    sds = jax.ShapeDtypeStruct
    return pl.pallas_call(
        mlp_kernel,
        grid=(B * per,),
        in_specs=[
            pl.BlockSpec(memory_space=pltpu.SMEM),
            row,
            pl.BlockSpec((1, 1, D), lambda i: (i // per, 0, 0)),
            row,
            row,
            whole(vec.shape),
            whole(bup.shape),
        ] + [anyspec] * 4,
        out_specs=[row, row, row, col, whole((4, D)), whole((1, FF))] + [anyspec] * 4,
        out_shape=[
            sds((B, S, D), bf16),
            sds((B, S, D), f32),
            sds((B, S, D), bf16),
            sds((B, D, S), bf16),
            sds((4, D), f32),
            sds((1, FF), f32),
            sds(ou_mine.shape, bf16),
            sds(ou_mine.shape, bf16),
            sds(d_mine.shape, bf16),
            sds(d_mine.shape, bf16),
        ],
        scratch_shapes=[
            pltpu.VMEM((D, D), bf16),
            pltpu.VMEM((D, FF), bf16),
            pltpu.VMEM((FF, D), bf16),
            pltpu.VMEM((D, D), f32),
            pltpu.VMEM((D, FF), f32),
            pltpu.VMEM((FF, D), f32),
            pltpu.VMEM((RT, D), f32),
            pltpu.VMEM((RT, D), f32),
            pltpu.VMEM((RT, D), bf16),
            pltpu.SemaphoreType.DMA((6,)),
        ],
        compiler_params=params(),
        name="mlp_both",
    )(core, tokens, trow, cot, mixed, vec, bup, ou_mine, ou_other, d_mine, d_other)


def qkv_back_kernel(core_ref, tok_ref, row_ref, gmid_ref, dq_ref, dk_ref, dv_ref, vec_ref, mine_ref, other_ref,
                    gin_ref, rsum_ref, vecg_ref, keep_ref, send_ref, w_ref, aw_ref, sems):
    b = pl.program_id(0)
    i = pl.program_id(1)
    core = core_ref[0]
    D = tok_ref.shape[2]

    @pl.when((b == 0) & (i == 0))
    def _():
        copies = place_halves(mine_ref, other_ref, w_ref, core, sems)
        for c in copies:
            c.start()
        aw_ref[...] = jnp.zeros_like(aw_ref)
        vecg_ref[...] = jnp.zeros_like(vecg_ref)
        for c in copies:
            c.wait()

    @pl.when(i == 0)
    def _():
        rsum_ref[...] = jnp.zeros_like(rsum_ref)

    base = tok_ref[0].astype(f32) + row_ref[0]
    normed, inv = normalize(base)
    hidden = (normed * vec_ref[0:1, :] + vec_ref[1:2, :]).astype(bf16)
    grads = (dq_ref[0], dk_ref[0], dv_ref[0])
    grad_hidden = None
    for n, g in enumerate(grads):
        cols = slice(n * D, (n + 1) * D)
        part = dg(g, w_ref[:, cols], 1, 1)
        grad_hidden = part if grad_hidden is None else grad_hidden + part
        aw_ref[:, cols] += dg(hidden, g, 0, 0)
    gbase = gmid_ref[0] + norm_back(grad_hidden, normed, inv, vec_ref[0:1, :])
    gin_ref[0] = gbase.astype(bf16)
    rsum_ref[0] += col_sum(gbase)
    vecg_ref[0:1, :] += col_sum(grad_hidden * normed)
    vecg_ref[1:2, :] += col_sum(grad_hidden)
    vecg_ref[2:3, :] += col_sum(grads[0].astype(f32))
    vecg_ref[3:4, :] += col_sum(grads[2].astype(f32))

    @pl.when((b == pl.num_programs(0) - 1) & (i == pl.num_programs(1) - 1))
    def _():
        w_ref[...] = aw_ref[...].astype(bf16)
        half = keep_ref.shape[1]
        at = pl.multiple_of(core * half, 128)
        rest = pl.multiple_of((1 - core) * half, 128)
        copies = (
            pltpu.make_async_copy(w_ref.at[:, pl.ds(at, half)], keep_ref, sems.at[0]),
            pltpu.make_async_copy(w_ref.at[:, pl.ds(rest, half)], send_ref, sems.at[1]),
        )
        for c in copies:
            c.start()
        for c in copies:
            c.wait()


def qkv_back_call(core, tokens, trow, gmid, dq, dk, dv, vec, mine, other):
    B, S, D = tokens.shape
    row = pl.BlockSpec((1, RT, D), lambda b, i: (b, i, 0))
    seq = pl.BlockSpec((1, 1, D), lambda b, i: (b, 0, 0))
    anyspec = pl.BlockSpec(memory_space=pl.ANY)
    sds = jax.ShapeDtypeStruct
    return pl.pallas_call(
        qkv_back_kernel,
        grid=(B, S // RT),
        in_specs=[
            pl.BlockSpec(memory_space=pltpu.SMEM),
            row,
            seq,
            row,
            row,
            row,
            row,
            pl.BlockSpec(vec.shape, lambda b, i: (0, 0)),
            anyspec,
            anyspec,
        ],
        out_specs=[row, seq, pl.BlockSpec((4, D), lambda b, i: (0, 0)), anyspec, anyspec],
        out_shape=[
            sds((B, S, D), bf16),
            sds((B, 1, D), f32),
            sds((4, D), f32),
            sds(mine.shape, bf16),
            sds(mine.shape, bf16),
        ],
        scratch_shapes=[
            pltpu.VMEM((D, 3 * D), bf16),
            pltpu.VMEM((D, 3 * D), f32),
            pltpu.SemaphoreType.DMA((2,)),
        ],
        compiler_params=params(),
        name="norm_qkv_back",
    )(core, tokens, trow, gmid, dq, dk, dv, vec, mine, other)


def key_ranges(segment_ids):
    B, S = segment_ids.shape
    tiles = segment_ids.reshape(B, S // QT, QT)
    before = jnp.sum((segment_ids[:, None, :] < tiles[:, :, :1]).astype(jnp.int32), axis=-1)
    upto = jnp.sum((segment_ids[:, None, :] <= tiles[:, :, -1:]).astype(jnp.int32), axis=-1)
    return (before // KT).reshape(-1), ((upto + KT - 1) // KT).reshape(-1)


def own_slice(array, index, size, axis):
    return lax.dynamic_slice_in_dim(array, index * size, size, axis)


def swap(array, axis):
    return lax.ppermute(array, axis, [(0, 1), (1, 0)])


def all_sum(array, axis):
    size = lax.axis_size(axis)
    step = 1
    while step < size:
        array = array + lax.ppermute(array, axis, [(i, i ^ step) for i in range(size)])
        step *= 2
    return array


def on_device(
    tokens,
    cot,
    segment_ids,
    block_map,
    timesteps,
    step_table,
    ln1_gain,
    ln1_bias,
    w_query,
    b_query,
    w_key,
    w_value,
    b_value,
    w_out,
    b_out,
    ln2_gain,
    ln2_bias,
    w_up,
    b_up,
    w_down,
    b_down,
):
    B, S, D = tokens.shape
    every = ("xrep", "core", "shard")
    n = lax.axis_size("shard")
    me = lax.axis_index("shard")
    core = lax.axis_index("core")
    own = ln1_gain.shape[0]
    FF = b_up.shape[0] * n
    hd, hf = D // 2, FF // 2
    core1 = core.reshape(1).astype(jnp.int32)

    qkv_local = jnp.concatenate([w_query, w_key, w_value], axis=1)
    qkv_mine = lax.all_gather(own_slice(qkv_local, core, 3 * hd, 1), "shard", axis=0, tiled=True)
    qkv_other = swap(qkv_mine, "core")
    ou_local = jnp.concatenate([own_slice(w_out, core, hd, 1), own_slice(w_up, core, hf, 1)], axis=1)
    ou_mine = lax.all_gather(ou_local, "shard", axis=0, tiled=True)
    ou_other = swap(ou_mine, "core")
    d_mine = lax.all_gather(own_slice(w_down, core, hd, 1), "shard", axis=0, tiled=True)
    d_other = swap(d_mine, "core")

    small = (ln1_gain, ln1_bias, b_query, b_value, b_out, ln2_gain, ln2_bias, b_down)
    packed = lax.all_gather(jnp.concatenate(small + (b_up,)), "shard", axis=0).astype(f32)
    g1, s1, bq, bv, bo, g2, s2, bd = [packed[:, i * own : (i + 1) * own].reshape(1, D) for i in range(8)]
    bup = packed[:, 8 * own :].reshape(1, FF)
    vec1 = jnp.concatenate([g1, s1], axis=0)
    bias = jnp.concatenate([bq, jnp.zeros_like(bq), bv], axis=1)
    vec2 = jnp.concatenate([bo, g2, s2, bd], axis=0)

    steps = lax.all_gather(timesteps, every, axis=0, tiled=True)
    own_rows = step_table.shape[0]
    group = lax.all_gather(timesteps, "shard", axis=0, tiled=True)
    spots = me * own_rows + lax.broadcasted_iota(jnp.int32, (1, own_rows), 1)
    picker = (group[:, None] == spots).astype(bf16)
    found = jnp.dot(picker, step_table, preferred_element_type=f32)
    trow = lax.psum_scatter(found, "shard", scatter_dimension=0, tiled=True).reshape(B, 1, D)

    lo, hi = key_ranges(segment_ids)
    segk = jnp.broadcast_to(segment_ids[:, :, None], (B, S, 128))
    segq = segment_ids[:, None, :]

    q, k, v, qT, kT, vT = qkv_call(core1, tokens, trow, vec1, bias, qkv_mine, qkv_other)
    mixed, mixedT, lse = attn_fwd(lo, hi, q, k, vT, segk, segq)
    out, gmid, gmix, gmixT, vecg2, bupg, ou_keep, ou_send, d_keep, d_send = mlp_call(
        core1, tokens, trow, cot, mixed, vec2, bup, ou_mine, ou_other, d_mine, d_other
    )

    def reduce_half(keep, send):
        half = (keep.astype(f32) + swap(send, "core").astype(f32)).astype(bf16)
        return lax.psum_scatter(half, "shard", scatter_dimension=0, tiled=True)

    def finish(part):
        half = all_sum(part.astype(f32), "xrep").astype(bf16)
        other = swap(half, "core").astype(f32)
        half = half.astype(f32)
        return jnp.where(core == 0, half, other), jnp.where(core == 0, other, half)

    d_part = reduce_half(d_keep, d_send)
    ou_part = reduce_half(ou_keep, ou_send)
    dq, dk, dv = attn_bwd(lo, hi, q, qT, k, kT, v, gmix, gmixT, mixedT, lse, segk, segq)
    gin, rsum, vecg1, qkv_keep, qkv_send = qkv_back_call(
        core1, tokens, trow, gmid, dq, dk, dv, vec1, qkv_mine, qkv_other
    )
    qkv_part = reduce_half(qkv_keep, qkv_send)

    flat = jnp.concatenate([vecg1, vecg2], axis=0)
    flat = lax.psum(jnp.concatenate([flat.reshape(-1), bupg.reshape(-1)]), every)
    vg = [own_slice(flat[i * D : (i + 1) * D], me, own, 0) for i in range(8)]
    g_bup = own_slice(flat[8 * D :], me, FF // n, 0)
    sums = lax.all_gather(rsum.reshape(B, D), every, axis=0, tiled=True)
    owners = me * own_rows + lax.broadcasted_iota(jnp.int32, (own_rows, 1), 0)
    g_table = jnp.dot(
        (owners == steps[None, :]).astype(f32), sums, precision=lax.Precision.HIGHEST, preferred_element_type=f32
    )

    d_left, d_right = finish(d_part)
    ou_left, ou_right = finish(ou_part)
    q_left, q_right = finish(qkv_part)
    g_down = jnp.concatenate([d_left, d_right], axis=1)
    g_out = jnp.concatenate([ou_left[:, :hd], ou_right[:, :hd]], axis=1)
    g_up = jnp.concatenate([ou_left[:, hd:], ou_right[:, hd:]], axis=1)
    g_qkv = jnp.concatenate([q_left, q_right], axis=1)
    g_q, g_k, g_v = g_qkv[:, :D], g_qkv[:, D : 2 * D], g_qkv[:, 2 * D :]
    return (
        out, gin, g_table, vg[0], vg[1], g_q, vg[2], g_k, g_v, vg[3], g_out, vg[4], vg[5], vg[6], g_up, g_bup, g_down, vg[7],
    )


def solution(mesh):
    rep, shard = mesh.shape["rep"], mesh.shape["shard"]
    fine = Mesh(mesh.devices.reshape(rep // 2, 2, shard), ("xrep", "core", "shard"))
    seqs = ("xrep", "core", "shard")
    mat, vec = P("shard", None), P("shard")
    rows3, rows2 = P(seqs, None, None), P(seqs, None)
    weights = (mat, vec, vec, mat, vec, mat, mat, vec, mat, vec, vec, vec, mat, vec, mat, vec)
    return jax.shard_map(
        on_device,
        mesh=fine,
        in_specs=(rows3, rows3, rows2, rows3, P(seqs)) + weights,
        out_specs=(rows3, rows3) + weights,
        check_vma=False,
    )
```

```python
import functools

import jax
import jax.numpy as jnp
from jax import lax
from jax.experimental import pallas as pl
from jax.experimental.pallas import tpu as pltpu
from jax.sharding import Mesh, PartitionSpec as P

HEADS = 12
HD = 64
QT = 256
KT = 256
RT = 512
FC = 512
EPS = 1e-05
NEG = -1e30
f32 = jnp.float32
bf16 = jnp.bfloat16
VMEM_BYTES = 60 * 1000 * 1024


def dg(x, y, cx, cy):
    return lax.dot_general(x, y, (((cx,), (cy,)), ((), ())), preferred_element_type=f32)


def normalize(values):
    center = values - jnp.mean(values, axis=-1, keepdims=True)
    inv_dev = lax.rsqrt(jnp.mean(center * center, axis=-1, keepdims=True) + EPS)
    return center * inv_dev, inv_dev


def norm_back(grad_hidden, normed, inv_dev, gain_row):
    grad_normed = grad_hidden * gain_row
    return inv_dev * (
        grad_normed
        - jnp.mean(grad_normed, axis=-1, keepdims=True)
        - normed * jnp.mean(grad_normed * normed, axis=-1, keepdims=True)
    )


def col_sum(values):
    return jnp.sum(values, axis=0, keepdims=True)


def gelu_parts(x):
    density = jnp.exp(-0.5 * x * x)
    t = 1.0 / (1.0 + 0.2316418882 * jnp.abs(x))
    poly = t * (0.127414796 + t * (-0.142248368 + t * (0.7107068705 + t * (-0.7265760135 + t * 0.5307027145))))
    tail = density * poly
    cdf = jnp.where(x >= 0.0, 1.0 - tail, tail)
    return x * cdf, cdf + x * (density * 0.3989422804014327)


def place_halves(mine, other, full, core, sems):
    half = mine.shape[1]
    at = pl.multiple_of(core * half, 128)
    rest = pl.multiple_of((1 - core) * half, 128)
    return (
        pltpu.make_async_copy(mine, full.at[:, pl.ds(at, half)], sems.at[0]),
        pltpu.make_async_copy(other, full.at[:, pl.ds(rest, half)], sems.at[1]),
    )


def params(**kw):
    return pltpu.CompilerParams(vmem_limit_bytes=VMEM_BYTES, **kw)


def qkv_kernel(core_ref, tok_ref, row_ref, vec_ref, bias_ref, mine_ref, other_ref,
               q_ref, k_ref, v_ref, qT_ref, kT_ref, vT_ref, w_ref, sems):
    @pl.when((pl.program_id(0) == 0) & (pl.program_id(1) == 0))
    def _():
        copies = place_halves(mine_ref, other_ref, w_ref, core_ref[0], sems)
        for c in copies:
            c.start()
        for c in copies:
            c.wait()

    width = tok_ref.shape[2]
    base = tok_ref[0].astype(f32) + row_ref[0]
    normed, unused = normalize(base)
    hidden = (normed * vec_ref[0:1, :] + vec_ref[1:2, :]).astype(bf16)
    scale = HD ** (-0.5)
    for n, (out, outT) in enumerate(((q_ref, qT_ref), (k_ref, kT_ref), (v_ref, vT_ref))):
        cols = slice(n * width, (n + 1) * width)
        rows = (dg(hidden, w_ref[:, cols], 1, 0) + bias_ref[:, cols]).astype(bf16)
        scaled = (rows.astype(f32) * scale).astype(bf16)
        out[0] = scaled if n == 0 else rows
        outT[0] = (rows if n == 2 else scaled).T


def qkv_call(core, tokens, trow, vec, bias, mine, other):
    B, S, D = tokens.shape
    row = pl.BlockSpec((1, RT, D), lambda b, i: (b, i, 0))
    col = pl.BlockSpec((1, D, RT), lambda b, i: (b, 0, i))
    anyspec = pl.BlockSpec(memory_space=pl.ANY)
    return pl.pallas_call(
        qkv_kernel,
        grid=(B, S // RT),
        in_specs=[
            pl.BlockSpec(memory_space=pltpu.SMEM),
            row,
            pl.BlockSpec((1, 1, D), lambda b, i: (b, 0, 0)),
            pl.BlockSpec(vec.shape, lambda b, i: (0, 0)),
            pl.BlockSpec(bias.shape, lambda b, i: (0, 0)),
            anyspec,
            anyspec,
        ],
        out_specs=[row, row, row, col, col, col],
        out_shape=[jax.ShapeDtypeStruct((B, S, D), bf16)] * 3 + [jax.ShapeDtypeStruct((B, D, S), bf16)] * 3,
        scratch_shapes=[pltpu.VMEM((D, 3 * D), bf16), pltpu.SemaphoreType.DMA((2,))],
        compiler_params=params(),
        cost_estimate=pl.CostEstimate(flops=6 * B * S * D * D, bytes_accessed=30 * 10**6, transcendentals=0),
        name="norm_qkv",
    )(core, tokens, trow, vec, bias, mine, other)

def head_mask(h, rows):
    lane=lax.broadcasted_iota(jnp.int32,(rows,256),1)
    return (lane//64)==h

def fwd_kernel(lo_ref, hi_ref, q_ref, k_ref, vT_ref, segk_ref, segq_ref, mixed_ref, mixedT_ref, lse_ref, acc, mrow, lrow):
    b=pl.program_id(0); i=pl.program_id(1)
    nq=pl.num_programs(1)
    lo=lo_ref[b*nq+i]; hi=hi_ref[b*nq+i]
    segq=segq_ref[0]
    acc[...]=jnp.zeros_like(acc)
    mrow[...]=jnp.full_like(mrow,NEG); lrow[...]=jnp.zeros_like(lrow)
    def body(c,carry):
        c0=pl.multiple_of(c*KT,KT)
        segk=segk_ref[0,pl.ds(c0,KT),:]
        same=jnp.concatenate([segk,segk],axis=1)==segq
        bias=jnp.where(same,0.0,NEG)
        def scores(quad):
            k4=k_ref[0,pl.ds(c0,KT),quad*256:(quad+1)*256]
            km=jnp.concatenate([jnp.where(head_mask(j,KT),k4,jnp.zeros_like(k4)) for j in range(4)],axis=0)
            return dg(km,q_ref[0,:,quad*256:(quad+1)*256],1,1)
        s_next=scores(0)
        for quad in range(HEADS//4):
            s4=s_next
            if quad+1<HEADS//4: s_next=scores(quad+1)
            for j in range(4):
                h=quad*4+j
                s=s4[j*KT:(j+1)*KT]+bias
                m_old=mrow[h:h+1,:]
                m_new=jnp.maximum(m_old,jnp.max(s,axis=0,keepdims=True))
                p=jnp.exp(s-m_new)
                alpha=jnp.exp(m_old-m_new)
                mrow[h:h+1,:]=m_new
                lrow[h:h+1,:]=lrow[h:h+1,:]*alpha+jnp.sum(p,axis=0,keepdims=True)
                o=dg(vT_ref[0,h*HD:(h+1)*HD,pl.ds(c0,KT)],p.astype(bf16),1,0)
                acc[h*HD:(h+1)*HD,:]=acc[h*HD:(h+1)*HD,:]*alpha+o
        return carry
    lax.fori_loop(lo,hi,body,0)
    inv=1.0/lrow[...]
    lse_ref[0]=mrow[...]+jnp.log(lrow[...])
    for h in range(HEADS):
        o=acc[h*HD:(h+1)*HD,:]*inv[h:h+1,:]
        mixedT_ref[0,h*HD:(h+1)*HD,:]=o
    mixed_ref[0]=mixedT_ref[0].astype(bf16).T

def attn_fwd(lo,hi,q,k,vT,segk,segq):
    B,S,D=q.shape; nq=S//QT
    return pl.pallas_call(fwd_kernel,
      grid_spec=pltpu.PrefetchScalarGridSpec(num_scalar_prefetch=2, grid=(B,nq),
        in_specs=[pl.BlockSpec((1,QT,D),lambda b,i,*_:(b,i,0)),
                  pl.BlockSpec((1,S,D),lambda b,i,*_:(b,0,0)),
                  pl.BlockSpec((1,D,S),lambda b,i,*_:(b,0,0)),
                  pl.BlockSpec((1,S,128),lambda b,i,*_:(b,0,0)),
                  pl.BlockSpec((1,1,QT),lambda b,i,*_:(b,0,i))],
        out_specs=[pl.BlockSpec((1,QT,D),lambda b,i,*_:(b,i,0)),
                   pl.BlockSpec((1,D,QT),lambda b,i,*_:(b,0,i)),
                   pl.BlockSpec((1,HEADS,QT),lambda b,i,*_:(b,0,i))],
        scratch_shapes=[pltpu.VMEM((D,QT),f32),pltpu.VMEM((HEADS,QT),f32),pltpu.VMEM((HEADS,QT),f32)]),
      out_shape=[jax.ShapeDtypeStruct((B,S,D),bf16),jax.ShapeDtypeStruct((B,D,S),f32),jax.ShapeDtypeStruct((B,HEADS,S),f32)],
      compiler_params=params(),
      cost_estimate=pl.CostEstimate(flops=16 * B * S * S * D, bytes_accessed=30 * 10**6, transcendentals=0),
      name="attn_fwd")(lo,hi,q,k,vT,segk,segq)

def bwd_kernel(lo_ref, hi_ref, q_ref, qT_ref, k_ref, kT_ref, v_ref, do_ref, doT_ref, oT_ref, lse_ref, segk_ref, segq_ref, after_ref,
               dq_ref, dk_ref, dv_ref, dqT, dkT, dvT, dlt):
    b=pl.program_id(0); i=pl.program_id(1)
    nq=pl.num_programs(1)
    lo=lo_ref[b*nq+i]; hi=hi_ref[b*nq+i]
    segq=segq_ref[0]
    @pl.when(i==0)
    def _():
        dkT[...]=jnp.zeros_like(dkT); dvT[...]=jnp.zeros_like(dvT)
    dqT[...]=jnp.zeros_like(dqT)
    for h in range(HEADS):
        sl=slice(h*HD,(h+1)*HD)
        dlt[h:h+1,:]=jnp.sum(doT_ref[0,sl,:]*oT_ref[0,sl,:],axis=0,keepdims=True)
    def body(c,carry):
        c0=pl.multiple_of(c*KT,KT)
        segk=segk_ref[0,pl.ds(c0,KT),:]
        same=jnp.concatenate([segk,segk],axis=1)==segq
        bias=jnp.where(same,0.0,NEG)
        def two(quad):
            ql=slice(quad*256,(quad+1)*256)
            k4=k_ref[0,pl.ds(c0,KT),ql]; v4=v_ref[0,pl.ds(c0,KT),ql]
            km=jnp.concatenate([jnp.where(head_mask(j,KT),k4,jnp.zeros_like(k4)) for j in range(4)],axis=0)
            vm=jnp.concatenate([jnp.where(head_mask(j,KT),v4,jnp.zeros_like(v4)) for j in range(4)],axis=0)
            return dg(km,q_ref[0,:,ql],1,1), dg(vm,do_ref[0,:,ql],1,1)
        nxt=two(0)
        for quad in range(HEADS//4):
            s4,dp4=nxt
            if quad+1<HEADS//4: nxt=two(quad+1)
            for j in range(4):
                h=quad*4+j; sl=slice(h*HD,(h+1)*HD)
                p=jnp.exp(s4[j*KT:(j+1)*KT]+bias-lse_ref[0,h:h+1,:])
                ds=(p*(dp4[j*KT:(j+1)*KT]-dlt[h:h+1,:])).astype(bf16)
                pb=p.astype(bf16)
                dvT[sl,pl.ds(c0,KT)]+=dg(doT_ref[0,sl,:],pb,1,1)
                dkT[sl,pl.ds(c0,KT)]+=dg(qT_ref[0,sl,:],ds,1,1)
                dqT[sl,:]+=dg(kT_ref[0,sl,pl.ds(c0,KT)],ds,1,0)
        return carry
    lax.fori_loop(lo,hi,body,0)
    dq_ref[0]=dqT[...].astype(bf16).T
    @pl.when(i==nq-1)
    def _():
        dk_ref[0]=dkT[...].astype(bf16).T
        dv_ref[0]=dvT[...].astype(bf16).T

def attn_bwd(lo,hi,q,qT,k,kT,v,do,doT,oT,lse,segk,segq,after):
    B,S,D=q.shape; nq=S//QT
    row=pl.BlockSpec((1,QT,D),lambda b,i,*_:(b,i,0))
    col=pl.BlockSpec((1,D,QT),lambda b,i,*_:(b,0,i))
    full=pl.BlockSpec((1,S,D),lambda b,i,*_:(b,0,0))
    fullT=pl.BlockSpec((1,D,S),lambda b,i,*_:(b,0,0))
    return pl.pallas_call(bwd_kernel,
      grid_spec=pltpu.PrefetchScalarGridSpec(num_scalar_prefetch=2, grid=(B,nq),
        in_specs=[row,col,full,fullT,full,row,col,col,
                  pl.BlockSpec((1,HEADS,QT),lambda b,i,*_:(b,0,i)),
                  pl.BlockSpec((1,S,128),lambda b,i,*_:(b,0,0)),
                  pl.BlockSpec((1,1,QT),lambda b,i,*_:(b,0,i)),
                  pl.BlockSpec(memory_space=pl.ANY)],
        out_specs=[row,full,full],
        scratch_shapes=[pltpu.VMEM((D,QT),f32),pltpu.VMEM((D,S),f32),pltpu.VMEM((D,S),f32),pltpu.VMEM((HEADS,QT),f32)]),
      out_shape=[jax.ShapeDtypeStruct((B,S,D),bf16)]*3,
      compiler_params=params(),
      cost_estimate=pl.CostEstimate(flops=32 * B * S * S * D, bytes_accessed=40 * 10**6, transcendentals=0),
      name="attn_bwd")(lo,hi,q,qT,k,kT,v,do,doT,oT,lse,segk,segq,after)


def mlp_chunks(hid, cot, wup, wdown, bup_ref, acc, gh2, aup, adown, bupg_ref):
    def chunk(j, carry):
        c0 = pl.multiple_of(j * FC, FC)
        cols = pl.ds(c0, FC)
        up = dg(hid, wup[:, cols], 1, 0) + bup_ref[:, cols]
        ga = dg(cot, wdown[cols, :], 1, 1)
        active, slope = gelu_parts(up)
        active = active.astype(bf16)
        gu = (ga * slope).astype(bf16)
        acc[0] += dg(active, wdown[cols, :], 1, 0)
        adown[cols, :] += dg(active, cot, 0, 0)
        gh2[0] += dg(gu, wup[:, cols], 1, 1)
        aup[:, cols] += dg(hid, gu, 0, 0)
        bupg_ref[:, cols] += col_sum(gu.astype(f32))
        return carry

    lax.fori_loop(0, wup.shape[1] // FC, chunk, 0)


def mlp_load(first, w_ref, extra, wup, wdown, sems):
    D, H = wup.shape
    at = D if first else 0
    pairs = [(w_ref.at[:, pl.ds(at, H)], wup)]
    pairs += [(w_ref.at[:, pl.ds(at + H + j * D, D)], wdown.at[pl.ds(j * D, D), :]) for j in range(H // D)]
    pairs += extra
    return [pltpu.make_async_copy(src, dst, sems.at[n]) for n, (src, dst) in enumerate(pairs)]


def mlp_store(core, wup, wdown, keep_ref, send_ref, extra, sems):
    D, H = wup.shape

    def run(up_to, down_to):
        pairs = [(wup, up_to.at[:, pl.ds(0, H)])]
        pairs += [(wdown.at[pl.ds(j * D, D), :], down_to.at[:, pl.ds(j * D, D)]) for j in range(H // D)]
        pairs += extra
        made = [pltpu.make_async_copy(src, dst, sems.at[n]) for n, (src, dst) in enumerate(pairs)]
        for c in made:
            c.start()
        for c in made:
            c.wait()

    @pl.when(core == 0)
    def _():
        run(keep_ref, send_ref)

    @pl.when(core != 0)
    def _():
        run(send_ref, keep_ref)


def mlp_first_kernel(core_ref, tok_ref, row_ref, cot_ref, mix_ref, vec_ref, bup_ref, w_ref,
                     acc_ref, gh2_ref, mid_ref, hid_ref, bupg_ref, keep_ref, send_ref,
                     wout, wup, wdown, aup, adown, sems):
    i = pl.program_id(0)
    D = tok_ref.shape[2]

    @pl.when(i == 0)
    def _():
        copies = mlp_load(True, w_ref, [(w_ref.at[:, pl.ds(0, D)], wout)], wup, wdown, sems)
        for c in copies:
            c.start()
        aup[...] = jnp.zeros_like(aup)
        adown[...] = jnp.zeros_like(adown)
        bupg_ref[...] = jnp.zeros_like(bupg_ref)
        for c in copies:
            c.wait()

    base = tok_ref[0].astype(f32) + row_ref[0]
    middle = base + dg(mix_ref[0], wout[...], 1, 0) + vec_ref[0:1, :]
    mid_ref[0] = middle
    normed, unused = normalize(middle)
    hid_ref[0] = (normed * vec_ref[1:2, :] + vec_ref[2:3, :]).astype(bf16)
    acc_ref[0] = middle + vec_ref[3:4, :]
    gh2_ref[...] = jnp.zeros_like(gh2_ref)
    mlp_chunks(hid_ref[0], cot_ref[0], wup, wdown, bup_ref, acc_ref, gh2_ref, aup, adown, bupg_ref)

    @pl.when(i == pl.num_programs(0) - 1)
    def _():
        wup[...] = aup[...].astype(bf16)
        wdown[...] = adown[...].astype(bf16)
        mlp_store(core_ref[0], wup, wdown, keep_ref, send_ref, [], sems)


def mlp_second_kernel(core_ref, accin_ref, gh2in_ref, mid_ref, hid_ref, cot_ref, mix_ref, vec_ref, bup_ref, wfirst_ref, w_ref,
                      out_ref, gmid_ref, gmix_ref, gmixT_ref, vecg_ref, bupg_ref, keep_ref, send_ref,
                      wout, wup, wdown, aout, aup, adown, acc, gh2, sems):
    i = pl.program_id(0)
    core = core_ref[0]
    D, H = wup.shape
    hd = D // 2

    @pl.when(i == 0)
    def _():
        copies = mlp_load(False, w_ref, [(wfirst_ref.at[:, pl.ds(0, D)], wout)], wup, wdown, sems)
        for c in copies:
            c.start()
        aout[...] = jnp.zeros_like(aout)
        aup[...] = jnp.zeros_like(aup)
        adown[...] = jnp.zeros_like(adown)
        vecg_ref[...] = jnp.zeros_like(vecg_ref)
        bupg_ref[...] = jnp.zeros_like(bupg_ref)
        for c in copies:
            c.wait()

    acc[...] = accin_ref[...]
    gh2[...] = gh2in_ref[...]
    cot = cot_ref[0]
    mlp_chunks(hid_ref[0], cot, wup, wdown, bup_ref, acc, gh2, aup, adown, bupg_ref)
    out_ref[0] = acc[0].astype(bf16)
    grad_hidden = gh2[0]
    normed, inv = normalize(mid_ref[0])
    cotf = cot.astype(f32)
    gmid = cotf + norm_back(grad_hidden, normed, inv, vec_ref[1:2, :])
    gmid_ref[0] = gmid
    branch = gmid.astype(bf16)
    vecg_ref[0:1, :] += col_sum(branch.astype(f32))
    vecg_ref[1:2, :] += col_sum(grad_hidden * normed)
    vecg_ref[2:3, :] += col_sum(grad_hidden)
    vecg_ref[3:4, :] += col_sum(cotf)
    aout[...] += dg(mix_ref[0], branch, 0, 0)
    gmix = dg(branch, wout[...], 1, 1).astype(bf16)
    gmix_ref[0] = gmix
    gmixT_ref[0] = gmix.T

    @pl.when(i == pl.num_programs(0) - 1)
    def _():
        wout[...] = aout[...].astype(bf16)
        wup[...] = aup[...].astype(bf16)
        wdown[...] = adown[...].astype(bf16)
        at = pl.multiple_of(core * hd, 128)
        rest = pl.multiple_of((1 - core) * hd, 128)
        extra = [
            (wout.at[:, pl.ds(at, hd)], keep_ref.at[:, pl.ds(H, hd)]),
            (wout.at[:, pl.ds(rest, hd)], send_ref.at[:, pl.ds(H, hd)]),
        ]
        mlp_store(core, wup, wdown, keep_ref, send_ref, extra, sems)


def mlp_specs(tokens):
    B, S, D = tokens.shape
    per = S // RT
    row = pl.BlockSpec((1, RT, D), lambda i: (i // per, i % per, 0))
    col = pl.BlockSpec((1, D, RT), lambda i: (i // per, 0, i % per))
    one = pl.BlockSpec((1, 1, D), lambda i: (i // per, 0, 0))
    return row, col, one, pl.BlockSpec(memory_space=pl.ANY), pl.BlockSpec(memory_space=pltpu.SMEM)


def whole(shape):
    return pl.BlockSpec(shape, lambda i: (0,) * len(shape))


def mlp_first(core, tokens, trow, cot, mixed, vec, bup, weights):
    B, S, D = tokens.shape
    H = bup.shape[1]
    row, col, one, anyspec, smem = mlp_specs(tokens)
    sds = jax.ShapeDtypeStruct
    return pl.pallas_call(
        mlp_first_kernel,
        grid=(B * S // RT,),
        in_specs=[smem, row, one, row, row, whole(vec.shape), whole(bup.shape), anyspec],
        out_specs=[row, row, row, row, whole((1, H)), anyspec, anyspec],
        out_shape=[sds((B, S, D), f32)] * 3 + [sds((B, S, D), bf16), sds((1, H), f32)] + [sds((D, H), bf16)] * 2,
        scratch_shapes=[
            pltpu.VMEM((D, D), bf16),
            pltpu.VMEM((D, H), bf16),
            pltpu.VMEM((H, D), bf16),
            pltpu.VMEM((D, H), f32),
            pltpu.VMEM((H, D), f32),
            pltpu.SemaphoreType.DMA((2 + H // D,)),
        ],
        compiler_params=params(),
        cost_estimate=pl.CostEstimate(flops=13 * B * S * D * H, bytes_accessed=60 * 10**6, transcendentals=0),
        name="mlp_first",
    )(core, tokens, trow, cot, mixed, vec, bup, weights)


def mlp_second(core, acc, gh2, mid, hid, cot, mixed, vec, bup, wfirst, weights):
    B, S, D = cot.shape
    H = bup.shape[1]
    row, col, one, anyspec, smem = mlp_specs(cot)
    sds = jax.ShapeDtypeStruct
    wide = sds((D, H + D // 2), bf16)
    return pl.pallas_call(
        mlp_second_kernel,
        grid=(B * S // RT,),
        in_specs=[smem] + [row] * 6 + [whole(vec.shape), whole(bup.shape), anyspec, anyspec],
        out_specs=[row, row, row, col, whole((4, D)), whole((1, H)), anyspec, anyspec],
        out_shape=[
            sds((B, S, D), bf16),
            sds((B, S, D), f32),
            sds((B, S, D), bf16),
            sds((B, D, S), bf16),
            sds((4, D), f32),
            sds((1, H), f32),
            wide,
            wide,
        ],
        scratch_shapes=[
            pltpu.VMEM((D, D), bf16),
            pltpu.VMEM((D, H), bf16),
            pltpu.VMEM((H, D), bf16),
            pltpu.VMEM((D, D), f32),
            pltpu.VMEM((D, H), f32),
            pltpu.VMEM((H, D), f32),
            pltpu.VMEM((1, RT, D), f32),
            pltpu.VMEM((1, RT, D), f32),
            pltpu.SemaphoreType.DMA((3 + H // D,)),
        ],
        compiler_params=params(),
        cost_estimate=pl.CostEstimate(flops=14 * B * S * D * H, bytes_accessed=60 * 10**6, transcendentals=0),
        name="mlp_second",
    )(core, acc, gh2, mid, hid, cot, mixed, vec, bup, wfirst, weights)


def qkv_back_kernel(core_ref, tok_ref, row_ref, gmid_ref, dq_ref, dk_ref, dv_ref, vec_ref, mine_ref, other_ref,
                    gin_ref, rsum_ref, vecg_ref, keep_ref, send_ref, w_ref, aw_ref, sems):
    b = pl.program_id(0)
    i = pl.program_id(1)
    core = core_ref[0]
    D = tok_ref.shape[2]

    @pl.when((b == 0) & (i == 0))
    def _():
        copies = place_halves(mine_ref, other_ref, w_ref, core, sems)
        for c in copies:
            c.start()
        aw_ref[...] = jnp.zeros_like(aw_ref)
        vecg_ref[...] = jnp.zeros_like(vecg_ref)
        for c in copies:
            c.wait()

    @pl.when(i == 0)
    def _():
        rsum_ref[...] = jnp.zeros_like(rsum_ref)

    base = tok_ref[0].astype(f32) + row_ref[0]
    normed, inv = normalize(base)
    hidden = (normed * vec_ref[0:1, :] + vec_ref[1:2, :]).astype(bf16)
    grads = (dq_ref[0], dk_ref[0], dv_ref[0])
    grad_hidden = None
    for n, g in enumerate(grads):
        cols = slice(n * D, (n + 1) * D)
        part = dg(g, w_ref[:, cols], 1, 1)
        grad_hidden = part if grad_hidden is None else grad_hidden + part
        aw_ref[:, cols] += dg(hidden, g, 0, 0)
    gbase = gmid_ref[0] + norm_back(grad_hidden, normed, inv, vec_ref[0:1, :])
    gin_ref[0] = gbase.astype(bf16)
    rsum_ref[0] += col_sum(gbase)
    vecg_ref[0:1, :] += col_sum(grad_hidden * normed)
    vecg_ref[1:2, :] += col_sum(grad_hidden)
    vecg_ref[2:3, :] += col_sum(grads[0].astype(f32))
    vecg_ref[3:4, :] += col_sum(grads[2].astype(f32))

    @pl.when((b == pl.num_programs(0) - 1) & (i == pl.num_programs(1) - 1))
    def _():
        w_ref[...] = aw_ref[...].astype(bf16)
        half = keep_ref.shape[1]
        at = pl.multiple_of(core * half, 128)
        rest = pl.multiple_of((1 - core) * half, 128)
        copies = (
            pltpu.make_async_copy(w_ref.at[:, pl.ds(at, half)], keep_ref, sems.at[0]),
            pltpu.make_async_copy(w_ref.at[:, pl.ds(rest, half)], send_ref, sems.at[1]),
        )
        for c in copies:
            c.start()
        for c in copies:
            c.wait()


def qkv_back_call(core, tokens, trow, gmid, dq, dk, dv, vec, mine, other):
    B, S, D = tokens.shape
    row = pl.BlockSpec((1, RT, D), lambda b, i: (b, i, 0))
    seq = pl.BlockSpec((1, 1, D), lambda b, i: (b, 0, 0))
    anyspec = pl.BlockSpec(memory_space=pl.ANY)
    sds = jax.ShapeDtypeStruct
    return pl.pallas_call(
        qkv_back_kernel,
        grid=(B, S // RT),
        in_specs=[
            pl.BlockSpec(memory_space=pltpu.SMEM),
            row,
            seq,
            row,
            row,
            row,
            row,
            pl.BlockSpec(vec.shape, lambda b, i: (0, 0)),
            anyspec,
            anyspec,
        ],
        out_specs=[row, seq, pl.BlockSpec((4, D), lambda b, i: (0, 0)), anyspec, anyspec],
        out_shape=[
            sds((B, S, D), bf16),
            sds((B, 1, D), f32),
            sds((4, D), f32),
            sds(mine.shape, bf16),
            sds(mine.shape, bf16),
        ],
        scratch_shapes=[
            pltpu.VMEM((D, 3 * D), bf16),
            pltpu.VMEM((D, 3 * D), f32),
            pltpu.SemaphoreType.DMA((2,)),
        ],
        compiler_params=params(),
        cost_estimate=pl.CostEstimate(flops=12 * B * S * D * D, bytes_accessed=40 * 10**6, transcendentals=0),
        name="norm_qkv_back",
    )(core, tokens, trow, gmid, dq, dk, dv, vec, mine, other)


def key_ranges(segment_ids):
    B, S = segment_ids.shape
    tiles = segment_ids.reshape(B, S // QT, QT)
    before = jnp.sum((segment_ids[:, None, :] < tiles[:, :, :1]).astype(jnp.int32), axis=-1)
    upto = jnp.sum((segment_ids[:, None, :] <= tiles[:, :, -1:]).astype(jnp.int32), axis=-1)
    return (before // KT).reshape(-1), ((upto + KT - 1) // KT).reshape(-1)


def own_slice(array, index, size, axis):
    return lax.dynamic_slice_in_dim(array, index * size, size, axis)


def swap(array, axis):
    return lax.ppermute(array, axis, [(0, 1), (1, 0)])


def all_sum(array, axis):
    size = lax.axis_size(axis)
    step = 1
    while step < size:
        came = lax.ppermute(array, axis, [(i, i ^ step) for i in range(size)])
        array = (array.astype(f32) + came.astype(f32)).astype(array.dtype)
        step *= 2
    return array


def gather_small(array, axis):
    size, me = lax.axis_size(axis), lax.axis_index(axis)
    step = 1
    while step < size:
        came = lax.ppermute(array, axis, [(i, i ^ step) for i in range(size)])
        low = (me & step) == 0
        array = jnp.concatenate([jnp.where(low, array, came), jnp.where(low, came, array)], axis=0)
        step *= 2
    return array


def scatter_small(array, axis):
    size, me = lax.axis_size(axis), lax.axis_index(axis)
    step = size // 2
    while step >= 1:
        half = array.shape[0] // 2
        low = (me & step) == 0
        keep = jnp.where(low, array[:half], array[half:])
        send = jnp.where(low, array[half:], array[:half])
        array = keep + lax.ppermute(send, axis, [(i, i ^ step) for i in range(size)])
        step //= 2
    return array


EXTRA = 8


def split_rows(values, width):
    high = lax.reduce_precision(values, 8, 7)
    parts = jnp.concatenate([high, values - high], axis=-2).astype(bf16)
    pad = [(0, 0)] * (parts.ndim - 1) + [(0, width - parts.shape[-1])]
    return jnp.pad(parts, pad)


def exchange_reduce(array, extra, axis):
    size = lax.axis_size(axis)
    rows, width = array.shape[0] // size, array.shape[1]
    extra = jnp.pad(extra, ((0, 0), (0, EXTRA - extra.shape[1]), (0, 0)))
    sent = jnp.concatenate([array.reshape(size, rows, width), extra], axis=1)
    came = lax.all_to_all(sent.reshape(size * (rows + EXTRA), width), axis, 0, 0, tiled=True)
    came = came.reshape(size, rows + EXTRA, width)
    return jnp.sum(came[:, :rows].astype(f32), axis=0).astype(bf16), came[:, rows:].astype(f32)


def on_device(
    tokens,
    cot,
    segment_ids,
    block_map,
    timesteps,
    step_table,
    ln1_gain,
    ln1_bias,
    w_query,
    b_query,
    w_key,
    w_value,
    b_value,
    w_out,
    b_out,
    ln2_gain,
    ln2_bias,
    w_up,
    b_up,
    w_down,
    b_down,
):
    B, S, D = tokens.shape
    n = lax.axis_size("shard")
    me = lax.axis_index("shard")
    core = lax.axis_index("core")
    own = ln1_gain.shape[0]
    FF = b_up.shape[0] * n
    hd = D // 2
    core1 = core.reshape(1).astype(jnp.int32)

    H = FF // 2
    J = FF // D
    thin = own // 2
    qkv_local = own_slice(jnp.concatenate([w_query, w_key, w_value], axis=1), core, 3 * hd, 1)
    qkv_mine = lax.all_gather(qkv_local, "shard", axis=0, tiled=True)
    up_core = own_slice(w_up, core, thin, 0).reshape(thin, n, 2, J, thin)
    up_core = up_core.transpose(0, 3, 1, 2, 4).reshape(thin, FF)
    out_core = own_slice(w_out, core, thin, 0)
    down_core = own_slice(w_down, core, J * thin, 0)
    down_core = [down_core[j * thin : (j + 1) * thin] for j in range(J)]
    local_a = jnp.concatenate([out_core, up_core[:, :H]] + down_core[: J // 2], axis=1)
    local_b = jnp.concatenate([up_core[:, H:]] + down_core[J // 2 :], axis=1)

    small = (ln1_gain, ln1_bias, b_query, b_value, b_out, ln2_gain, ln2_bias, b_down, b_up)
    small = jnp.concatenate([v.astype(f32) for v in small] + [timesteps.astype(f32)])
    packed = gather_small(small[None], "shard")
    g1, s1, bq, bv, bo, g2, s2, bd = [packed[:, i * own : (i + 1) * own].reshape(1, D) for i in range(8)]
    width = 8 * own + FF // n
    bup = packed[:, 8 * own : width].reshape(n, 2, J, thin).transpose(2, 0, 1, 3).reshape(1, FF)
    group = packed[:, width:].reshape(n * B, 1).astype(jnp.int32)
    vec1 = jnp.concatenate([g1, s1], axis=0)
    bias = jnp.concatenate([bq, jnp.zeros_like(bq), bv], axis=1)
    vec2 = jnp.concatenate([bo, g2, s2, bd], axis=0)

    own_rows = step_table.shape[0]
    spots = me * own_rows + lax.broadcasted_iota(jnp.int32, (1, own_rows), 1)
    found = jnp.dot((group == spots).astype(bf16), step_table, preferred_element_type=f32)
    trow = scatter_small(found, "shard").reshape(B, 1, D)
    qkv_mine, trow, vec1 = lax.optimization_barrier((qkv_mine, trow, vec1))
    qkv_other = swap(qkv_mine, "core")
    local_a, qkv_mine = lax.optimization_barrier((local_a, qkv_mine))
    w_a = lax.all_gather(local_a, ("shard", "core"), axis=0, tiled=True)

    lo, hi = key_ranges(segment_ids)
    segk = jnp.broadcast_to(segment_ids[:, :, None], (B, S, 128))
    segq = segment_ids[:, None, :]

    q, k, v, qT, kT, vT = qkv_call(core1, tokens, trow, vec1, bias, qkv_mine, qkv_other)
    mixed, mixedT, lse = attn_fwd(lo, hi, q, k, vT, segk, segq)
    local_b, w_a, mixed = lax.optimization_barrier((local_b, w_a, mixed))
    w_b = lax.all_gather(local_b, ("shard", "core"), axis=0, tiled=True)
    def core_sum(keep, send):
        return (keep.astype(f32) + swap(send, "core").astype(f32)).astype(bf16)

    def finish(part):
        half = all_sum(part, "xrep").astype(bf16)
        other = swap(half, "core").astype(f32)
        half = half.astype(f32)
        return jnp.where(core == 0, half, other), jnp.where(core == 0, other, half)

    acc, gh2, mid, hid, bupg_a, keep, send = mlp_first(core1, tokens, trow, cot, mixed, vec2, bup[:, :H], w_a)
    half_a = core_sum(keep, send)
    part_a = lax.all_to_all(half_a, "shard", 0, 0, tiled=True).reshape(n, own, H)
    part_a = jnp.sum(part_a.astype(f32), axis=0).astype(bf16)
    acc, half_a = lax.optimization_barrier((acc, half_a))
    out, gmid, gmix, gmixT, vecg2, bupg_b, keep, send = mlp_second(
        core1, acc, gh2, mid, hid, cot, mixed, vec2, bup[:, H:], w_a, w_b
    )
    half_b = core_sum(keep, send)
    half_b, part_a = lax.optimization_barrier((half_b, part_a))
    bupg = jnp.concatenate([bupg_a, bupg_b], axis=1)
    bupg = bupg.reshape(J, n, 2, thin).transpose(1, 2, 0, 3).reshape(n, FF // n)
    vectors = jnp.concatenate([vecg2[i].reshape(n, own) for i in range(4)] + [bupg], axis=1)
    part_b, came_b = exchange_reduce(half_b, split_rows(vectors[:, None], half_b.shape[1]), "shard")
    dq, dk, dv = attn_bwd(lo, hi, q, qT, k, kT, v, gmix, gmixT, mixedT, lse, segk, segq, half_b)
    gin, rsum, vecg1, qkv_keep, qkv_send = qkv_back_call(
        core1, tokens, trow, gmid, dq, dk, dv, vec1, qkv_mine, qkv_other
    )
    qkv_half = core_sum(qkv_keep, qkv_send)
    qkv_half, part_b, came_b = lax.optimization_barrier((qkv_half, part_b, came_b))
    vectors = jnp.concatenate([vecg1[i].reshape(n, own) for i in range(4)], axis=1)
    wide = qkv_half.shape[1]
    digits = jnp.stack([timesteps // 32, timesteps % 32], axis=1).astype(f32)
    table_rows = jnp.concatenate([rsum.reshape(B, D), digits], axis=1)
    table_rows = jnp.broadcast_to(split_rows(table_rows, wide)[None], (n, 2 * B, wide))
    extra = jnp.concatenate([split_rows(vectors[:, None], wide), table_rows], axis=1)
    qkv_part, came_q = exchange_reduce(qkv_half, extra, "shard")

    vg_b = jnp.sum(came_b[:, :2], axis=(0, 1))[: 4 * own + FF // n]
    vg_q = jnp.sum(came_q[:, :2], axis=(0, 1))[: 4 * own]
    vg = all_sum(all_sum(jnp.concatenate([vg_q, vg_b])[None], "core"), "xrep").reshape(-1)
    g_bup = vg[8 * own :]
    vg = [vg[i * own : (i + 1) * own] for i in range(8)]
    sums = (came_q[:, 2 : 2 + B] + came_q[:, 2 + B : 2 + 2 * B])[:, :, : D + 2].reshape(n * B, D + 2)
    for axis in ("core", "xrep"):
        sums = gather_small(sums, axis)
    own_rows = step_table.shape[0]
    rows = me * own_rows + lax.broadcasted_iota(jnp.int32, (own_rows, 1), 0)
    steps = 32 * sums[:, D] + sums[:, D + 1]
    match = (rows == steps.astype(jnp.int32)[None, :]).astype(f32)
    g_table = jnp.dot(match, sums[:, :D], precision=lax.Precision.HIGHEST, preferred_element_type=f32)

    a_up, a_down = finish(part_a)
    b_up_, b_down_ = finish(part_b)
    g_up = jnp.concatenate([a_up, b_up_[:, :H]], axis=1)
    g_up = g_up.reshape(own, J, n, 2, thin).transpose(0, 2, 3, 1, 4).reshape(own, FF)
    blocks = jnp.concatenate([a_down, b_down_[:, :H]], axis=1).reshape(2, thin, J, D)
    g_down = blocks.transpose(0, 2, 1, 3).reshape(FF // n, D)
    g_out = jnp.concatenate([b_up_[:, H:], b_down_[:, H:]], axis=1)
    qkv_part, g_up, g_down, g_out = lax.optimization_barrier((qkv_part, g_up, g_down, g_out))
    q_left, q_right = finish(qkv_part)
    g_qkv = jnp.concatenate([q_left, q_right], axis=1)
    g_q, g_k, g_v = g_qkv[:, :D], g_qkv[:, D : 2 * D], g_qkv[:, 2 * D :]
    return (
        out, gin, g_table, vg[0], vg[1], g_q, vg[2], g_k, g_v, vg[3], g_out, vg[4], vg[5], vg[6], g_up, g_bup, g_down, vg[7],
    )


def solution(mesh):
    rep, shard = mesh.shape["rep"], mesh.shape["shard"]
    fine = Mesh(mesh.devices.reshape(rep // 2, 2, shard), ("xrep", "core", "shard"))
    seqs = ("xrep", "core", "shard")
    mat, vec = P("shard", None), P("shard")
    rows3, rows2 = P(seqs, None, None), P(seqs, None)
    weights = (mat, vec, vec, mat, vec, mat, mat, vec, mat, vec, vec, vec, mat, vec, mat, vec)
    return jax.shard_map(
        on_device,
        mesh=fine,
        in_specs=(rows3, rows3, rows2, rows3, P(seqs)) + weights,
        out_specs=(rows3, rows3) + weights,
        check_vma=False,
    )
```

```python
import functools

import jax
import jax.numpy as jnp
from jax import lax
from jax.experimental import pallas as pl
from jax.experimental.pallas import tpu as pltpu
from jax.sharding import Mesh, PartitionSpec as P

HEADS = 12
HD = 64
QT = 256
KT = 256
RT = 512
MT = 512
MT2 = 512
FC = 768
EPS = 1e-05
NEG = -1e30
LOG2E = 1.4426950408889634
f32 = jnp.float32
bf16 = jnp.bfloat16
VMEM_BYTES = 60 * 1000 * 1024


def dg(x, y, cx, cy):
    return lax.dot_general(x, y, (((cx,), (cy,)), ((), ())), preferred_element_type=f32)


def normalize(values):
    center = values - jnp.mean(values, axis=-1, keepdims=True)
    inv_dev = lax.rsqrt(jnp.mean(center * center, axis=-1, keepdims=True) + EPS)
    return center * inv_dev, inv_dev


def norm_back(grad_hidden, normed, inv_dev, gain_row):
    grad_normed = grad_hidden * gain_row
    return inv_dev * (
        grad_normed
        - jnp.mean(grad_normed, axis=-1, keepdims=True)
        - normed * jnp.mean(grad_normed * normed, axis=-1, keepdims=True)
    )


def col_sum(values):
    return jnp.sum(values, axis=0, keepdims=True)


def gelu_parts(x):
    density = jnp.exp(-0.5 * x * x)
    t = 1.0 / (1.0 + 0.2316418882 * jnp.abs(x))
    poly = t * (0.127414796 + t * (-0.142248368 + t * (0.7107068705 + t * (-0.7265760135 + t * 0.5307027145))))
    tail = density * poly
    cdf = jnp.where(x >= 0.0, 1.0 - tail, tail)
    return x * cdf, cdf + x * (density * 0.3989422804014327)


def place_halves(mine, other, full, core, sems):
    half = mine.shape[1]
    at = pl.multiple_of(core * half, 128)
    rest = pl.multiple_of((1 - core) * half, 128)
    return (
        pltpu.make_async_copy(mine, full.at[:, pl.ds(at, half)], sems.at[0]),
        pltpu.make_async_copy(other, full.at[:, pl.ds(rest, half)], sems.at[1]),
    )


def params(**kw):
    return pltpu.CompilerParams(vmem_limit_bytes=VMEM_BYTES, **kw)


def qkv_kernel(core_ref, tok_ref, row_ref, vec_ref, bias_ref, mine_ref, other_ref,
               q_ref, k_ref, v_ref, qT_ref, kT_ref, vT_ref, hid_ref, w_ref, sems):
    @pl.when((pl.program_id(0) == 0) & (pl.program_id(1) == 0))
    def _():
        copies = place_halves(mine_ref, other_ref, w_ref, core_ref[0], sems)
        for c in copies:
            c.start()
        for c in copies:
            c.wait()

    width = tok_ref.shape[2]
    base = tok_ref[0].astype(f32) + row_ref[0]
    normed, unused = normalize(base)
    hidden = (normed * vec_ref[0:1, :] + vec_ref[1:2, :]).astype(bf16)
    hid_ref[0] = hidden
    scale = HD ** (-0.5)
    for n, (out, outT) in enumerate(((q_ref, qT_ref), (k_ref, kT_ref), (v_ref, vT_ref))):
        cols = slice(n * width, (n + 1) * width)
        exact = dg(hidden, w_ref[:, cols], 1, 0) + bias_ref[:, cols]
        rows = exact.astype(bf16)
        scaled = (rows.astype(f32) * scale).astype(bf16)
        out[0] = (exact * (scale * LOG2E)).astype(bf16) if n == 0 else rows
        outT[0] = (rows if n == 2 else scaled).T


def qkv_call(core, tokens, trow, vec, bias, mine, other):
    B, S, D = tokens.shape
    row = pl.BlockSpec((1, RT, D), lambda b, i: (b, i, 0))
    col = pl.BlockSpec((1, D, RT), lambda b, i: (b, 0, i))
    anyspec = pl.BlockSpec(memory_space=pl.ANY)
    return pl.pallas_call(
        qkv_kernel,
        grid=(B, S // RT),
        in_specs=[
            pl.BlockSpec(memory_space=pltpu.SMEM),
            row,
            pl.BlockSpec((1, 1, D), lambda b, i: (b, 0, 0)),
            pl.BlockSpec(vec.shape, lambda b, i: (0, 0)),
            pl.BlockSpec(bias.shape, lambda b, i: (0, 0)),
            anyspec,
            anyspec,
        ],
        out_specs=[row, row, row, col, col, col, row],
        out_shape=[jax.ShapeDtypeStruct((B, S, D), bf16)] * 3
        + [jax.ShapeDtypeStruct((B, D, S), bf16)] * 3
        + [jax.ShapeDtypeStruct((B, S, D), bf16)],
        scratch_shapes=[pltpu.VMEM((D, 3 * D), bf16), pltpu.SemaphoreType.DMA((2,))],
        compiler_params=params(),
        cost_estimate=pl.CostEstimate(flops=6 * B * S * D * D, bytes_accessed=30 * 10**6, transcendentals=0),
        name="norm_qkv",
    )(core, tokens, trow, vec, bias, mine, other)

def head_mask(h, rows):
    lane=lax.broadcasted_iota(jnp.int32,(rows,256),1)
    return (lane//64)==h

SAVED = True
HPAD = 16


def masked_heads(block):
    return jnp.concatenate([jnp.where(head_mask(j, block.shape[0]), block, jnp.zeros_like(block)) for j in range(4)], axis=0)


def fwd_kernel(lo_ref, hi_ref, q_ref, k_ref, vT_ref, segk_ref, segq_ref,
               mixed_ref, mixedT_ref, prob_ref, fac_ref, acc, mrow, lrow):
    b = pl.program_id(0)
    i = pl.program_id(1)
    nq = pl.num_programs(1)
    segq = segq_ref[0]
    acc[...] = jnp.zeros_like(acc)
    mrow[...] = jnp.full_like(mrow, NEG)
    lrow[...] = jnp.zeros_like(lrow)

    def body(c, carry):
        c0 = pl.multiple_of(c * KT, KT)
        segk = segk_ref[0, pl.ds(c0, KT), :]
        bias = jnp.where(jnp.concatenate([segk, segk], axis=1) == segq, 0.0, NEG)

        def scores(quad):
            cols = slice(quad * 256, (quad + 1) * 256)
            return dg(masked_heads(k_ref[0, pl.ds(c0, KT), cols]), q_ref[0, :, cols], 1, 1)

        ready = scores(0)
        for quad in range(HEADS // 4):
            s4 = ready
            if quad + 1 < HEADS // 4:
                ready = scores(quad + 1)
            for j in range(4):
                h = quad * 4 + j
                rows = slice(h * HD, (h + 1) * HD)
                s = s4[j * KT : (j + 1) * KT] + bias
                m_old = mrow[h : h + 1, :]
                m_new = jnp.maximum(m_old, jnp.max(s, axis=0, keepdims=True))
                p = jnp.exp2(s - m_new)
                alpha = jnp.exp2(m_old - m_new)
                mrow[h : h + 1, :] = m_new
                lrow[h : h + 1, :] = lrow[h : h + 1, :] * alpha + jnp.sum(p, axis=0, keepdims=True)
                pb = p.astype(bf16)
                prob_ref[0, 0, h, pl.ds(c0, KT), :] = pb
                acc[rows, :] = acc[rows, :] * alpha + dg(vT_ref[0, rows, pl.ds(c0, KT)], pb, 1, 0)
        fac_ref[0, 0, c] = mrow[...]
        return carry

    lax.fori_loop(lo_ref[b * nq + i], hi_ref[b * nq + i], body, 0)
    total = lrow[0:HEADS, :]
    inv = 1.0 / total
    lse = mrow[0:HEADS, :] + jnp.log2(total)
    for c in range(fac_ref.shape[2]):
        fac_ref[0, 0, c, 0:HEADS, :] = jnp.exp2(fac_ref[0, 0, c, 0:HEADS, :] - lse)
    for h in range(HEADS):
        rows = slice(h * HD, (h + 1) * HD)
        mixedT_ref[0, rows, :] = acc[rows, :] * inv[h : h + 1, :]
    mixed_ref[0] = mixedT_ref[0].astype(bf16).T


def attn_fwd(lo, hi, q, k, vT, segk, segq):
    B, S, D = q.shape
    nq = S // QT
    nk = S // KT
    row = pl.BlockSpec((1, QT, D), lambda b, i, *_: (b, i, 0))
    col = pl.BlockSpec((1, D, QT), lambda b, i, *_: (b, 0, i))
    sds = jax.ShapeDtypeStruct
    return pl.pallas_call(
        fwd_kernel,
        grid_spec=pltpu.PrefetchScalarGridSpec(
            num_scalar_prefetch=2,
            grid=(B, nq),
            in_specs=[
                row,
                pl.BlockSpec((1, S, D), lambda b, i, *_: (b, 0, 0)),
                pl.BlockSpec((1, D, S), lambda b, i, *_: (b, 0, 0)),
                pl.BlockSpec((1, S, 128), lambda b, i, *_: (b, 0, 0)),
                pl.BlockSpec((1, 1, QT), lambda b, i, *_: (b, 0, i)),
            ],
            out_specs=[
                row,
                col,
                pl.BlockSpec((1, 1, HEADS, S, QT), lambda b, i, *_: (b, i, 0, 0, 0)),
                pl.BlockSpec((1, 1, nk, HPAD, QT), lambda b, i, *_: (b, i, 0, 0, 0)),
            ],
            scratch_shapes=[pltpu.VMEM((D, QT), f32), pltpu.VMEM((HPAD, QT), f32), pltpu.VMEM((HPAD, QT), f32)],
        ),
        out_shape=[
            sds((B, S, D), bf16),
            sds((B, D, S), f32),
            sds((B, nq, HEADS, S, QT), bf16),
            sds((B, nq, nk, HPAD, QT), f32),
        ],
        compiler_params=params(),
        cost_estimate=pl.CostEstimate(flops=16 * B * S * S * D, bytes_accessed=80 * 10**6, transcendentals=0),
        name="attn_fwd",
    )(lo, hi, q, k, vT, segk, segq)


def bwd_kernel(lo_ref, hi_ref, qT_ref, kT_ref, v_ref, do_ref, doT_ref, oT_ref, prob_ref, fac_ref, after_ref,
               dq_ref, dk_ref, dv_ref, dqT, dkT, dvT, dlt):
    b = pl.program_id(0)
    i = pl.program_id(1)
    nq = pl.num_programs(1)

    @pl.when(i == 0)
    def _():
        dkT[...] = jnp.zeros_like(dkT)
        dvT[...] = jnp.zeros_like(dvT)

    dqT[...] = jnp.zeros_like(dqT)
    for h in range(HEADS):
        rows = slice(h * HD, (h + 1) * HD)
        dlt[h : h + 1, :] = jnp.sum(doT_ref[0, rows, :].astype(f32) * oT_ref[0, rows, :], axis=0, keepdims=True)

    def body(c, carry):
        c0 = pl.multiple_of(c * KT, KT)
        keys = pl.ds(c0, KT)

        def products(quad):
            cols = slice(quad * 256, (quad + 1) * 256)
            return dg(masked_heads(v_ref[0, keys, cols]), do_ref[0, :, cols], 1, 1)

        ready = products(0)
        for quad in range(HEADS // 4):
            dp4 = ready
            if quad + 1 < HEADS // 4:
                ready = products(quad + 1)
            for j in range(4):
                h = quad * 4 + j
                rows = slice(h * HD, (h + 1) * HD)
                factor = fac_ref[0, 0, c, h : h + 1, :]
                pb = prob_ref[0, 0, h, keys, :]
                ds = (pb.astype(f32) * ((dp4[j * KT : (j + 1) * KT] - dlt[h : h + 1, :]) * factor)).astype(bf16)
                scaled = (doT_ref[0, rows, :].astype(f32) * factor).astype(bf16)
                dvT[rows, keys] += dg(scaled, pb, 1, 1)
                dkT[rows, keys] += dg(qT_ref[0, rows, :], ds, 1, 1)
                dqT[rows, :] += dg(kT_ref[0, rows, keys], ds, 1, 0)
        return carry

    lax.fori_loop(lo_ref[b * nq + i], hi_ref[b * nq + i], body, 0)
    dq_ref[0] = dqT[...].astype(bf16).T

    @pl.when(i == nq - 1)
    def _():
        dk_ref[0] = dkT[...].astype(bf16).T
        dv_ref[0] = dvT[...].astype(bf16).T


def attn_bwd(lo, hi, qT, kT, v, do, doT, oT, prob, fac, after):
    B, S, D = v.shape
    nq = S // QT
    nk = S // KT
    row = pl.BlockSpec((1, QT, D), lambda b, i, *_: (b, i, 0))
    col = pl.BlockSpec((1, D, QT), lambda b, i, *_: (b, 0, i))
    full = pl.BlockSpec((1, S, D), lambda b, i, *_: (b, 0, 0))
    fullT = pl.BlockSpec((1, D, S), lambda b, i, *_: (b, 0, 0))
    return pl.pallas_call(
        bwd_kernel,
        grid_spec=pltpu.PrefetchScalarGridSpec(
            num_scalar_prefetch=2,
            grid=(B, nq),
            in_specs=[
                col,
                fullT,
                full,
                row,
                col,
                col,
                pl.BlockSpec((1, 1, HEADS, S, QT), lambda b, i, *_: (b, i, 0, 0, 0)),
                pl.BlockSpec((1, 1, nk, HPAD, QT), lambda b, i, *_: (b, i, 0, 0, 0)),
                pl.BlockSpec(memory_space=pl.ANY),
            ],
            out_specs=[row, full, full],
            scratch_shapes=[
                pltpu.VMEM((D, QT), f32),
                pltpu.VMEM((D, S), f32),
                pltpu.VMEM((D, S), f32),
                pltpu.VMEM((HPAD, QT), f32),
            ],
        ),
        out_shape=[jax.ShapeDtypeStruct((B, S, D), bf16)] * 3,
        compiler_params=params(),
        cost_estimate=pl.CostEstimate(flops=32 * B * S * S * D, bytes_accessed=90 * 10**6, transcendentals=0),
        name="attn_bwd",
    )(lo, hi, qT, kT, v, do, doT, oT, prob, fac, after)


def mlp_chunks(hid, cot, wup, wdown, bup_ref, acc, gh2, aup, adown, bupg_ref):
    count = wup.shape[1] // FC

    def products(j):
        cols = slice(j * FC, (j + 1) * FC)
        return dg(hid, wup[:, cols], 1, 0) + bup_ref[:, cols], dg(cot, wdown[cols, :], 1, 1)

    ready = products(0)
    for j in range(count):
        cols = slice(j * FC, (j + 1) * FC)
        up, ga = ready
        if j + 1 < count:
            ready = products(j + 1)
        active, slope = gelu_parts(up)
        active = active.astype(bf16)
        gu = (ga * slope).astype(bf16)
        acc[0] += dg(active, wdown[cols, :], 1, 0)
        adown[cols, :] += dg(active, cot, 0, 0)
        gh2[0] += dg(gu, wup[:, cols], 1, 1)
        aup[:, cols] += dg(hid, gu, 0, 0)
        bupg_ref[:, cols] += col_sum(gu.astype(f32))


def mlp_load(first, w_ref, extra, wup, wdown, sems):
    D, H = wup.shape
    at = D if first else 0
    pairs = [(w_ref.at[:, pl.ds(at, H)], wup)]
    pairs += [(w_ref.at[:, pl.ds(at + H + j * D, D)], wdown.at[pl.ds(j * D, D), :]) for j in range(H // D)]
    pairs += extra
    return [pltpu.make_async_copy(src, dst, sems.at[n]) for n, (src, dst) in enumerate(pairs)]


def mlp_store(core, wup, wdown, keep_ref, send_ref, extra, sems):
    D, H = wup.shape

    def run(up_to, down_to):
        pairs = [(wup, up_to.at[:, pl.ds(0, H)])]
        pairs += [(wdown.at[pl.ds(j * D, D), :], down_to.at[:, pl.ds(j * D, D)]) for j in range(H // D)]
        pairs += extra
        made = [pltpu.make_async_copy(src, dst, sems.at[n]) for n, (src, dst) in enumerate(pairs)]
        for c in made:
            c.start()
        for c in made:
            c.wait()

    @pl.when(core == 0)
    def _():
        run(keep_ref, send_ref)

    @pl.when(core != 0)
    def _():
        run(send_ref, keep_ref)


def mlp_first_kernel(core_ref, tok_ref, row_ref, cot_ref, mix_ref, vec_ref, bup_ref, w_ref,
                     acc_ref, gh2_ref, mid_ref, hid_ref, bupg_ref, keep_ref, send_ref,
                     wout, wup, wdown, aup, adown, acc, gh2, sems):
    i = pl.program_id(0)
    D = tok_ref.shape[2]

    @pl.when(i == 0)
    def _():
        copies = mlp_load(True, w_ref, [(w_ref.at[:, pl.ds(0, D)], wout)], wup, wdown, sems)
        for c in copies:
            c.start()
        aup[...] = jnp.zeros_like(aup)
        adown[...] = jnp.zeros_like(adown)
        bupg_ref[...] = jnp.zeros_like(bupg_ref)
        for c in copies:
            c.wait()

    base = tok_ref[0].astype(f32) + row_ref[0]
    middle = base + dg(mix_ref[0], wout[...], 1, 0) + vec_ref[0:1, :]
    mid_ref[0] = middle
    normed, unused = normalize(middle)
    hid_ref[0] = (normed * vec_ref[1:2, :] + vec_ref[2:3, :]).astype(bf16)
    acc[...] = jnp.zeros_like(acc)
    gh2[...] = jnp.zeros_like(gh2)
    mlp_chunks(hid_ref[0], cot_ref[0], wup, wdown, bup_ref, acc, gh2, aup, adown, bupg_ref)
    acc_ref[...] = acc[...].astype(bf16)
    gh2_ref[...] = gh2[...].astype(bf16)

    @pl.when(i == pl.num_programs(0) - 1)
    def _():
        wup[...] = aup[...].astype(bf16)
        wdown[...] = adown[...].astype(bf16)
        mlp_store(core_ref[0], wup, wdown, keep_ref, send_ref, [], sems)


def mlp_second_kernel(core_ref, accin_ref, gh2in_ref, mid_ref, hid_ref, cot_ref, mix_ref, vec_ref, bup_ref, wfirst_ref, w_ref,
                      out_ref, gmid_ref, gmix_ref, gmixT_ref, vecg_ref, bupg_ref, keep_ref, send_ref,
                      wout, wup, wdown, aout, aup, adown, acc, gh2, sems):
    i = pl.program_id(0)
    core = core_ref[0]
    D, H = wup.shape
    hd = D // 2

    @pl.when(i == 0)
    def _():
        copies = mlp_load(False, w_ref, [(wfirst_ref.at[:, pl.ds(0, D)], wout)], wup, wdown, sems)
        for c in copies:
            c.start()
        aout[...] = jnp.zeros_like(aout)
        aup[...] = jnp.zeros_like(aup)
        adown[...] = jnp.zeros_like(adown)
        vecg_ref[...] = jnp.zeros_like(vecg_ref)
        bupg_ref[...] = jnp.zeros_like(bupg_ref)
        for c in copies:
            c.wait()

    acc[...] = accin_ref[...].astype(f32) + mid_ref[...] + vec_ref[3:4, :]
    gh2[...] = gh2in_ref[...].astype(f32)
    cot = cot_ref[0]
    mlp_chunks(hid_ref[0], cot, wup, wdown, bup_ref, acc, gh2, aup, adown, bupg_ref)
    out_ref[0] = acc[0].astype(bf16)
    grad_hidden = gh2[0]
    normed, inv = normalize(mid_ref[0])
    cotf = cot.astype(f32)
    gmid = cotf + norm_back(grad_hidden, normed, inv, vec_ref[1:2, :])
    gmid_ref[0] = gmid
    branch = gmid.astype(bf16)
    vecg_ref[0:1, :] += col_sum(branch.astype(f32))
    vecg_ref[1:2, :] += col_sum(grad_hidden * normed)
    vecg_ref[2:3, :] += col_sum(grad_hidden)
    vecg_ref[3:4, :] += col_sum(cotf)
    aout[...] += dg(mix_ref[0], branch, 0, 0)
    gmix = dg(branch, wout[...], 1, 1).astype(bf16)
    gmix_ref[0] = gmix
    gmixT_ref[0] = gmix.T

    @pl.when(i == pl.num_programs(0) - 1)
    def _():
        wout[...] = aout[...].astype(bf16)
        wup[...] = aup[...].astype(bf16)
        wdown[...] = adown[...].astype(bf16)
        at = pl.multiple_of(core * hd, 128)
        rest = pl.multiple_of((1 - core) * hd, 128)
        extra = [
            (wout.at[:, pl.ds(at, hd)], keep_ref.at[:, pl.ds(H, hd)]),
            (wout.at[:, pl.ds(rest, hd)], send_ref.at[:, pl.ds(H, hd)]),
        ]
        mlp_store(core, wup, wdown, keep_ref, send_ref, extra, sems)


def mlp_specs(tokens, tile):
    B, S, D = tokens.shape
    per = S // tile
    row = pl.BlockSpec((1, tile, D), lambda i: (i // per, i % per, 0))
    col = pl.BlockSpec((1, D, tile), lambda i: (i // per, 0, i % per))
    one = pl.BlockSpec((1, 1, D), lambda i: (i // per, 0, 0))
    return row, col, one, pl.BlockSpec(memory_space=pl.ANY), pl.BlockSpec(memory_space=pltpu.SMEM)


def whole(shape):
    return pl.BlockSpec(shape, lambda i: (0,) * len(shape))


def mlp_first(core, tokens, trow, cot, mixed, vec, bup, weights):
    B, S, D = tokens.shape
    H = bup.shape[1]
    row, col, one, anyspec, smem = mlp_specs(tokens, MT)
    sds = jax.ShapeDtypeStruct
    return pl.pallas_call(
        mlp_first_kernel,
        grid=(B * S // MT,),
        in_specs=[smem, row, one, row, row, whole(vec.shape), whole(bup.shape), anyspec],
        out_specs=[row, row, row, row, whole((1, H)), anyspec, anyspec],
        out_shape=[sds((B, S, D), bf16)] * 2 + [sds((B, S, D), f32), sds((B, S, D), bf16), sds((1, H), f32)] + [sds((D, H), bf16)] * 2,
        scratch_shapes=[
            pltpu.VMEM((D, D), bf16),
            pltpu.VMEM((D, H), bf16),
            pltpu.VMEM((H, D), bf16),
            pltpu.VMEM((D, H), f32),
            pltpu.VMEM((H, D), f32),
            pltpu.VMEM((1, MT, D), f32),
            pltpu.VMEM((1, MT, D), f32),
            pltpu.SemaphoreType.DMA((2 + H // D,)),
        ],
        compiler_params=params(),
        cost_estimate=pl.CostEstimate(flops=13 * B * S * D * H, bytes_accessed=60 * 10**6, transcendentals=0),
        name="mlp_first",
    )(core, tokens, trow, cot, mixed, vec, bup, weights)


def mlp_second(core, acc, gh2, mid, hid, cot, mixed, vec, bup, wfirst, weights):
    B, S, D = cot.shape
    H = bup.shape[1]
    row, col, one, anyspec, smem = mlp_specs(cot, MT2)
    sds = jax.ShapeDtypeStruct
    wide = sds((D, H + D // 2), bf16)
    return pl.pallas_call(
        mlp_second_kernel,
        grid=(B * S // MT2,),
        in_specs=[smem] + [row] * 6 + [whole(vec.shape), whole(bup.shape), anyspec, anyspec],
        out_specs=[row, row, row, col, whole((4, D)), whole((1, H)), anyspec, anyspec],
        out_shape=[
            sds((B, S, D), bf16),
            sds((B, S, D), f32),
            sds((B, S, D), bf16),
            sds((B, D, S), bf16),
            sds((4, D), f32),
            sds((1, H), f32),
            wide,
            wide,
        ],
        scratch_shapes=[
            pltpu.VMEM((D, D), bf16),
            pltpu.VMEM((D, H), bf16),
            pltpu.VMEM((H, D), bf16),
            pltpu.VMEM((D, D), f32),
            pltpu.VMEM((D, H), f32),
            pltpu.VMEM((H, D), f32),
            pltpu.VMEM((1, MT2, D), f32),
            pltpu.VMEM((1, MT2, D), f32),
            pltpu.SemaphoreType.DMA((3 + H // D,)),
        ],
        compiler_params=params(),
        cost_estimate=pl.CostEstimate(flops=14 * B * S * D * H, bytes_accessed=60 * 10**6, transcendentals=0),
        name="mlp_second",
    )(core, acc, gh2, mid, hid, cot, mixed, vec, bup, wfirst, weights)


def qkv_weights_kernel(core_ref, hid_ref, dq_ref, dk_ref, dv_ref, keep_ref, send_ref, aw_ref, low_ref, sems):
    b = pl.program_id(0)
    i = pl.program_id(1)
    core = core_ref[0]
    D = hid_ref.shape[2]

    @pl.when((b == 0) & (i == 0))
    def _():
        aw_ref[...] = jnp.zeros_like(aw_ref)

    for n, g in enumerate((dq_ref[0], dk_ref[0], dv_ref[0])):
        aw_ref[:, n * D : (n + 1) * D] += dg(hid_ref[0], g, 0, 0)

    @pl.when((b == pl.num_programs(0) - 1) & (i == pl.num_programs(1) - 1))
    def _():
        low_ref[...] = aw_ref[...].astype(bf16)
        half = keep_ref.shape[1]
        at = pl.multiple_of(core * half, 128)
        rest = pl.multiple_of((1 - core) * half, 128)
        copies = (
            pltpu.make_async_copy(low_ref.at[:, pl.ds(at, half)], keep_ref, sems.at[0]),
            pltpu.make_async_copy(low_ref.at[:, pl.ds(rest, half)], send_ref, sems.at[1]),
        )
        for c in copies:
            c.start()
        for c in copies:
            c.wait()


def qkv_weights_call(core, hid, dq, dk, dv):
    B, S, D = hid.shape
    row = pl.BlockSpec((1, S, D), lambda b, i: (b, i, 0))
    anyspec = pl.BlockSpec(memory_space=pl.ANY)
    half = jax.ShapeDtypeStruct((D, 3 * D // 2), bf16)
    return pl.pallas_call(
        qkv_weights_kernel,
        grid=(B, 1),
        in_specs=[pl.BlockSpec(memory_space=pltpu.SMEM), row, row, row, row],
        out_specs=[anyspec, anyspec],
        out_shape=[half, half],
        scratch_shapes=[pltpu.VMEM((D, 3 * D), f32), pltpu.VMEM((D, 3 * D), bf16), pltpu.SemaphoreType.DMA((2,))],
        compiler_params=params(),
        cost_estimate=pl.CostEstimate(flops=6 * B * S * D * D, bytes_accessed=20 * 10**6, transcendentals=0),
        name="qkv_weights",
    )(core, hid, dq, dk, dv)


def qkv_back_kernel(core_ref, tok_ref, row_ref, gmid_ref, dq_ref, dk_ref, dv_ref, vec_ref, mine_ref, other_ref, after_ref,
                    gin_ref, rsum_ref, vecg_ref, w_ref, sems):
    b = pl.program_id(0)
    i = pl.program_id(1)

    @pl.when((b == 0) & (i == 0))
    def _():
        copies = place_halves(mine_ref, other_ref, w_ref, core_ref[0], sems)
        for c in copies:
            c.start()
        vecg_ref[...] = jnp.zeros_like(vecg_ref)
        for c in copies:
            c.wait()

    @pl.when(i == 0)
    def _():
        rsum_ref[...] = jnp.zeros_like(rsum_ref)

    grads = (dq_ref[0], dk_ref[0], dv_ref[0])
    grad_hidden = dg(jnp.concatenate(grads, axis=1), w_ref[...], 1, 1)
    base = tok_ref[0].astype(f32) + row_ref[0]
    normed, inv = normalize(base)
    gbase = gmid_ref[0] + norm_back(grad_hidden, normed, inv, vec_ref[0:1, :])
    gin_ref[0] = gbase.astype(bf16)
    rsum_ref[0] += col_sum(gbase)
    vecg_ref[0:1, :] += col_sum(grad_hidden * normed)
    vecg_ref[1:2, :] += col_sum(grad_hidden)
    vecg_ref[2:3, :] += col_sum(grads[0].astype(f32))
    vecg_ref[3:4, :] += col_sum(grads[2].astype(f32))


def qkv_back_call(core, tokens, trow, gmid, dq, dk, dv, vec, mine, other, after):
    B, S, D = tokens.shape
    row = pl.BlockSpec((1, RT, D), lambda b, i: (b, i, 0))
    seq = pl.BlockSpec((1, 1, D), lambda b, i: (b, 0, 0))
    anyspec = pl.BlockSpec(memory_space=pl.ANY)
    sds = jax.ShapeDtypeStruct
    return pl.pallas_call(
        qkv_back_kernel,
        grid=(B, S // RT),
        in_specs=[
            pl.BlockSpec(memory_space=pltpu.SMEM),
            row,
            seq,
            row,
            row,
            row,
            row,
            pl.BlockSpec(vec.shape, lambda b, i: (0, 0)),
            anyspec,
            anyspec,
            anyspec,
        ],
        out_specs=[row, seq, pl.BlockSpec((4, D), lambda b, i: (0, 0))],
        out_shape=[sds((B, S, D), bf16), sds((B, 1, D), f32), sds((4, D), f32)],
        scratch_shapes=[pltpu.VMEM((D, 3 * D), bf16), pltpu.SemaphoreType.DMA((2,))],
        compiler_params=params(),
        cost_estimate=pl.CostEstimate(flops=6 * B * S * D * D, bytes_accessed=40 * 10**6, transcendentals=0),
        name="norm_qkv_back",
    )(core, tokens, trow, gmid, dq, dk, dv, vec, mine, other, after)


def key_ranges(segment_ids):
    B, S = segment_ids.shape
    tiles = segment_ids.reshape(B, S // QT, QT)
    before = jnp.sum((segment_ids[:, None, :] < tiles[:, :, :1]).astype(jnp.int32), axis=-1)
    upto = jnp.sum((segment_ids[:, None, :] <= tiles[:, :, -1:]).astype(jnp.int32), axis=-1)
    return (before // KT).reshape(-1), ((upto + KT - 1) // KT).reshape(-1)


def own_slice(array, index, size, axis):
    return lax.dynamic_slice_in_dim(array, index * size, size, axis)


def swap(array, axis):
    return lax.ppermute(array, axis, [(0, 1), (1, 0)])


def all_sum(array, axis):
    size = lax.axis_size(axis)
    step = 1
    while step < size:
        came = lax.ppermute(array, axis, [(i, i ^ step) for i in range(size)])
        array = (array.astype(f32) + came.astype(f32)).astype(array.dtype)
        step *= 2
    return array


def gather_small(array, axis):
    size, me = lax.axis_size(axis), lax.axis_index(axis)
    step = 1
    while step < size:
        came = lax.ppermute(array, axis, [(i, i ^ step) for i in range(size)])
        low = (me & step) == 0
        array = jnp.concatenate([jnp.where(low, array, came), jnp.where(low, came, array)], axis=0)
        step *= 2
    return array


def scatter_small(array, axis):
    size, me = lax.axis_size(axis), lax.axis_index(axis)
    step = size // 2
    while step >= 1:
        half = array.shape[0] // 2
        low = (me & step) == 0
        keep = jnp.where(low, array[:half], array[half:])
        send = jnp.where(low, array[half:], array[:half])
        array = keep + lax.ppermute(send, axis, [(i, i ^ step) for i in range(size)])
        step //= 2
    return array


EXTRA = 8


def split_rows(values, width):
    high = lax.reduce_precision(values, 8, 7)
    parts = jnp.concatenate([high, values - high], axis=-2).astype(bf16)
    pad = [(0, 0)] * (parts.ndim - 1) + [(0, width - parts.shape[-1])]
    return jnp.pad(parts, pad)


def exchange_reduce(array, extra, axis):
    size = lax.axis_size(axis)
    rows, width = array.shape[0] // size, array.shape[1]
    extra = jnp.pad(extra, ((0, 0), (0, EXTRA - extra.shape[1]), (0, 0)))
    sent = jnp.concatenate([array.reshape(size, rows, width), extra], axis=1)
    came = lax.all_to_all(sent.reshape(size * (rows + EXTRA), width), axis, 0, 0, tiled=True)
    came = came.reshape(size, rows + EXTRA, width)
    return jnp.sum(came[:, :rows].astype(f32), axis=0).astype(bf16), came[:, rows:].astype(f32)


def direct_exchange(array, axis):
    size, me = lax.axis_size(axis), lax.axis_index(axis)
    came = [own_slice(array, me, 1, 0)]
    for r in range(1, size):
        came.append(lax.ppermute(own_slice(array, me ^ r, 1, 0), axis, [(i, i ^ r) for i in range(size)]))
    return jnp.concatenate(came, axis=0)


def on_device(
    tokens,
    cot,
    segment_ids,
    block_map,
    timesteps,
    step_table,
    ln1_gain,
    ln1_bias,
    w_query,
    b_query,
    w_key,
    w_value,
    b_value,
    w_out,
    b_out,
    ln2_gain,
    ln2_bias,
    w_up,
    b_up,
    w_down,
    b_down,
):
    B, S, D = tokens.shape
    n = lax.axis_size("shard")
    me = lax.axis_index("shard")
    core = lax.axis_index("core")
    own = ln1_gain.shape[0]
    FF = b_up.shape[0] * n
    hd = D // 2
    core1 = core.reshape(1).astype(jnp.int32)

    H = FF // 2
    J = FF // D
    thin = own // 2
    qkv_local = own_slice(jnp.concatenate([w_query, w_key, w_value], axis=1), core, 3 * hd, 1)
    qkv_mine = lax.all_gather(qkv_local, "shard", axis=0, tiled=True)
    up_core = own_slice(w_up, core, thin, 0).reshape(thin, n, 2, J, thin)
    up_core = up_core.transpose(0, 3, 1, 2, 4).reshape(thin, FF)
    out_core = own_slice(w_out, core, thin, 0)
    down_core = own_slice(w_down, core, J * thin, 0)
    down_core = [down_core[j * thin : (j + 1) * thin] for j in range(J)]
    local_a = jnp.concatenate([out_core, up_core[:, :H]] + down_core[: J // 2], axis=1)
    local_b = jnp.concatenate([up_core[:, H:]] + down_core[J // 2 :], axis=1)

    small = (ln1_gain, ln1_bias, b_query, b_value, b_out, ln2_gain, ln2_bias, b_down, b_up)
    small = jnp.concatenate([v.astype(f32) for v in small] + [timesteps.astype(f32)])
    packed = gather_small(small[None], "shard")
    g1, s1, bq, bv, bo, g2, s2, bd = [packed[:, i * own : (i + 1) * own].reshape(1, D) for i in range(8)]
    width = 8 * own + FF // n
    bup = packed[:, 8 * own : width].reshape(n, 2, J, thin).transpose(2, 0, 1, 3).reshape(1, FF)
    group = packed[:, width:].reshape(n * B, 1).astype(jnp.int32)
    vec1 = jnp.concatenate([g1, s1], axis=0)
    bias = jnp.concatenate([bq, jnp.zeros_like(bq), bv], axis=1)
    vec2 = jnp.concatenate([bo, g2, s2, bd], axis=0)

    own_rows = step_table.shape[0]
    spots = me * own_rows + lax.broadcasted_iota(jnp.int32, (1, own_rows), 1)
    found = jnp.dot((group == spots).astype(bf16), step_table, preferred_element_type=f32)
    trow = scatter_small(found, "shard").reshape(B, 1, D)
    qkv_mine, trow, vec1 = lax.optimization_barrier((qkv_mine, trow, vec1))
    qkv_other = swap(qkv_mine, "core")
    local_a, qkv_mine = lax.optimization_barrier((local_a, qkv_mine))
    w_a = lax.all_gather(local_a, ("shard", "core"), axis=0, tiled=True)

    lo, hi = key_ranges(segment_ids)
    segk = jnp.broadcast_to(segment_ids[:, :, None], (B, S, 128))
    segq = segment_ids[:, None, :]

    q, k, v, qT, kT, vT, hid1 = qkv_call(core1, tokens, trow, vec1, bias, qkv_mine, qkv_other)
    mixed, mixedT, prob, fac = attn_fwd(lo, hi, q, k, vT, segk, segq)
    local_b, w_a, mixed = lax.optimization_barrier((local_b, w_a, mixed))
    w_b = lax.all_gather(local_b, ("shard", "core"), axis=0, tiled=True)
    def core_sum(keep, send):
        return (keep.astype(f32) + swap(send, "core").astype(f32)).astype(bf16)

    def finish(part):
        half = all_sum(part, "xrep").astype(bf16)
        other = swap(half, "core").astype(f32)
        half = half.astype(f32)
        return jnp.where(core == 0, half, other), jnp.where(core == 0, other, half)

    acc, gh2, mid, hid, bupg_a, keep, send = mlp_first(core1, tokens, trow, cot, mixed, vec2, bup[:, :H], w_a)
    half_a = core_sum(keep, send)
    part_a = lax.all_to_all(half_a, "shard", 0, 0, tiled=True).reshape(n, own, H)
    part_a = jnp.sum(part_a.astype(f32), axis=0).astype(bf16)
    acc, half_a = lax.optimization_barrier((acc, half_a))
    out, gmid, gmix, gmixT, vecg2, bupg_b, keep, send = mlp_second(
        core1, acc, gh2, mid, hid, cot, mixed, vec2, bup[:, H:], w_a, w_b
    )
    half_b = core_sum(keep, send)
    half_b, part_a = lax.optimization_barrier((half_b, part_a))
    bupg = jnp.concatenate([bupg_a, bupg_b], axis=1)
    bupg = bupg.reshape(J, n, 2, thin).transpose(1, 2, 0, 3).reshape(n, FF // n)
    vectors = jnp.concatenate([vecg2[i].reshape(n, own) for i in range(4)] + [bupg], axis=1)
    part_b, came_b = exchange_reduce(half_b, split_rows(vectors[:, None], half_b.shape[1]), "shard")
    dq, dk, dv = attn_bwd(lo, hi, qT, kT, v, gmix, gmixT, mixedT, prob, fac, half_b)
    keep, send = qkv_weights_call(core1, hid1, dq, dk, dv)
    qkv_half = core_sum(keep, send)
    qkv_half, part_b, came_b = lax.optimization_barrier((qkv_half, part_b, came_b))
    came = lax.all_to_all(qkv_half, "shard", 0, 0, tiled=True).reshape(n, own, 3 * hd)
    qkv_part = jnp.sum(came.astype(f32), axis=0).astype(bf16)
    gin, rsum, vecg1 = qkv_back_call(
        core1, tokens, trow, gmid, dq, dk, dv, vec1, qkv_mine, qkv_other, qkv_half
    )
    vectors = jnp.concatenate([vecg1[i].reshape(n, own) for i in range(4)], axis=1)
    wide = -(-(D + 2) // 128) * 128
    digits = jnp.stack([timesteps // 32, timesteps % 32], axis=1).astype(f32)
    table_rows = jnp.concatenate([rsum.reshape(B, D), digits], axis=1)
    table_rows = jnp.broadcast_to(jnp.pad(table_rows, ((0, 0), (0, wide - D - 2)))[None], (n, B, wide))
    extra = jnp.concatenate([jnp.pad(vectors, ((0, 0), (0, wide - 4 * own)))[:, None], table_rows], axis=1)
    extra, qkv_part = lax.optimization_barrier((extra, qkv_part))
    came_q = direct_exchange(extra, "shard")

    vg_b = jnp.sum(came_b[:, :2], axis=(0, 1))[: 4 * own + FF // n]
    vg_q = jnp.sum(came_q[:, 0], axis=0)[: 4 * own]
    vg = all_sum(all_sum(jnp.concatenate([vg_q, vg_b])[None], "core"), "xrep").reshape(-1)
    g_bup = vg[8 * own :]
    vg = [vg[i * own : (i + 1) * own] for i in range(8)]
    sums = came_q[:, 1:].reshape(n * B, wide)
    for axis in ("core", "xrep"):
        sums = gather_small(sums, axis)
    own_rows = step_table.shape[0]
    rows = me * own_rows + lax.broadcasted_iota(jnp.int32, (own_rows, 1), 0)
    steps = 32 * sums[:, D] + sums[:, D + 1]
    match = (rows == steps.astype(jnp.int32)[None, :]).astype(f32)
    g_table = jnp.dot(match, sums[:, :D], precision=lax.Precision.HIGHEST, preferred_element_type=f32)

    a_up, a_down = finish(part_a)
    b_up_, b_down_ = finish(part_b)
    g_up = jnp.concatenate([a_up, b_up_[:, :H]], axis=1)
    g_up = g_up.reshape(own, J, n, 2, thin).transpose(0, 2, 3, 1, 4).reshape(own, FF)
    blocks = jnp.concatenate([a_down, b_down_[:, :H]], axis=1).reshape(2, thin, J, D)
    g_down = blocks.transpose(0, 2, 1, 3).reshape(FF // n, D)
    g_out = jnp.concatenate([b_up_[:, H:], b_down_[:, H:]], axis=1)
    q_left, q_right = finish(qkv_part)
    g_qkv = jnp.concatenate([q_left, q_right], axis=1)
    g_q, g_k, g_v = g_qkv[:, :D], g_qkv[:, D : 2 * D], g_qkv[:, 2 * D :]
    return (
        out, gin, g_table, vg[0], vg[1], g_q, vg[2], g_k, g_v, vg[3], g_out, vg[4], vg[5], vg[6], g_up, g_bup, g_down, vg[7],
    )


def solution(mesh):
    rep, shard = mesh.shape["rep"], mesh.shape["shard"]
    fine = Mesh(mesh.devices.reshape(rep // 2, 2, shard), ("xrep", "core", "shard"))
    seqs = ("xrep", "core", "shard")
    mat, vec = P("shard", None), P("shard")
    rows3, rows2 = P(seqs, None, None), P(seqs, None)
    weights = (mat, vec, vec, mat, vec, mat, mat, vec, mat, vec, vec, vec, mat, vec, mat, vec)
    return jax.shard_map(
        on_device,
        mesh=fine,
        in_specs=(rows3, rows3, rows2, rows3, P(seqs)) + weights,
        out_specs=(rows3, rows3) + weights,
        check_vma=False,
    )
```

```python
import functools

import jax
import jax.numpy as jnp
from jax import lax
from jax.experimental import pallas as pl
from jax.experimental.pallas import tpu as pltpu
from jax.sharding import Mesh, PartitionSpec as P

HEADS = 12
HD = 64
QT = 256
KT = 256
RT = 512
MT = 512
MT2 = 512
FC = 768
EPS = 1e-05
NEG = -1e30
LOG2E = 1.4426950408889634
f32 = jnp.float32
bf16 = jnp.bfloat16
VMEM_BYTES = 60 * 1000 * 1024


def dg(x, y, cx, cy):
    return lax.dot_general(x, y, (((cx,), (cy,)), ((), ())), preferred_element_type=f32)


def normalize(values):
    center = values - jnp.mean(values, axis=-1, keepdims=True)
    inv_dev = lax.rsqrt(jnp.mean(center * center, axis=-1, keepdims=True) + EPS)
    return center * inv_dev, inv_dev


def norm_back(grad_hidden, normed, inv_dev, gain_row):
    grad_normed = grad_hidden * gain_row
    return inv_dev * (
        grad_normed
        - jnp.mean(grad_normed, axis=-1, keepdims=True)
        - normed * jnp.mean(grad_normed * normed, axis=-1, keepdims=True)
    )


def col_sum(values):
    return jnp.sum(values, axis=0, keepdims=True)


def gelu_parts(x):
    density = jnp.exp(-0.5 * x * x)
    t = 1.0 / (1.0 + 0.2316418882 * jnp.abs(x))
    poly = t * (0.127414796 + t * (-0.142248368 + t * (0.7107068705 + t * (-0.7265760135 + t * 0.5307027145))))
    tail = density * poly
    cdf = jnp.where(x >= 0.0, 1.0 - tail, tail)
    return x * cdf, cdf + x * (density * 0.3989422804014327)


def place_halves(mine, other, full, core, sems):
    half = mine.shape[1]
    at = pl.multiple_of(core * half, 128)
    rest = pl.multiple_of((1 - core) * half, 128)
    return (
        pltpu.make_async_copy(mine, full.at[:, pl.ds(at, half)], sems.at[0]),
        pltpu.make_async_copy(other, full.at[:, pl.ds(rest, half)], sems.at[1]),
    )


def params(**kw):
    return pltpu.CompilerParams(vmem_limit_bytes=VMEM_BYTES, **kw)


def qkv_kernel(core_ref, tok_ref, row_ref, vec_ref, bias_ref, mine_ref, other_ref,
               q_ref, k_ref, v_ref, qT_ref, kT_ref, vT_ref, hid_ref, w_ref, sems):
    @pl.when((pl.program_id(0) == 0) & (pl.program_id(1) == 0))
    def _():
        copies = place_halves(mine_ref, other_ref, w_ref, core_ref[0], sems)
        for c in copies:
            c.start()
        for c in copies:
            c.wait()

    width = tok_ref.shape[2]
    base = tok_ref[0].astype(f32) + row_ref[0]
    normed, unused = normalize(base)
    hidden = (normed * vec_ref[0:1, :] + vec_ref[1:2, :]).astype(bf16)
    hid_ref[0] = hidden
    scale = HD ** (-0.5)
    for n, (out, outT) in enumerate(((q_ref, qT_ref), (k_ref, kT_ref), (v_ref, vT_ref))):
        cols = slice(n * width, (n + 1) * width)
        exact = dg(hidden, w_ref[:, cols], 1, 0) + bias_ref[:, cols]
        rows = exact.astype(bf16)
        scaled = (rows.astype(f32) * scale).astype(bf16)
        out[0] = (exact * (scale * LOG2E)).astype(bf16) if n == 0 else rows
        outT[0] = (rows if n == 2 else scaled).T


def qkv_call(core, tokens, trow, vec, bias, mine, other):
    B, S, D = tokens.shape
    row = pl.BlockSpec((1, RT, D), lambda b, i: (b, i, 0))
    col = pl.BlockSpec((1, D, RT), lambda b, i: (b, 0, i))
    anyspec = pl.BlockSpec(memory_space=pl.ANY)
    return pl.pallas_call(
        qkv_kernel,
        grid=(B, S // RT),
        in_specs=[
            pl.BlockSpec(memory_space=pltpu.SMEM),
            row,
            pl.BlockSpec((1, 1, D), lambda b, i: (b, 0, 0)),
            pl.BlockSpec(vec.shape, lambda b, i: (0, 0)),
            pl.BlockSpec(bias.shape, lambda b, i: (0, 0)),
            anyspec,
            anyspec,
        ],
        out_specs=[row, row, row, col, col, col, row],
        out_shape=[jax.ShapeDtypeStruct((B, S, D), bf16)] * 3
        + [jax.ShapeDtypeStruct((B, D, S), bf16)] * 3
        + [jax.ShapeDtypeStruct((B, S, D), bf16)],
        scratch_shapes=[pltpu.VMEM((D, 3 * D), bf16), pltpu.SemaphoreType.DMA((2,))],
        compiler_params=params(),
        cost_estimate=pl.CostEstimate(flops=6 * B * S * D * D, bytes_accessed=30 * 10**6, transcendentals=0),
        name="norm_qkv",
    )(core, tokens, trow, vec, bias, mine, other)

def head_mask(h, rows):
    lane=lax.broadcasted_iota(jnp.int32,(rows,256),1)
    return (lane//64)==h

SAVED = True
HPAD = 16


def masked_heads(block):
    return jnp.concatenate([jnp.where(head_mask(j, block.shape[0]), block, jnp.zeros_like(block)) for j in range(4)], axis=0)


def fwd_kernel(lo_ref, hi_ref, q_ref, k_ref, vT_ref, segk_ref, segq_ref,
               mixed_ref, mixedT_ref, prob_ref, fac_ref, acc, mrow, lrow):
    b = pl.program_id(0)
    i = pl.program_id(1)
    nq = pl.num_programs(1)
    segq = segq_ref[0]
    acc[...] = jnp.zeros_like(acc)
    mrow[...] = jnp.full_like(mrow, NEG)
    lrow[...] = jnp.zeros_like(lrow)

    def body(c, carry):
        c0 = pl.multiple_of(c * KT, KT)
        segk = segk_ref[0, pl.ds(c0, KT), :]
        bias = jnp.where(jnp.concatenate([segk, segk], axis=1) == segq, 0.0, NEG)

        def scores(quad):
            cols = slice(quad * 256, (quad + 1) * 256)
            return dg(masked_heads(k_ref[0, pl.ds(c0, KT), cols]), q_ref[0, :, cols], 1, 1)

        ready = scores(0)
        for quad in range(HEADS // 4):
            s4 = ready
            if quad + 1 < HEADS // 4:
                ready = scores(quad + 1)
            for j in range(4):
                h = quad * 4 + j
                rows = slice(h * HD, (h + 1) * HD)
                s = s4[j * KT : (j + 1) * KT] + bias
                m_old = mrow[h : h + 1, :]
                m_new = jnp.maximum(m_old, jnp.max(s, axis=0, keepdims=True))
                p = jnp.exp2(s - m_new)
                alpha = jnp.exp2(m_old - m_new)
                mrow[h : h + 1, :] = m_new
                lrow[h : h + 1, :] = lrow[h : h + 1, :] * alpha + jnp.sum(p, axis=0, keepdims=True)
                pb = p.astype(bf16)
                prob_ref[0, 0, h, pl.ds(c0, KT), :] = pb
                acc[rows, :] = acc[rows, :] * alpha + dg(vT_ref[0, rows, pl.ds(c0, KT)], pb, 1, 0)
        fac_ref[0, 0, c] = mrow[...]
        return carry

    lax.fori_loop(lo_ref[b * nq + i], hi_ref[b * nq + i], body, 0)
    total = lrow[0:HEADS, :]
    inv = 1.0 / total
    lse = mrow[0:HEADS, :] + jnp.log2(total)
    for c in range(fac_ref.shape[2]):
        fac_ref[0, 0, c, 0:HEADS, :] = jnp.exp2(fac_ref[0, 0, c, 0:HEADS, :] - lse)
    for h in range(HEADS):
        rows = slice(h * HD, (h + 1) * HD)
        mixedT_ref[0, rows, :] = acc[rows, :] * inv[h : h + 1, :]
    mixed_ref[0] = mixedT_ref[0].astype(bf16).T


def attn_fwd(lo, hi, q, k, vT, segk, segq):
    B, S, D = q.shape
    nq = S // QT
    nk = S // KT
    row = pl.BlockSpec((1, QT, D), lambda b, i, *_: (b, i, 0))
    col = pl.BlockSpec((1, D, QT), lambda b, i, *_: (b, 0, i))
    sds = jax.ShapeDtypeStruct
    return pl.pallas_call(
        fwd_kernel,
        grid_spec=pltpu.PrefetchScalarGridSpec(
            num_scalar_prefetch=2,
            grid=(B, nq),
            in_specs=[
                row,
                pl.BlockSpec((1, S, D), lambda b, i, *_: (b, 0, 0)),
                pl.BlockSpec((1, D, S), lambda b, i, *_: (b, 0, 0)),
                pl.BlockSpec((1, S, 128), lambda b, i, *_: (b, 0, 0)),
                pl.BlockSpec((1, 1, QT), lambda b, i, *_: (b, 0, i)),
            ],
            out_specs=[
                row,
                col,
                pl.BlockSpec((1, 1, HEADS, S, QT), lambda b, i, *_: (b, i, 0, 0, 0)),
                pl.BlockSpec((1, 1, nk, HPAD, QT), lambda b, i, *_: (b, i, 0, 0, 0)),
            ],
            scratch_shapes=[pltpu.VMEM((D, QT), f32), pltpu.VMEM((HPAD, QT), f32), pltpu.VMEM((HPAD, QT), f32)],
        ),
        out_shape=[
            sds((B, S, D), bf16),
            sds((B, D, S), f32),
            sds((B, nq, HEADS, S, QT), bf16),
            sds((B, nq, nk, HPAD, QT), f32),
        ],
        compiler_params=params(),
        cost_estimate=pl.CostEstimate(flops=16 * B * S * S * D, bytes_accessed=80 * 10**6, transcendentals=0),
        name="attn_fwd",
    )(lo, hi, q, k, vT, segk, segq)


def bwd_kernel(lo_ref, hi_ref, qT_ref, kT_ref, v_ref, do_ref, doT_ref, oT_ref, prob_ref, fac_ref, after_ref,
               dq_ref, dk_ref, dv_ref, dqT, dkT, dvT, dlt):
    b = pl.program_id(0)
    i = pl.program_id(1)
    nq = pl.num_programs(1)

    @pl.when(i == 0)
    def _():
        dkT[...] = jnp.zeros_like(dkT)
        dvT[...] = jnp.zeros_like(dvT)

    dqT[...] = jnp.zeros_like(dqT)
    for h in range(HEADS):
        rows = slice(h * HD, (h + 1) * HD)
        dlt[h : h + 1, :] = jnp.sum(doT_ref[0, rows, :].astype(f32) * oT_ref[0, rows, :], axis=0, keepdims=True)

    def body(c, carry):
        c0 = pl.multiple_of(c * KT, KT)
        keys = pl.ds(c0, KT)

        def products(quad):
            cols = slice(quad * 256, (quad + 1) * 256)
            return dg(masked_heads(v_ref[0, keys, cols]), do_ref[0, :, cols], 1, 1)

        ready = products(0)
        for quad in range(HEADS // 4):
            dp4 = ready
            if quad + 1 < HEADS // 4:
                ready = products(quad + 1)
            for j in range(4):
                h = quad * 4 + j
                rows = slice(h * HD, (h + 1) * HD)
                factor = fac_ref[0, 0, c, h : h + 1, :]
                pb = prob_ref[0, 0, h, keys, :]
                ds = (pb.astype(f32) * ((dp4[j * KT : (j + 1) * KT] - dlt[h : h + 1, :]) * factor)).astype(bf16)
                scaled = (doT_ref[0, rows, :].astype(f32) * factor).astype(bf16)
                dvT[rows, keys] += dg(scaled, pb, 1, 1)
                dkT[rows, keys] += dg(qT_ref[0, rows, :], ds, 1, 1)
                dqT[rows, :] += dg(kT_ref[0, rows, keys], ds, 1, 0)
        return carry

    lax.fori_loop(lo_ref[b * nq + i], hi_ref[b * nq + i], body, 0)
    dq_ref[0] = dqT[...].astype(bf16).T

    @pl.when(i == nq - 1)
    def _():
        dk_ref[0] = dkT[...].astype(bf16).T
        dv_ref[0] = dvT[...].astype(bf16).T


def attn_bwd(lo, hi, qT, kT, v, do, doT, oT, prob, fac, after):
    B, S, D = v.shape
    nq = S // QT
    nk = S // KT
    row = pl.BlockSpec((1, QT, D), lambda b, i, *_: (b, i, 0))
    col = pl.BlockSpec((1, D, QT), lambda b, i, *_: (b, 0, i))
    full = pl.BlockSpec((1, S, D), lambda b, i, *_: (b, 0, 0))
    fullT = pl.BlockSpec((1, D, S), lambda b, i, *_: (b, 0, 0))
    return pl.pallas_call(
        bwd_kernel,
        grid_spec=pltpu.PrefetchScalarGridSpec(
            num_scalar_prefetch=2,
            grid=(B, nq),
            in_specs=[
                col,
                fullT,
                full,
                row,
                col,
                col,
                pl.BlockSpec((1, 1, HEADS, S, QT), lambda b, i, *_: (b, i, 0, 0, 0)),
                pl.BlockSpec((1, 1, nk, HPAD, QT), lambda b, i, *_: (b, i, 0, 0, 0)),
                pl.BlockSpec(memory_space=pl.ANY),
            ],
            out_specs=[row, full, full],
            scratch_shapes=[
                pltpu.VMEM((D, QT), f32),
                pltpu.VMEM((D, S), f32),
                pltpu.VMEM((D, S), f32),
                pltpu.VMEM((HPAD, QT), f32),
            ],
        ),
        out_shape=[jax.ShapeDtypeStruct((B, S, D), bf16)] * 3,
        compiler_params=params(),
        cost_estimate=pl.CostEstimate(flops=32 * B * S * S * D, bytes_accessed=90 * 10**6, transcendentals=0),
        name="attn_bwd",
    )(lo, hi, qT, kT, v, do, doT, oT, prob, fac, after)


def mlp_chunks(hid, cot, wup, wdown, bup_ref, acc, gh2, aup, adown, bupg_ref):
    count = wup.shape[1] // FC

    def products(j):
        cols = slice(j * FC, (j + 1) * FC)
        return dg(hid, wup[:, cols], 1, 0) + bup_ref[:, cols], dg(cot, wdown[cols, :], 1, 1)

    ready = products(0)
    for j in range(count):
        cols = slice(j * FC, (j + 1) * FC)
        up, ga = ready
        if j + 1 < count:
            ready = products(j + 1)
        active, slope = gelu_parts(up)
        active = active.astype(bf16)
        gu = (ga * slope).astype(bf16)
        acc[0] += dg(active, wdown[cols, :], 1, 0)
        adown[cols, :] += dg(active, cot, 0, 0)
        gh2[0] += dg(gu, wup[:, cols], 1, 1)
        aup[:, cols] += dg(hid, gu, 0, 0)
        bupg_ref[:, cols] += col_sum(gu.astype(f32))


def mlp_load(first, w_ref, extra, wup, wdown, sems):
    D, H = wup.shape
    at = D if first else 0
    pairs = [(w_ref.at[:, pl.ds(at, H)], wup)]
    pairs += [(w_ref.at[:, pl.ds(at + H + j * D, D)], wdown.at[pl.ds(j * D, D), :]) for j in range(H // D)]
    pairs += extra
    return [pltpu.make_async_copy(src, dst, sems.at[n]) for n, (src, dst) in enumerate(pairs)]


def mlp_store(core, wup, wdown, keep_ref, send_ref, extra, sems):
    D, H = wup.shape

    def run(up_to, down_to):
        pairs = [(wup, up_to.at[:, pl.ds(0, H)])]
        pairs += [(wdown.at[pl.ds(j * D, D), :], down_to.at[:, pl.ds(j * D, D)]) for j in range(H // D)]
        pairs += extra
        made = [pltpu.make_async_copy(src, dst, sems.at[n]) for n, (src, dst) in enumerate(pairs)]
        for c in made:
            c.start()
        for c in made:
            c.wait()

    @pl.when(core == 0)
    def _():
        run(keep_ref, send_ref)

    @pl.when(core != 0)
    def _():
        run(send_ref, keep_ref)


def mlp_first_kernel(core_ref, tok_ref, row_ref, cot_ref, mix_ref, vec_ref, bup_ref, w_ref,
                     acc_ref, gh2_ref, mid_ref, hid_ref, bupg_ref, keep_ref, send_ref,
                     wout, wup, wdown, aup, adown, acc, gh2, sems):
    i = pl.program_id(0)
    D = tok_ref.shape[2]

    @pl.when(i == 0)
    def _():
        copies = mlp_load(True, w_ref, [(w_ref.at[:, pl.ds(0, D)], wout)], wup, wdown, sems)
        for c in copies:
            c.start()
        aup[...] = jnp.zeros_like(aup)
        adown[...] = jnp.zeros_like(adown)
        bupg_ref[...] = jnp.zeros_like(bupg_ref)
        for c in copies:
            c.wait()

    base = tok_ref[0].astype(f32) + row_ref[0]
    middle = base + dg(mix_ref[0], wout[...], 1, 0) + vec_ref[0:1, :]
    mid_ref[0] = middle
    normed, unused = normalize(middle)
    hid_ref[0] = (normed * vec_ref[1:2, :] + vec_ref[2:3, :]).astype(bf16)
    acc[...] = jnp.zeros_like(acc)
    gh2[...] = jnp.zeros_like(gh2)
    mlp_chunks(hid_ref[0], cot_ref[0], wup, wdown, bup_ref, acc, gh2, aup, adown, bupg_ref)
    acc_ref[...] = acc[...].astype(bf16)
    gh2_ref[...] = gh2[...].astype(bf16)

    @pl.when(i == pl.num_programs(0) - 1)
    def _():
        wup[...] = aup[...].astype(bf16)
        wdown[...] = adown[...].astype(bf16)
        mlp_store(core_ref[0], wup, wdown, keep_ref, send_ref, [], sems)


def mlp_second_kernel(core_ref, accin_ref, gh2in_ref, mid_ref, hid_ref, cot_ref, mix_ref, vec_ref, bup_ref, wfirst_ref, w_ref,
                      out_ref, gmid_ref, gmix_ref, gmixT_ref, vecg_ref, bupg_ref, keep_ref, send_ref,
                      wout, wup, wdown, aout, aup, adown, acc, gh2, sems):
    i = pl.program_id(0)
    core = core_ref[0]
    D, H = wup.shape
    hd = D // 2

    @pl.when(i == 0)
    def _():
        copies = mlp_load(False, w_ref, [(wfirst_ref.at[:, pl.ds(0, D)], wout)], wup, wdown, sems)
        for c in copies:
            c.start()
        aout[...] = jnp.zeros_like(aout)
        aup[...] = jnp.zeros_like(aup)
        adown[...] = jnp.zeros_like(adown)
        vecg_ref[...] = jnp.zeros_like(vecg_ref)
        bupg_ref[...] = jnp.zeros_like(bupg_ref)
        for c in copies:
            c.wait()

    acc[...] = accin_ref[...].astype(f32) + mid_ref[...] + vec_ref[3:4, :]
    gh2[...] = gh2in_ref[...].astype(f32)
    cot = cot_ref[0]
    mlp_chunks(hid_ref[0], cot, wup, wdown, bup_ref, acc, gh2, aup, adown, bupg_ref)
    out_ref[0] = acc[0].astype(bf16)
    grad_hidden = gh2[0]
    normed, inv = normalize(mid_ref[0])
    cotf = cot.astype(f32)
    gmid = cotf + norm_back(grad_hidden, normed, inv, vec_ref[1:2, :])
    gmid_ref[0] = gmid
    branch = gmid.astype(bf16)
    vecg_ref[0:1, :] += col_sum(branch.astype(f32))
    vecg_ref[1:2, :] += col_sum(grad_hidden * normed)
    vecg_ref[2:3, :] += col_sum(grad_hidden)
    vecg_ref[3:4, :] += col_sum(cotf)
    aout[...] += dg(mix_ref[0], branch, 0, 0)
    gmix = dg(branch, wout[...], 1, 1).astype(bf16)
    gmix_ref[0] = gmix
    gmixT_ref[0] = gmix.T

    @pl.when(i == pl.num_programs(0) - 1)
    def _():
        wout[...] = aout[...].astype(bf16)
        wup[...] = aup[...].astype(bf16)
        wdown[...] = adown[...].astype(bf16)
        at = pl.multiple_of(core * hd, 128)
        rest = pl.multiple_of((1 - core) * hd, 128)
        extra = [
            (wout.at[:, pl.ds(at, hd)], keep_ref.at[:, pl.ds(H, hd)]),
            (wout.at[:, pl.ds(rest, hd)], send_ref.at[:, pl.ds(H, hd)]),
        ]
        mlp_store(core, wup, wdown, keep_ref, send_ref, extra, sems)


def mlp_specs(tokens, tile):
    B, S, D = tokens.shape
    per = S // tile
    row = pl.BlockSpec((1, tile, D), lambda i: (i // per, i % per, 0))
    col = pl.BlockSpec((1, D, tile), lambda i: (i // per, 0, i % per))
    one = pl.BlockSpec((1, 1, D), lambda i: (i // per, 0, 0))
    return row, col, one, pl.BlockSpec(memory_space=pl.ANY), pl.BlockSpec(memory_space=pltpu.SMEM)


def whole(shape):
    return pl.BlockSpec(shape, lambda i: (0,) * len(shape))


def mlp_first(core, tokens, trow, cot, mixed, vec, bup, weights):
    B, S, D = tokens.shape
    H = bup.shape[1]
    row, col, one, anyspec, smem = mlp_specs(tokens, MT)
    sds = jax.ShapeDtypeStruct
    return pl.pallas_call(
        mlp_first_kernel,
        grid=(B * S // MT,),
        in_specs=[smem, row, one, row, row, whole(vec.shape), whole(bup.shape), anyspec],
        out_specs=[row, row, row, row, whole((1, H)), anyspec, anyspec],
        out_shape=[sds((B, S, D), bf16)] * 2 + [sds((B, S, D), f32), sds((B, S, D), bf16), sds((1, H), f32)] + [sds((D, H), bf16)] * 2,
        scratch_shapes=[
            pltpu.VMEM((D, D), bf16),
            pltpu.VMEM((D, H), bf16),
            pltpu.VMEM((H, D), bf16),
            pltpu.VMEM((D, H), f32),
            pltpu.VMEM((H, D), f32),
            pltpu.VMEM((1, MT, D), f32),
            pltpu.VMEM((1, MT, D), f32),
            pltpu.SemaphoreType.DMA((2 + H // D,)),
        ],
        compiler_params=params(),
        cost_estimate=pl.CostEstimate(flops=13 * B * S * D * H, bytes_accessed=60 * 10**6, transcendentals=0),
        name="mlp_first",
    )(core, tokens, trow, cot, mixed, vec, bup, weights)


def mlp_second(core, acc, gh2, mid, hid, cot, mixed, vec, bup, wfirst, weights):
    B, S, D = cot.shape
    H = bup.shape[1]
    row, col, one, anyspec, smem = mlp_specs(cot, MT2)
    sds = jax.ShapeDtypeStruct
    wide = sds((D, H + D // 2), bf16)
    return pl.pallas_call(
        mlp_second_kernel,
        grid=(B * S // MT2,),
        in_specs=[smem] + [row] * 6 + [whole(vec.shape), whole(bup.shape), anyspec, anyspec],
        out_specs=[row, row, row, col, whole((4, D)), whole((1, H)), anyspec, anyspec],
        out_shape=[
            sds((B, S, D), bf16),
            sds((B, S, D), f32),
            sds((B, S, D), bf16),
            sds((B, D, S), bf16),
            sds((4, D), f32),
            sds((1, H), f32),
            wide,
            wide,
        ],
        scratch_shapes=[
            pltpu.VMEM((D, D), bf16),
            pltpu.VMEM((D, H), bf16),
            pltpu.VMEM((H, D), bf16),
            pltpu.VMEM((D, D), f32),
            pltpu.VMEM((D, H), f32),
            pltpu.VMEM((H, D), f32),
            pltpu.VMEM((1, MT2, D), f32),
            pltpu.VMEM((1, MT2, D), f32),
            pltpu.SemaphoreType.DMA((3 + H // D,)),
        ],
        compiler_params=params(),
        cost_estimate=pl.CostEstimate(flops=14 * B * S * D * H, bytes_accessed=60 * 10**6, transcendentals=0),
        name="mlp_second",
    )(core, acc, gh2, mid, hid, cot, mixed, vec, bup, wfirst, weights)


def qkv_weights_kernel(core_ref, hid_ref, dq_ref, dk_ref, dv_ref, keep_ref, send_ref, aw_ref, low_ref, sems):
    b = pl.program_id(0)
    i = pl.program_id(1)
    core = core_ref[0]
    D = hid_ref.shape[2]

    @pl.when((b == 0) & (i == 0))
    def _():
        aw_ref[...] = jnp.zeros_like(aw_ref)

    for n, g in enumerate((dq_ref[0], dk_ref[0], dv_ref[0])):
        aw_ref[:, n * D : (n + 1) * D] += dg(hid_ref[0], g, 0, 0)

    @pl.when((b == pl.num_programs(0) - 1) & (i == pl.num_programs(1) - 1))
    def _():
        low_ref[...] = aw_ref[...].astype(bf16)
        half = keep_ref.shape[1]
        at = pl.multiple_of(core * half, 128)
        rest = pl.multiple_of((1 - core) * half, 128)
        copies = (
            pltpu.make_async_copy(low_ref.at[:, pl.ds(at, half)], keep_ref, sems.at[0]),
            pltpu.make_async_copy(low_ref.at[:, pl.ds(rest, half)], send_ref, sems.at[1]),
        )
        for c in copies:
            c.start()
        for c in copies:
            c.wait()


def qkv_weights_call(core, hid, dq, dk, dv):
    B, S, D = hid.shape
    row = pl.BlockSpec((1, S, D), lambda b, i: (b, i, 0))
    anyspec = pl.BlockSpec(memory_space=pl.ANY)
    half = jax.ShapeDtypeStruct((D, 3 * D // 2), bf16)
    return pl.pallas_call(
        qkv_weights_kernel,
        grid=(B, 1),
        in_specs=[pl.BlockSpec(memory_space=pltpu.SMEM), row, row, row, row],
        out_specs=[anyspec, anyspec],
        out_shape=[half, half],
        scratch_shapes=[pltpu.VMEM((D, 3 * D), f32), pltpu.VMEM((D, 3 * D), bf16), pltpu.SemaphoreType.DMA((2,))],
        compiler_params=params(),
        cost_estimate=pl.CostEstimate(flops=6 * B * S * D * D, bytes_accessed=20 * 10**6, transcendentals=0),
        name="qkv_weights",
    )(core, hid, dq, dk, dv)


def qkv_back_kernel(core_ref, tok_ref, row_ref, gmid_ref, dq_ref, dk_ref, dv_ref, vec_ref, mine_ref, other_ref, after_ref,
                    gin_ref, rsum_ref, vecg_ref, w_ref, sems):
    b = pl.program_id(0)
    i = pl.program_id(1)

    @pl.when((b == 0) & (i == 0))
    def _():
        copies = place_halves(mine_ref, other_ref, w_ref, core_ref[0], sems)
        for c in copies:
            c.start()
        vecg_ref[...] = jnp.zeros_like(vecg_ref)
        for c in copies:
            c.wait()

    @pl.when(i == 0)
    def _():
        rsum_ref[...] = jnp.zeros_like(rsum_ref)

    grads = (dq_ref[0], dk_ref[0], dv_ref[0])
    grad_hidden = dg(jnp.concatenate(grads, axis=1), w_ref[...], 1, 1)
    base = tok_ref[0].astype(f32) + row_ref[0]
    normed, inv = normalize(base)
    gbase = gmid_ref[0] + norm_back(grad_hidden, normed, inv, vec_ref[0:1, :])
    gin_ref[0] = gbase.astype(bf16)
    rsum_ref[0] += col_sum(gbase)
    vecg_ref[0:1, :] += col_sum(grad_hidden * normed)
    vecg_ref[1:2, :] += col_sum(grad_hidden)
    vecg_ref[2:3, :] += col_sum(grads[0].astype(f32))
    vecg_ref[3:4, :] += col_sum(grads[2].astype(f32))


def qkv_back_call(core, tokens, trow, gmid, dq, dk, dv, vec, mine, other, after):
    B, S, D = tokens.shape
    row = pl.BlockSpec((1, RT, D), lambda b, i: (b, i, 0))
    seq = pl.BlockSpec((1, 1, D), lambda b, i: (b, 0, 0))
    anyspec = pl.BlockSpec(memory_space=pl.ANY)
    sds = jax.ShapeDtypeStruct
    return pl.pallas_call(
        qkv_back_kernel,
        grid=(B, S // RT),
        in_specs=[
            pl.BlockSpec(memory_space=pltpu.SMEM),
            row,
            seq,
            row,
            row,
            row,
            row,
            pl.BlockSpec(vec.shape, lambda b, i: (0, 0)),
            anyspec,
            anyspec,
            anyspec,
        ],
        out_specs=[row, seq, pl.BlockSpec((4, D), lambda b, i: (0, 0))],
        out_shape=[sds((B, S, D), bf16), sds((B, 1, D), f32), sds((4, D), f32)],
        scratch_shapes=[pltpu.VMEM((D, 3 * D), bf16), pltpu.SemaphoreType.DMA((2,))],
        compiler_params=params(),
        cost_estimate=pl.CostEstimate(flops=6 * B * S * D * D, bytes_accessed=40 * 10**6, transcendentals=0),
        name="norm_qkv_back",
    )(core, tokens, trow, gmid, dq, dk, dv, vec, mine, other, after)


def key_ranges(segment_ids):
    B, S = segment_ids.shape
    tiles = segment_ids.reshape(B, S // QT, QT)
    before = jnp.sum((segment_ids[:, None, :] < tiles[:, :, :1]).astype(jnp.int32), axis=-1)
    upto = jnp.sum((segment_ids[:, None, :] <= tiles[:, :, -1:]).astype(jnp.int32), axis=-1)
    return (before // KT).reshape(-1), ((upto + KT - 1) // KT).reshape(-1)


def own_slice(array, index, size, axis):
    return lax.dynamic_slice_in_dim(array, index * size, size, axis)


def swap(array, axis):
    return lax.ppermute(array, axis, [(0, 1), (1, 0)])


def all_sum(array, axis):
    size = lax.axis_size(axis)
    step = 1
    while step < size:
        came = lax.ppermute(array, axis, [(i, i ^ step) for i in range(size)])
        array = (array.astype(f32) + came.astype(f32)).astype(array.dtype)
        step *= 2
    return array


def gather_small(array, axis):
    size, me = lax.axis_size(axis), lax.axis_index(axis)
    step = 1
    while step < size:
        came = lax.ppermute(array, axis, [(i, i ^ step) for i in range(size)])
        low = (me & step) == 0
        array = jnp.concatenate([jnp.where(low, array, came), jnp.where(low, came, array)], axis=0)
        step *= 2
    return array


def scatter_small(array, axis):
    size, me = lax.axis_size(axis), lax.axis_index(axis)
    step = size // 2
    while step >= 1:
        half = array.shape[0] // 2
        low = (me & step) == 0
        keep = jnp.where(low, array[:half], array[half:])
        send = jnp.where(low, array[half:], array[:half])
        array = keep + lax.ppermute(send, axis, [(i, i ^ step) for i in range(size)])
        step //= 2
    return array


EXTRA = 8


def split_rows(values, width):
    high = lax.reduce_precision(values, 8, 7)
    parts = jnp.concatenate([high, values - high], axis=-2).astype(bf16)
    pad = [(0, 0)] * (parts.ndim - 1) + [(0, width - parts.shape[-1])]
    return jnp.pad(parts, pad)


def exchange_reduce(array, extra, axis):
    size = lax.axis_size(axis)
    rows, width = array.shape[0] // size, array.shape[1]
    extra = jnp.pad(extra, ((0, 0), (0, EXTRA - extra.shape[1]), (0, 0)))
    sent = jnp.concatenate([array.reshape(size, rows, width), extra], axis=1)
    came = lax.all_to_all(sent.reshape(size * (rows + EXTRA), width), axis, 0, 0, tiled=True)
    came = came.reshape(size, rows + EXTRA, width)
    return jnp.sum(came[:, :rows].astype(f32), axis=0).astype(bf16), came[:, rows:].astype(f32)


def direct_exchange(array, axis):
    size, me = lax.axis_size(axis), lax.axis_index(axis)
    came = [own_slice(array, me, 1, 0)]
    for r in range(1, size):
        came.append(lax.ppermute(own_slice(array, me ^ r, 1, 0), axis, [(i, i ^ r) for i in range(size)]))
    return jnp.concatenate(came, axis=0)


def on_device(
    tokens,
    cot,
    segment_ids,
    block_map,
    timesteps,
    step_table,
    ln1_gain,
    ln1_bias,
    w_query,
    b_query,
    w_key,
    w_value,
    b_value,
    w_out,
    b_out,
    ln2_gain,
    ln2_bias,
    w_up,
    b_up,
    w_down,
    b_down,
):
    B, S, D = tokens.shape
    n = lax.axis_size("shard")
    me = lax.axis_index("shard")
    core = lax.axis_index("core")
    own = ln1_gain.shape[0]
    FF = b_up.shape[0] * n
    hd = D // 2
    core1 = core.reshape(1).astype(jnp.int32)

    H = FF // 2
    J = FF // D
    thin = own // 2
    qkv_local = own_slice(jnp.concatenate([w_query, w_key, w_value], axis=1), core, 3 * hd, 1)
    qkv_mine = lax.all_gather(qkv_local, "shard", axis=0, tiled=True)
    up_core = own_slice(w_up, core, thin, 0).reshape(thin, n, 2, J, thin)
    up_core = up_core.transpose(0, 3, 1, 2, 4).reshape(thin, FF)
    out_core = own_slice(w_out, core, thin, 0)
    down_core = own_slice(w_down, core, J * thin, 0)
    down_core = [down_core[j * thin : (j + 1) * thin] for j in range(J)]
    local_a = jnp.concatenate([out_core, up_core[:, :H]] + down_core[: J // 2], axis=1)
    local_b = jnp.concatenate([up_core[:, H:]] + down_core[J // 2 :], axis=1)

    small = (ln1_gain, ln1_bias, b_query, b_value, b_out, ln2_gain, ln2_bias, b_down, b_up)
    small = jnp.concatenate([v.astype(f32) for v in small] + [timesteps.astype(f32)])
    packed = gather_small(small[None], "shard")
    g1, s1, bq, bv, bo, g2, s2, bd = [packed[:, i * own : (i + 1) * own].reshape(1, D) for i in range(8)]
    width = 8 * own + FF // n
    bup = packed[:, 8 * own : width].reshape(n, 2, J, thin).transpose(2, 0, 1, 3).reshape(1, FF)
    group = packed[:, width:].reshape(n * B, 1).astype(jnp.int32)
    vec1 = jnp.concatenate([g1, s1], axis=0)
    bias = jnp.concatenate([bq, jnp.zeros_like(bq), bv], axis=1)
    vec2 = jnp.concatenate([bo, g2, s2, bd], axis=0)

    own_rows = step_table.shape[0]
    spots = me * own_rows + lax.broadcasted_iota(jnp.int32, (1, own_rows), 1)
    found = jnp.dot((group == spots).astype(bf16), step_table, preferred_element_type=f32)
    trow = scatter_small(found, "shard").reshape(B, 1, D)
    qkv_mine, trow, vec1 = lax.optimization_barrier((qkv_mine, trow, vec1))
    qkv_other = swap(qkv_mine, "core")
    local_a, qkv_mine = lax.optimization_barrier((local_a, qkv_mine))
    w_a = lax.all_gather(local_a, ("shard", "core"), axis=0, tiled=True)

    lo, hi = key_ranges(segment_ids)
    segk = jnp.broadcast_to(segment_ids[:, :, None], (B, S, 128))
    segq = segment_ids[:, None, :]

    q, k, v, qT, kT, vT, hid1 = qkv_call(core1, tokens, trow, vec1, bias, qkv_mine, qkv_other)
    mixed, mixedT, prob, fac = attn_fwd(lo, hi, q, k, vT, segk, segq)
    local_b, w_a, mixed = lax.optimization_barrier((local_b, w_a, mixed))
    w_b = lax.all_gather(local_b, ("shard", "core"), axis=0, tiled=True)
    def core_sum(keep, send):
        return (keep.astype(f32) + swap(send, "core").astype(f32)).astype(bf16)

    def two(half, other):
        half, other = half.astype(f32), other.astype(f32)
        return jnp.where(core == 0, half, other), jnp.where(core == 0, other, half)

    def finish(part):
        half = all_sum(part, "xrep")
        return two(half, swap(half, "core"))

    acc, gh2, mid, hid, bupg_a, keep, send = mlp_first(core1, tokens, trow, cot, mixed, vec2, bup[:, :H], w_a)
    half_a = core_sum(keep, send)
    part_a = lax.all_to_all(half_a, "shard", 0, 0, tiled=True).reshape(n, own, H)
    part_a = jnp.sum(part_a.astype(f32), axis=0).astype(bf16)
    acc, half_a = lax.optimization_barrier((acc, half_a))
    out, gmid, gmix, gmixT, vecg2, bupg_b, keep, send = mlp_second(
        core1, acc, gh2, mid, hid, cot, mixed, vec2, bup[:, H:], w_a, w_b
    )
    half_b = core_sum(keep, send)
    half_b, part_a = lax.optimization_barrier((half_b, part_a))
    bupg = jnp.concatenate([bupg_a, bupg_b], axis=1)
    bupg = bupg.reshape(J, n, 2, thin).transpose(1, 2, 0, 3).reshape(n, FF // n)
    vectors = jnp.concatenate([vecg2[i].reshape(n, own) for i in range(4)] + [bupg], axis=1)
    part_b, came_b = exchange_reduce(half_b, split_rows(vectors[:, None], half_b.shape[1]), "shard")
    dq, dk, dv = attn_bwd(lo, hi, qT, kT, v, gmix, gmixT, mixedT, prob, fac, half_b)
    part_a = all_sum(part_a, "xrep")
    dq, part_a = lax.optimization_barrier((dq, part_a))
    other_a = swap(part_a, "core")
    keep, send = qkv_weights_call(core1, hid1, dq, dk, dv)
    keep, other_a = lax.optimization_barrier((keep, other_a))
    qkv_half = core_sum(keep, send)
    qkv_half, part_b, came_b = lax.optimization_barrier((qkv_half, part_b, came_b))
    came = lax.all_to_all(qkv_half, "shard", 0, 0, tiled=True).reshape(n, own, 3 * hd)
    qkv_part = jnp.sum(came.astype(f32), axis=0).astype(bf16)
    gin, rsum, vecg1 = qkv_back_call(
        core1, tokens, trow, gmid, dq, dk, dv, vec1, qkv_mine, qkv_other, qkv_half
    )
    part_b, part_a, other_a, vecg1 = lax.optimization_barrier((part_b, part_a, other_a, vecg1))
    vectors = jnp.concatenate([vecg1[i].reshape(n, own) for i in range(4)], axis=1)
    thick = -(-(D + 2) // 128) * 128
    digits = jnp.stack([timesteps // 32, timesteps % 32], axis=1).astype(f32)
    table_rows = jnp.concatenate([rsum.reshape(B, D), digits], axis=1)
    table_rows = jnp.broadcast_to(jnp.pad(table_rows, ((0, 0), (0, thick - D - 2)))[None], (n, B, thick))
    vectors = jnp.pad(vectors, ((0, 0), (0, thick - 4 * own)))[:, None]
    came_q = direct_exchange(jnp.concatenate([table_rows, vectors], axis=1), "shard")
    came_q, qkv_part = lax.optimization_barrier((came_q, qkv_part))

    vg_b = jnp.sum(came_b[:, :2], axis=(0, 1))[: 4 * own + FF // n]
    vg_q = jnp.sum(came_q[:, B], axis=0)[: 4 * own]
    vg = jnp.concatenate([vg_q, vg_b])
    lines = -(-vg.shape[0] // thick)
    vg = jnp.pad(vg, (0, lines * thick - vg.shape[0])).reshape(lines, thick)
    sums = jnp.concatenate([came_q[:, :B].reshape(n * B, thick), vg], axis=0)[None]
    for axis in ("core", "xrep"):
        sums = gather_small(sums, axis)
    vg = jnp.sum(sums[:, n * B :], axis=0).reshape(-1)
    sums = sums[:, : n * B].reshape(-1, thick)
    g_bup = vg[8 * own : 8 * own + FF // n]
    vg = [vg[i * own : (i + 1) * own] for i in range(8)]
    own_rows = step_table.shape[0]
    rows = me * own_rows + lax.broadcasted_iota(jnp.int32, (own_rows, 1), 0)
    steps = 32 * sums[:, D] + sums[:, D + 1]
    match = (rows == steps.astype(jnp.int32)[None, :]).astype(f32)
    g_table = jnp.dot(match, sums[:, :D], precision=lax.Precision.HIGHEST, preferred_element_type=f32)

    a_up, a_down = two(part_a, other_a)
    b_up_, b_down_ = finish(part_b)
    g_up = jnp.concatenate([a_up, b_up_[:, :H]], axis=1)
    g_up = g_up.reshape(own, J, n, 2, thin).transpose(0, 2, 3, 1, 4).reshape(own, FF)
    blocks = jnp.concatenate([a_down, b_down_[:, :H]], axis=1).reshape(2, thin, J, D)
    g_down = blocks.transpose(0, 2, 1, 3).reshape(FF // n, D)
    g_out = jnp.concatenate([b_up_[:, H:], b_down_[:, H:]], axis=1)
    q_left, q_right = finish(qkv_part)
    g_qkv = jnp.concatenate([q_left, q_right], axis=1)
    g_q, g_k, g_v = g_qkv[:, :D], g_qkv[:, D : 2 * D], g_qkv[:, 2 * D :]
    return (
        out, gin, g_table, vg[0], vg[1], g_q, vg[2], g_k, g_v, vg[3], g_out, vg[4], vg[5], vg[6], g_up, g_bup, g_down, vg[7],
    )


def solution(mesh):
    rep, shard = mesh.shape["rep"], mesh.shape["shard"]
    fine = Mesh(mesh.devices.reshape(rep // 2, 2, shard), ("xrep", "core", "shard"))
    seqs = ("xrep", "core", "shard")
    mat, vec = P("shard", None), P("shard")
    rows3, rows2 = P(seqs, None, None), P(seqs, None)
    weights = (mat, vec, vec, mat, vec, mat, mat, vec, mat, vec, vec, vec, mat, vec, mat, vec)
    return jax.shard_map(
        on_device,
        mesh=fine,
        in_specs=(rows3, rows3, rows2, rows3, P(seqs)) + weights,
        out_specs=(rows3, rows3) + weights,
        check_vma=False,
    )
```

```python
import functools

import jax
import jax.numpy as jnp
from jax import lax
from jax.experimental import pallas as pl
from jax.experimental.pallas import tpu as pltpu
from jax.sharding import Mesh, PartitionSpec as P

HEADS = 12
HD = 64
QT = 256
KT = 256
RT = 512
MT = 512
MT2 = 512
FC = 768
EPS = 1e-05
NEG = -1e30
LOG2E = 1.4426950408889634
f32 = jnp.float32
bf16 = jnp.bfloat16
VMEM_BYTES = 60 * 1000 * 1024


def dg(x, y, cx, cy):
    return lax.dot_general(x, y, (((cx,), (cy,)), ((), ())), preferred_element_type=f32)


def normalize(values):
    center = values - jnp.mean(values, axis=-1, keepdims=True)
    inv_dev = lax.rsqrt(jnp.mean(center * center, axis=-1, keepdims=True) + EPS)
    return center * inv_dev, inv_dev


def norm_back(grad_hidden, normed, inv_dev, gain_row):
    grad_normed = grad_hidden * gain_row
    return inv_dev * (
        grad_normed
        - jnp.mean(grad_normed, axis=-1, keepdims=True)
        - normed * jnp.mean(grad_normed * normed, axis=-1, keepdims=True)
    )


def col_sum(values):
    return jnp.sum(values, axis=0, keepdims=True)


def gelu_parts(x):
    density = jnp.exp(-0.5 * x * x)
    t = 1.0 / (1.0 + 0.2316418882 * jnp.abs(x))
    poly = t * (0.127414796 + t * (-0.142248368 + t * (0.7107068705 + t * (-0.7265760135 + t * 0.5307027145))))
    tail = density * poly
    cdf = jnp.where(x >= 0.0, 1.0 - tail, tail)
    return x * cdf, cdf + x * (density * 0.3989422804014327)


def place_halves(mine, other, full, core, sems):
    half = mine.shape[1]
    at = pl.multiple_of(core * half, 128)
    rest = pl.multiple_of((1 - core) * half, 128)
    return (
        pltpu.make_async_copy(mine, full.at[:, pl.ds(at, half)], sems.at[0]),
        pltpu.make_async_copy(other, full.at[:, pl.ds(rest, half)], sems.at[1]),
    )


def params(**kw):
    return pltpu.CompilerParams(vmem_limit_bytes=VMEM_BYTES, **kw)


def qkv_kernel(core_ref, tok_ref, row_ref, vec_ref, bias_ref, mine_ref, other_ref,
               q_ref, k_ref, v_ref, qT_ref, kT_ref, vT_ref, hid_ref, w_ref, sems):
    @pl.when((pl.program_id(0) == 0) & (pl.program_id(1) == 0))
    def _():
        copies = place_halves(mine_ref, other_ref, w_ref, core_ref[0], sems)
        for c in copies:
            c.start()
        for c in copies:
            c.wait()

    width = tok_ref.shape[2]
    base = tok_ref[0].astype(f32) + row_ref[0]
    normed, unused = normalize(base)
    hidden = (normed * vec_ref[0:1, :] + vec_ref[1:2, :]).astype(bf16)
    hid_ref[0] = hidden
    scale = HD ** (-0.5)
    for n, (out, outT) in enumerate(((q_ref, qT_ref), (k_ref, kT_ref), (v_ref, vT_ref))):
        cols = slice(n * width, (n + 1) * width)
        exact = dg(hidden, w_ref[:, cols], 1, 0) + bias_ref[:, cols]
        rows = exact.astype(bf16)
        scaled = (rows.astype(f32) * scale).astype(bf16)
        out[0] = (exact * (scale * LOG2E)).astype(bf16) if n == 0 else rows
        outT[0] = (rows if n == 2 else scaled).T


def qkv_call(core, tokens, trow, vec, bias, mine, other):
    B, S, D = tokens.shape
    row = pl.BlockSpec((1, RT, D), lambda b, i: (b, i, 0))
    col = pl.BlockSpec((1, D, RT), lambda b, i: (b, 0, i))
    anyspec = pl.BlockSpec(memory_space=pl.ANY)
    return pl.pallas_call(
        qkv_kernel,
        grid=(B, S // RT),
        in_specs=[
            pl.BlockSpec(memory_space=pltpu.SMEM),
            row,
            pl.BlockSpec((1, 1, D), lambda b, i: (b, 0, 0)),
            pl.BlockSpec(vec.shape, lambda b, i: (0, 0)),
            pl.BlockSpec(bias.shape, lambda b, i: (0, 0)),
            anyspec,
            anyspec,
        ],
        out_specs=[row, row, row, col, col, col, row],
        out_shape=[jax.ShapeDtypeStruct((B, S, D), bf16)] * 3
        + [jax.ShapeDtypeStruct((B, D, S), bf16)] * 3
        + [jax.ShapeDtypeStruct((B, S, D), bf16)],
        scratch_shapes=[pltpu.VMEM((D, 3 * D), bf16), pltpu.SemaphoreType.DMA((2,))],
        compiler_params=params(),
        cost_estimate=pl.CostEstimate(flops=6 * B * S * D * D, bytes_accessed=30 * 10**6, transcendentals=0),
        name="norm_qkv",
    )(core, tokens, trow, vec, bias, mine, other)

def head_mask(h, rows):
    lane=lax.broadcasted_iota(jnp.int32,(rows,256),1)
    return (lane//64)==h

SAVED = True
HPAD = 16
HROWS = HD + 16


def masked_heads(block):
    return jnp.concatenate([jnp.where(head_mask(j, block.shape[0]), block, jnp.zeros_like(block)) for j in range(4)], axis=0)


def fwd_kernel(lo_ref, hi_ref, q_ref, k_ref, vT_ref, segk_ref, segq_ref,
               mixed_ref, mixedT_ref, prob_ref, fac_ref, acc, mrow):
    b = pl.program_id(0)
    i = pl.program_id(1)
    nq = pl.num_programs(1)
    segq = segq_ref[0]
    acc[...] = jnp.zeros_like(acc)
    mrow[...] = jnp.full_like(mrow, NEG)
    ones = jnp.ones((HROWS - HD, KT), bf16)

    def body(c, carry):
        c0 = pl.multiple_of(c * KT, KT)
        segk = segk_ref[0, pl.ds(c0, KT), :]
        bias = jnp.where(jnp.concatenate([segk, segk], axis=1) == segq, 0.0, NEG)

        def scores(quad):
            cols = slice(quad * 256, (quad + 1) * 256)
            return dg(masked_heads(k_ref[0, pl.ds(c0, KT), cols]), q_ref[0, :, cols], 1, 1)

        ready = scores(0)
        for quad in range(HEADS // 4):
            s4 = ready
            if quad + 1 < HEADS // 4:
                ready = scores(quad + 1)
            for j in range(4):
                h = quad * 4 + j
                rows = slice(h * HD, (h + 1) * HD)
                s = s4[j * KT : (j + 1) * KT] + bias
                m_old = mrow[h : h + 1, :]
                m_new = jnp.maximum(m_old, jnp.max(s, axis=0, keepdims=True))
                p = jnp.exp2(s - m_new)
                alpha = jnp.exp2(m_old - m_new)
                mrow[h : h + 1, :] = m_new
                pb = p.astype(bf16)
                prob_ref[0, 0, h, pl.ds(c0, KT), :] = pb
                values = jnp.concatenate([vT_ref[0, rows, pl.ds(c0, KT)], ones], axis=0)
                held = slice(h * HROWS, h * HROWS + HD + 8)
                acc[held, :] = acc[held, :] * alpha + dg(values, pb, 1, 0)[: HD + 8]
        fac_ref[0, 0, c] = mrow[...]
        return carry

    lax.fori_loop(lo_ref[b * nq + i], hi_ref[b * nq + i], body, 0)
    total = jnp.concatenate([acc[h * HROWS + HD : h * HROWS + HD + 1, :] for h in range(HEADS)], axis=0)
    inv = 1.0 / total
    lse = mrow[0:HEADS, :] + jnp.log2(total)
    for c in range(fac_ref.shape[2]):
        fac_ref[0, 0, c, 0:HEADS, :] = jnp.exp2(fac_ref[0, 0, c, 0:HEADS, :] - lse)
    for h in range(HEADS):
        rows = slice(h * HD, (h + 1) * HD)
        mixedT_ref[0, rows, :] = acc[h * HROWS : h * HROWS + HD, :] * inv[h : h + 1, :]
    mixed_ref[0] = mixedT_ref[0].astype(bf16).T


def attn_fwd(lo, hi, q, k, vT, segk, segq):
    B, S, D = q.shape
    nq = S // QT
    nk = S // KT
    row = pl.BlockSpec((1, QT, D), lambda b, i, *_: (b, i, 0))
    col = pl.BlockSpec((1, D, QT), lambda b, i, *_: (b, 0, i))
    sds = jax.ShapeDtypeStruct
    return pl.pallas_call(
        fwd_kernel,
        grid_spec=pltpu.PrefetchScalarGridSpec(
            num_scalar_prefetch=2,
            grid=(B, nq),
            in_specs=[
                row,
                pl.BlockSpec((1, S, D), lambda b, i, *_: (b, 0, 0)),
                pl.BlockSpec((1, D, S), lambda b, i, *_: (b, 0, 0)),
                pl.BlockSpec((1, S, 128), lambda b, i, *_: (b, 0, 0)),
                pl.BlockSpec((1, 1, QT), lambda b, i, *_: (b, 0, i)),
            ],
            out_specs=[
                row,
                col,
                pl.BlockSpec((1, 1, HEADS, S, QT), lambda b, i, *_: (b, i, 0, 0, 0)),
                pl.BlockSpec((1, 1, nk, HPAD, QT), lambda b, i, *_: (b, i, 0, 0, 0)),
            ],
            scratch_shapes=[pltpu.VMEM((HEADS * HROWS, QT), f32), pltpu.VMEM((HPAD, QT), f32)],
        ),
        out_shape=[
            sds((B, S, D), bf16),
            sds((B, D, S), f32),
            sds((B, nq, HEADS, S, QT), bf16),
            sds((B, nq, nk, HPAD, QT), f32),
        ],
        compiler_params=params(),
        cost_estimate=pl.CostEstimate(flops=16 * B * S * S * D, bytes_accessed=80 * 10**6, transcendentals=0),
        name="attn_fwd",
    )(lo, hi, q, k, vT, segk, segq)


def bwd_kernel(lo_ref, hi_ref, qT_ref, kT_ref, v_ref, do_ref, doT_ref, oT_ref, prob_ref, fac_ref, after_ref,
               dq_ref, dk_ref, dv_ref, dqT, dkT, dvT, dlt):
    b = pl.program_id(0)
    i = pl.program_id(1)
    nq = pl.num_programs(1)

    @pl.when(i == 0)
    def _():
        dkT[...] = jnp.zeros_like(dkT)
        dvT[...] = jnp.zeros_like(dvT)

    dqT[...] = jnp.zeros_like(dqT)
    for h in range(HEADS):
        rows = slice(h * HD, (h + 1) * HD)
        dlt[h : h + 1, :] = jnp.sum(doT_ref[0, rows, :].astype(f32) * oT_ref[0, rows, :], axis=0, keepdims=True)

    def body(c, carry):
        c0 = pl.multiple_of(c * KT, KT)
        keys = pl.ds(c0, KT)

        def products(quad):
            cols = slice(quad * 256, (quad + 1) * 256)
            return dg(masked_heads(v_ref[0, keys, cols]), do_ref[0, :, cols], 1, 1)

        ready = products(0)
        for quad in range(HEADS // 4):
            dp4 = ready
            if quad + 1 < HEADS // 4:
                ready = products(quad + 1)
            for j in range(4):
                h = quad * 4 + j
                rows = slice(h * HD, (h + 1) * HD)
                factor = fac_ref[0, 0, c, h : h + 1, :]
                pb = prob_ref[0, 0, h, keys, :]
                ds = (pb.astype(f32) * ((dp4[j * KT : (j + 1) * KT] - dlt[h : h + 1, :]) * factor)).astype(bf16)
                scaled = (doT_ref[0, rows, :].astype(f32) * factor).astype(bf16)
                dvT[rows, keys] += dg(scaled, pb, 1, 1)
                dkT[rows, keys] += dg(qT_ref[0, rows, :], ds, 1, 1)
                dqT[rows, :] += dg(kT_ref[0, rows, keys], ds, 1, 0)
        return carry

    lax.fori_loop(lo_ref[b * nq + i], hi_ref[b * nq + i], body, 0)
    dq_ref[0] = dqT[...].astype(bf16).T

    @pl.when(i == nq - 1)
    def _():
        dk_ref[0] = dkT[...].astype(bf16).T
        dv_ref[0] = dvT[...].astype(bf16).T


def attn_bwd(lo, hi, qT, kT, v, do, doT, oT, prob, fac, after):
    B, S, D = v.shape
    nq = S // QT
    nk = S // KT
    row = pl.BlockSpec((1, QT, D), lambda b, i, *_: (b, i, 0))
    col = pl.BlockSpec((1, D, QT), lambda b, i, *_: (b, 0, i))
    full = pl.BlockSpec((1, S, D), lambda b, i, *_: (b, 0, 0))
    fullT = pl.BlockSpec((1, D, S), lambda b, i, *_: (b, 0, 0))
    return pl.pallas_call(
        bwd_kernel,
        grid_spec=pltpu.PrefetchScalarGridSpec(
            num_scalar_prefetch=2,
            grid=(B, nq),
            in_specs=[
                col,
                fullT,
                full,
                row,
                col,
                col,
                pl.BlockSpec((1, 1, HEADS, S, QT), lambda b, i, *_: (b, i, 0, 0, 0)),
                pl.BlockSpec((1, 1, nk, HPAD, QT), lambda b, i, *_: (b, i, 0, 0, 0)),
                pl.BlockSpec(memory_space=pl.ANY),
            ],
            out_specs=[row, full, full],
            scratch_shapes=[
                pltpu.VMEM((D, QT), f32),
                pltpu.VMEM((D, S), f32),
                pltpu.VMEM((D, S), f32),
                pltpu.VMEM((HPAD, QT), f32),
            ],
        ),
        out_shape=[jax.ShapeDtypeStruct((B, S, D), bf16)] * 3,
        compiler_params=params(),
        cost_estimate=pl.CostEstimate(flops=32 * B * S * S * D, bytes_accessed=90 * 10**6, transcendentals=0),
        name="attn_bwd",
    )(lo, hi, qT, kT, v, do, doT, oT, prob, fac, after)


def mlp_chunks(hid, cot, wup, wdown, bup_ref, acc, gh2, aup, adown, bupg_ref):
    count = wup.shape[1] // FC

    def products(j):
        cols = slice(j * FC, (j + 1) * FC)
        return dg(hid, wup[:, cols], 1, 0) + bup_ref[:, cols], dg(cot, wdown[cols, :], 1, 1)

    ready = products(0)
    for j in range(count):
        cols = slice(j * FC, (j + 1) * FC)
        up, ga = ready
        if j + 1 < count:
            ready = products(j + 1)
        active, slope = gelu_parts(up)
        active = active.astype(bf16)
        gu = (ga * slope).astype(bf16)
        acc[0] += dg(active, wdown[cols, :], 1, 0)
        adown[cols, :] += dg(active, cot, 0, 0)
        gh2[0] += dg(gu, wup[:, cols], 1, 1)
        aup[:, cols] += dg(hid, gu, 0, 0)
        bupg_ref[:, cols] += col_sum(gu.astype(f32))


def mlp_load(first, w_ref, extra, wup, wdown, sems):
    D, H = wup.shape
    at = D if first else 0
    pairs = [(w_ref.at[:, pl.ds(at, H)], wup)]
    pairs += [(w_ref.at[:, pl.ds(at + H + j * D, D)], wdown.at[pl.ds(j * D, D), :]) for j in range(H // D)]
    pairs += extra
    return [pltpu.make_async_copy(src, dst, sems.at[n]) for n, (src, dst) in enumerate(pairs)]


def mlp_store(core, wup, wdown, keep_ref, send_ref, extra, sems):
    D, H = wup.shape

    def run(up_to, down_to):
        pairs = [(wup, up_to.at[:, pl.ds(0, H)])]
        pairs += [(wdown.at[pl.ds(j * D, D), :], down_to.at[:, pl.ds(j * D, D)]) for j in range(H // D)]
        pairs += extra
        made = [pltpu.make_async_copy(src, dst, sems.at[n]) for n, (src, dst) in enumerate(pairs)]
        for c in made:
            c.start()
        for c in made:
            c.wait()

    @pl.when(core == 0)
    def _():
        run(keep_ref, send_ref)

    @pl.when(core != 0)
    def _():
        run(send_ref, keep_ref)


def mlp_first_kernel(core_ref, tok_ref, row_ref, cot_ref, mix_ref, vec_ref, bup_ref, w_ref,
                     acc_ref, gh2_ref, mid_ref, hid_ref, bupg_ref, keep_ref, send_ref,
                     wout, wup, wdown, aup, adown, acc, gh2, sems):
    i = pl.program_id(0)
    D = tok_ref.shape[2]

    @pl.when(i == 0)
    def _():
        copies = mlp_load(True, w_ref, [(w_ref.at[:, pl.ds(0, D)], wout)], wup, wdown, sems)
        for c in copies:
            c.start()
        aup[...] = jnp.zeros_like(aup)
        adown[...] = jnp.zeros_like(adown)
        bupg_ref[...] = jnp.zeros_like(bupg_ref)
        for c in copies:
            c.wait()

    base = tok_ref[0].astype(f32) + row_ref[0]
    middle = base + dg(mix_ref[0], wout[...], 1, 0) + vec_ref[0:1, :]
    mid_ref[0] = middle
    normed, unused = normalize(middle)
    hid_ref[0] = (normed * vec_ref[1:2, :] + vec_ref[2:3, :]).astype(bf16)
    acc[...] = jnp.zeros_like(acc)
    gh2[...] = jnp.zeros_like(gh2)
    mlp_chunks(hid_ref[0], cot_ref[0], wup, wdown, bup_ref, acc, gh2, aup, adown, bupg_ref)
    acc_ref[...] = acc[...].astype(bf16)
    gh2_ref[...] = gh2[...].astype(bf16)

    @pl.when(i == pl.num_programs(0) - 1)
    def _():
        wup[...] = aup[...].astype(bf16)
        wdown[...] = adown[...].astype(bf16)
        mlp_store(core_ref[0], wup, wdown, keep_ref, send_ref, [], sems)


def mlp_second_kernel(core_ref, accin_ref, gh2in_ref, mid_ref, hid_ref, cot_ref, mix_ref, vec_ref, bup_ref, wfirst_ref, w_ref,
                      out_ref, gmid_ref, gmix_ref, gmixT_ref, vecg_ref, bupg_ref, keep_ref, send_ref,
                      wout, wup, wdown, aout, aup, adown, acc, gh2, sems):
    i = pl.program_id(0)
    core = core_ref[0]
    D, H = wup.shape
    hd = D // 2

    @pl.when(i == 0)
    def _():
        copies = mlp_load(False, w_ref, [(wfirst_ref.at[:, pl.ds(0, D)], wout)], wup, wdown, sems)
        for c in copies:
            c.start()
        aout[...] = jnp.zeros_like(aout)
        aup[...] = jnp.zeros_like(aup)
        adown[...] = jnp.zeros_like(adown)
        vecg_ref[...] = jnp.zeros_like(vecg_ref)
        bupg_ref[...] = jnp.zeros_like(bupg_ref)
        for c in copies:
            c.wait()

    acc[...] = accin_ref[...].astype(f32) + mid_ref[...] + vec_ref[3:4, :]
    gh2[...] = gh2in_ref[...].astype(f32)
    cot = cot_ref[0]
    mlp_chunks(hid_ref[0], cot, wup, wdown, bup_ref, acc, gh2, aup, adown, bupg_ref)
    out_ref[0] = acc[0].astype(bf16)
    grad_hidden = gh2[0]
    normed, inv = normalize(mid_ref[0])
    cotf = cot.astype(f32)
    gmid = cotf + norm_back(grad_hidden, normed, inv, vec_ref[1:2, :])
    gmid_ref[0] = gmid
    branch = gmid.astype(bf16)
    vecg_ref[0:1, :] += col_sum(branch.astype(f32))
    vecg_ref[1:2, :] += col_sum(grad_hidden * normed)
    vecg_ref[2:3, :] += col_sum(grad_hidden)
    vecg_ref[3:4, :] += col_sum(cotf)
    aout[...] += dg(mix_ref[0], branch, 0, 0)
    gmix = dg(branch, wout[...], 1, 1).astype(bf16)
    gmix_ref[0] = gmix
    gmixT_ref[0] = gmix.T

    @pl.when(i == pl.num_programs(0) - 1)
    def _():
        wout[...] = aout[...].astype(bf16)
        wup[...] = aup[...].astype(bf16)
        wdown[...] = adown[...].astype(bf16)
        at = pl.multiple_of(core * hd, 128)
        rest = pl.multiple_of((1 - core) * hd, 128)
        extra = [
            (wout.at[:, pl.ds(at, hd)], keep_ref.at[:, pl.ds(H, hd)]),
            (wout.at[:, pl.ds(rest, hd)], send_ref.at[:, pl.ds(H, hd)]),
        ]
        mlp_store(core, wup, wdown, keep_ref, send_ref, extra, sems)


def mlp_specs(tokens, tile):
    B, S, D = tokens.shape
    per = S // tile
    row = pl.BlockSpec((1, tile, D), lambda i: (i // per, i % per, 0))
    col = pl.BlockSpec((1, D, tile), lambda i: (i // per, 0, i % per))
    one = pl.BlockSpec((1, 1, D), lambda i: (i // per, 0, 0))
    return row, col, one, pl.BlockSpec(memory_space=pl.ANY), pl.BlockSpec(memory_space=pltpu.SMEM)


def whole(shape):
    return pl.BlockSpec(shape, lambda i: (0,) * len(shape))


def mlp_first(core, tokens, trow, cot, mixed, vec, bup, weights):
    B, S, D = tokens.shape
    H = bup.shape[1]
    row, col, one, anyspec, smem = mlp_specs(tokens, MT)
    sds = jax.ShapeDtypeStruct
    return pl.pallas_call(
        mlp_first_kernel,
        grid=(B * S // MT,),
        in_specs=[smem, row, one, row, row, whole(vec.shape), whole(bup.shape), anyspec],
        out_specs=[row, row, row, row, whole((1, H)), anyspec, anyspec],
        out_shape=[sds((B, S, D), bf16)] * 2 + [sds((B, S, D), f32), sds((B, S, D), bf16), sds((1, H), f32)] + [sds((D, H), bf16)] * 2,
        scratch_shapes=[
            pltpu.VMEM((D, D), bf16),
            pltpu.VMEM((D, H), bf16),
            pltpu.VMEM((H, D), bf16),
            pltpu.VMEM((D, H), f32),
            pltpu.VMEM((H, D), f32),
            pltpu.VMEM((1, MT, D), f32),
            pltpu.VMEM((1, MT, D), f32),
            pltpu.SemaphoreType.DMA((2 + H // D,)),
        ],
        compiler_params=params(),
        cost_estimate=pl.CostEstimate(flops=13 * B * S * D * H, bytes_accessed=60 * 10**6, transcendentals=0),
        name="mlp_first",
    )(core, tokens, trow, cot, mixed, vec, bup, weights)


def mlp_second(core, acc, gh2, mid, hid, cot, mixed, vec, bup, wfirst, weights):
    B, S, D = cot.shape
    H = bup.shape[1]
    row, col, one, anyspec, smem = mlp_specs(cot, MT2)
    sds = jax.ShapeDtypeStruct
    wide = sds((D, H + D // 2), bf16)
    return pl.pallas_call(
        mlp_second_kernel,
        grid=(B * S // MT2,),
        in_specs=[smem] + [row] * 6 + [whole(vec.shape), whole(bup.shape), anyspec, anyspec],
        out_specs=[row, row, row, col, whole((4, D)), whole((1, H)), anyspec, anyspec],
        out_shape=[
            sds((B, S, D), bf16),
            sds((B, S, D), f32),
            sds((B, S, D), bf16),
            sds((B, D, S), bf16),
            sds((4, D), f32),
            sds((1, H), f32),
            wide,
            wide,
        ],
        scratch_shapes=[
            pltpu.VMEM((D, D), bf16),
            pltpu.VMEM((D, H), bf16),
            pltpu.VMEM((H, D), bf16),
            pltpu.VMEM((D, D), f32),
            pltpu.VMEM((D, H), f32),
            pltpu.VMEM((H, D), f32),
            pltpu.VMEM((1, MT2, D), f32),
            pltpu.VMEM((1, MT2, D), f32),
            pltpu.SemaphoreType.DMA((3 + H // D,)),
        ],
        compiler_params=params(),
        cost_estimate=pl.CostEstimate(flops=14 * B * S * D * H, bytes_accessed=60 * 10**6, transcendentals=0),
        name="mlp_second",
    )(core, acc, gh2, mid, hid, cot, mixed, vec, bup, wfirst, weights)


def qkv_weights_kernel(core_ref, hid_ref, dq_ref, dk_ref, dv_ref, keep_ref, send_ref, aw_ref, low_ref, sems):
    b = pl.program_id(0)
    i = pl.program_id(1)
    core = core_ref[0]
    D = hid_ref.shape[2]

    @pl.when((b == 0) & (i == 0))
    def _():
        aw_ref[...] = jnp.zeros_like(aw_ref)

    for n, g in enumerate((dq_ref[0], dk_ref[0], dv_ref[0])):
        aw_ref[:, n * D : (n + 1) * D] += dg(hid_ref[0], g, 0, 0)

    @pl.when((b == pl.num_programs(0) - 1) & (i == pl.num_programs(1) - 1))
    def _():
        low_ref[...] = aw_ref[...].astype(bf16)
        half = keep_ref.shape[1]
        at = pl.multiple_of(core * half, 128)
        rest = pl.multiple_of((1 - core) * half, 128)
        copies = (
            pltpu.make_async_copy(low_ref.at[:, pl.ds(at, half)], keep_ref, sems.at[0]),
            pltpu.make_async_copy(low_ref.at[:, pl.ds(rest, half)], send_ref, sems.at[1]),
        )
        for c in copies:
            c.start()
        for c in copies:
            c.wait()


def qkv_weights_call(core, hid, dq, dk, dv):
    B, S, D = hid.shape
    row = pl.BlockSpec((1, RT, D), lambda b, i: (b, i, 0))
    anyspec = pl.BlockSpec(memory_space=pl.ANY)
    half = jax.ShapeDtypeStruct((D, 3 * D // 2), bf16)
    return pl.pallas_call(
        qkv_weights_kernel,
        grid=(B, S // RT),
        in_specs=[pl.BlockSpec(memory_space=pltpu.SMEM), row, row, row, row],
        out_specs=[anyspec, anyspec],
        out_shape=[half, half],
        scratch_shapes=[pltpu.VMEM((D, 3 * D), f32), pltpu.VMEM((D, 3 * D), bf16), pltpu.SemaphoreType.DMA((2,))],
        compiler_params=params(),
        cost_estimate=pl.CostEstimate(flops=6 * B * S * D * D, bytes_accessed=20 * 10**6, transcendentals=0),
        name="qkv_weights",
    )(core, hid, dq, dk, dv)


def qkv_back_kernel(core_ref, tok_ref, row_ref, gmid_ref, dq_ref, dk_ref, dv_ref, vec_ref, mine_ref, other_ref, after_ref,
                    gin_ref, rsum_ref, vecg_ref, w_ref, sems):
    b = pl.program_id(0)
    i = pl.program_id(1)

    @pl.when((b == 0) & (i == 0))
    def _():
        copies = place_halves(mine_ref, other_ref, w_ref, core_ref[0], sems)
        for c in copies:
            c.start()
        vecg_ref[...] = jnp.zeros_like(vecg_ref)
        for c in copies:
            c.wait()

    @pl.when(i == 0)
    def _():
        rsum_ref[...] = jnp.zeros_like(rsum_ref)

    grads = (dq_ref[0], dk_ref[0], dv_ref[0])
    grad_hidden = dg(jnp.concatenate(grads, axis=1), w_ref[...], 1, 1)
    base = tok_ref[0].astype(f32) + row_ref[0]
    normed, inv = normalize(base)
    gbase = gmid_ref[0] + norm_back(grad_hidden, normed, inv, vec_ref[0:1, :])
    gin_ref[0] = gbase.astype(bf16)
    rsum_ref[0] += col_sum(gbase)
    vecg_ref[0:1, :] += col_sum(grad_hidden * normed)
    vecg_ref[1:2, :] += col_sum(grad_hidden)
    vecg_ref[2:3, :] += col_sum(grads[0].astype(f32))
    vecg_ref[3:4, :] += col_sum(grads[2].astype(f32))


def qkv_back_call(core, tokens, trow, gmid, dq, dk, dv, vec, mine, other, after):
    B, S, D = tokens.shape
    row = pl.BlockSpec((1, RT, D), lambda b, i: (b, i, 0))
    seq = pl.BlockSpec((1, 1, D), lambda b, i: (b, 0, 0))
    anyspec = pl.BlockSpec(memory_space=pl.ANY)
    sds = jax.ShapeDtypeStruct
    return pl.pallas_call(
        qkv_back_kernel,
        grid=(B, S // RT),
        in_specs=[
            pl.BlockSpec(memory_space=pltpu.SMEM),
            row,
            seq,
            row,
            row,
            row,
            row,
            pl.BlockSpec(vec.shape, lambda b, i: (0, 0)),
            anyspec,
            anyspec,
            anyspec,
        ],
        out_specs=[row, seq, pl.BlockSpec((4, D), lambda b, i: (0, 0))],
        out_shape=[sds((B, S, D), bf16), sds((B, 1, D), f32), sds((4, D), f32)],
        scratch_shapes=[pltpu.VMEM((D, 3 * D), bf16), pltpu.SemaphoreType.DMA((2,))],
        compiler_params=params(),
        cost_estimate=pl.CostEstimate(flops=6 * B * S * D * D, bytes_accessed=40 * 10**6, transcendentals=0),
        name="norm_qkv_back",
    )(core, tokens, trow, gmid, dq, dk, dv, vec, mine, other, after)


def key_ranges(segment_ids):
    B, S = segment_ids.shape
    tiles = segment_ids.reshape(B, S // QT, QT)
    before = jnp.sum((segment_ids[:, None, :] < tiles[:, :, :1]).astype(jnp.int32), axis=-1)
    upto = jnp.sum((segment_ids[:, None, :] <= tiles[:, :, -1:]).astype(jnp.int32), axis=-1)
    return (before // KT).reshape(-1), ((upto + KT - 1) // KT).reshape(-1)


def own_slice(array, index, size, axis):
    return lax.dynamic_slice_in_dim(array, index * size, size, axis)


def swap(array, axis):
    return lax.ppermute(array, axis, [(0, 1), (1, 0)])


def all_sum(array, axis):
    size = lax.axis_size(axis)
    step = 1
    while step < size:
        came = lax.ppermute(array, axis, [(i, i ^ step) for i in range(size)])
        array = (array.astype(f32) + came.astype(f32)).astype(array.dtype)
        step *= 2
    return array


def gather_small(array, axis):
    size, me = lax.axis_size(axis), lax.axis_index(axis)
    step = 1
    while step < size:
        came = lax.ppermute(array, axis, [(i, i ^ step) for i in range(size)])
        low = (me & step) == 0
        array = jnp.concatenate([jnp.where(low, array, came), jnp.where(low, came, array)], axis=0)
        step *= 2
    return array


def scatter_small(array, axis):
    size, me = lax.axis_size(axis), lax.axis_index(axis)
    step = size // 2
    while step >= 1:
        half = array.shape[0] // 2
        low = (me & step) == 0
        keep = jnp.where(low, array[:half], array[half:])
        send = jnp.where(low, array[half:], array[:half])
        array = keep + lax.ppermute(send, axis, [(i, i ^ step) for i in range(size)])
        step //= 2
    return array


EXTRA = 8


def split_rows(values, width):
    high = lax.reduce_precision(values, 8, 7)
    parts = jnp.concatenate([high, values - high], axis=-2).astype(bf16)
    pad = [(0, 0)] * (parts.ndim - 1) + [(0, width - parts.shape[-1])]
    return jnp.pad(parts, pad)


def exchange_reduce(array, extra, axis):
    size = lax.axis_size(axis)
    rows, width = array.shape[0] // size, array.shape[1]
    extra = jnp.pad(extra, ((0, 0), (0, EXTRA - extra.shape[1]), (0, 0)))
    sent = jnp.concatenate([array.reshape(size, rows, width), extra], axis=1)
    came = lax.all_to_all(sent.reshape(size * (rows + EXTRA), width), axis, 0, 0, tiled=True)
    came = came.reshape(size, rows + EXTRA, width)
    return jnp.sum(came[:, :rows].astype(f32), axis=0).astype(bf16), came[:, rows:].astype(f32)


def direct_exchange(array, axis):
    size, me = lax.axis_size(axis), lax.axis_index(axis)
    came = [own_slice(array, me, 1, 0)]
    for r in range(1, size):
        came.append(lax.ppermute(own_slice(array, me ^ r, 1, 0), axis, [(i, i ^ r) for i in range(size)]))
    return jnp.concatenate(came, axis=0)


def on_device(
    tokens,
    cot,
    segment_ids,
    block_map,
    timesteps,
    step_table,
    ln1_gain,
    ln1_bias,
    w_query,
    b_query,
    w_key,
    w_value,
    b_value,
    w_out,
    b_out,
    ln2_gain,
    ln2_bias,
    w_up,
    b_up,
    w_down,
    b_down,
):
    B, S, D = tokens.shape
    n = lax.axis_size("shard")
    me = lax.axis_index("shard")
    core = lax.axis_index("core")
    own = ln1_gain.shape[0]
    FF = b_up.shape[0] * n
    hd = D // 2
    core1 = core.reshape(1).astype(jnp.int32)

    H = FF // 2
    J = FF // D
    thin = own // 2
    qkv_local = own_slice(jnp.concatenate([w_query, w_key, w_value], axis=1), core, 3 * hd, 1)
    qkv_mine = lax.all_gather(qkv_local, "shard", axis=0, tiled=True)
    up_core = own_slice(w_up, core, thin, 0).reshape(thin, n, 2, J, thin)
    up_core = up_core.transpose(0, 3, 1, 2, 4).reshape(thin, FF)
    out_core = own_slice(w_out, core, thin, 0)
    down_core = own_slice(w_down, core, J * thin, 0)
    down_core = [down_core[j * thin : (j + 1) * thin] for j in range(J)]
    local_a = jnp.concatenate([out_core, up_core[:, :H]] + down_core[: J // 2], axis=1)
    local_b = jnp.concatenate([up_core[:, H:]] + down_core[J // 2 :], axis=1)

    small = (ln1_gain, ln1_bias, b_query, b_value, b_out, ln2_gain, ln2_bias, b_down, b_up)
    small = jnp.concatenate([v.astype(f32) for v in small] + [timesteps.astype(f32)])
    packed = gather_small(small[None], "shard")
    g1, s1, bq, bv, bo, g2, s2, bd = [packed[:, i * own : (i + 1) * own].reshape(1, D) for i in range(8)]
    width = 8 * own + FF // n
    bup = packed[:, 8 * own : width].reshape(n, 2, J, thin).transpose(2, 0, 1, 3).reshape(1, FF)
    group = packed[:, width:].reshape(n * B, 1).astype(jnp.int32)
    vec1 = jnp.concatenate([g1, s1], axis=0)
    bias = jnp.concatenate([bq, jnp.zeros_like(bq), bv], axis=1)
    vec2 = jnp.concatenate([bo, g2, s2, bd], axis=0)

    own_rows = step_table.shape[0]
    spots = me * own_rows + lax.broadcasted_iota(jnp.int32, (1, own_rows), 1)
    found = jnp.dot((group == spots).astype(bf16), step_table, preferred_element_type=f32)
    trow = scatter_small(found, "shard").reshape(B, 1, D)
    qkv_mine, trow, vec1 = lax.optimization_barrier((qkv_mine, trow, vec1))
    qkv_other = swap(qkv_mine, "core")
    local_a, qkv_mine = lax.optimization_barrier((local_a, qkv_mine))
    w_a = lax.all_gather(local_a, ("shard", "core"), axis=0, tiled=True)

    lo, hi = key_ranges(segment_ids)
    segk = jnp.broadcast_to(segment_ids[:, :, None], (B, S, 128))
    segq = segment_ids[:, None, :]

    q, k, v, qT, kT, vT, hid1 = qkv_call(core1, tokens, trow, vec1, bias, qkv_mine, qkv_other)
    mixed, mixedT, prob, fac = attn_fwd(lo, hi, q, k, vT, segk, segq)
    local_b, w_a, mixed = lax.optimization_barrier((local_b, w_a, mixed))
    w_b = lax.all_gather(local_b, ("shard", "core"), axis=0, tiled=True)
    def core_sum(keep, send):
        return (keep.astype(f32) + swap(send, "core").astype(f32)).astype(bf16)

    def two(half, other):
        half, other = half.astype(f32), other.astype(f32)
        return jnp.where(core == 0, half, other), jnp.where(core == 0, other, half)

    def finish(part):
        half = all_sum(part, "xrep")
        return two(half, swap(half, "core"))

    acc, gh2, mid, hid, bupg_a, keep, send = mlp_first(core1, tokens, trow, cot, mixed, vec2, bup[:, :H], w_a)
    half_a = core_sum(keep, send)
    part_a = lax.all_to_all(half_a, "shard", 0, 0, tiled=True).reshape(n, own, H)
    part_a = jnp.sum(part_a.astype(f32), axis=0).astype(bf16)
    acc, half_a = lax.optimization_barrier((acc, half_a))
    out, gmid, gmix, gmixT, vecg2, bupg_b, keep, send = mlp_second(
        core1, acc, gh2, mid, hid, cot, mixed, vec2, bup[:, H:], w_a, w_b
    )
    half_b = core_sum(keep, send)
    half_b, part_a = lax.optimization_barrier((half_b, part_a))
    bupg = jnp.concatenate([bupg_a, bupg_b], axis=1)
    bupg = bupg.reshape(J, n, 2, thin).transpose(1, 2, 0, 3).reshape(n, FF // n)
    vectors = jnp.concatenate([vecg2[i].reshape(n, own) for i in range(4)] + [bupg], axis=1)
    part_b, came_b = exchange_reduce(half_b, split_rows(vectors[:, None], half_b.shape[1]), "shard")
    dq, dk, dv = attn_bwd(lo, hi, qT, kT, v, gmix, gmixT, mixedT, prob, fac, half_b)
    part_a = all_sum(part_a, "xrep")
    dq, part_a = lax.optimization_barrier((dq, part_a))
    other_a = swap(part_a, "core")
    keep, send = qkv_weights_call(core1, hid1, dq, dk, dv)
    keep, other_a = lax.optimization_barrier((keep, other_a))
    qkv_half = core_sum(keep, send)
    qkv_half, part_b, came_b = lax.optimization_barrier((qkv_half, part_b, came_b))
    came = lax.all_to_all(qkv_half, "shard", 0, 0, tiled=True).reshape(n, own, 3 * hd)
    qkv_part = jnp.sum(came.astype(f32), axis=0).astype(bf16)
    gin, rsum, vecg1 = qkv_back_call(
        core1, tokens, trow, gmid, dq, dk, dv, vec1, qkv_mine, qkv_other, qkv_half
    )
    part_b, part_a, other_a, vecg1 = lax.optimization_barrier((part_b, part_a, other_a, vecg1))
    vectors = jnp.concatenate([vecg1[i].reshape(n, own) for i in range(4)], axis=1)
    thick = -(-(D + 2) // 128) * 128
    digits = jnp.stack([timesteps // 32, timesteps % 32], axis=1).astype(f32)
    table_rows = jnp.concatenate([rsum.reshape(B, D), digits], axis=1)
    table_rows = jnp.broadcast_to(jnp.pad(table_rows, ((0, 0), (0, thick - D - 2)))[None], (n, B, thick))
    vectors = jnp.pad(vectors, ((0, 0), (0, thick - 4 * own)))[:, None]
    came_q = direct_exchange(jnp.concatenate([table_rows, vectors], axis=1), "shard")
    came_q, qkv_part = lax.optimization_barrier((came_q, qkv_part))

    vg_b = jnp.sum(came_b[:, :2], axis=(0, 1))[: 4 * own + FF // n]
    vg_q = jnp.sum(came_q[:, B], axis=0)[: 4 * own]
    vg = jnp.concatenate([vg_q, vg_b])
    lines = -(-vg.shape[0] // thick)
    vg = jnp.pad(vg, (0, lines * thick - vg.shape[0])).reshape(lines, thick)
    sums = jnp.concatenate([came_q[:, :B].reshape(n * B, thick), vg], axis=0)[None]
    for axis in ("core", "xrep"):
        sums = gather_small(sums, axis)
    vg = jnp.sum(sums[:, n * B :], axis=0).reshape(-1)
    sums = sums[:, : n * B].reshape(-1, thick)
    g_bup = vg[8 * own : 8 * own + FF // n]
    vg = [vg[i * own : (i + 1) * own] for i in range(8)]
    own_rows = step_table.shape[0]
    rows = me * own_rows + lax.broadcasted_iota(jnp.int32, (own_rows, 1), 0)
    steps = 32 * sums[:, D] + sums[:, D + 1]
    match = (rows == steps.astype(jnp.int32)[None, :]).astype(f32)
    g_table = jnp.dot(match, sums[:, :D], precision=lax.Precision.HIGHEST, preferred_element_type=f32)

    a_up, a_down = two(part_a, other_a)
    b_up_, b_down_ = finish(part_b)
    g_up = jnp.concatenate([a_up, b_up_[:, :H]], axis=1)
    g_up = g_up.reshape(own, J, n, 2, thin).transpose(0, 2, 3, 1, 4).reshape(own, FF)
    blocks = jnp.concatenate([a_down, b_down_[:, :H]], axis=1).reshape(2, thin, J, D)
    g_down = blocks.transpose(0, 2, 1, 3).reshape(FF // n, D)
    g_out = jnp.concatenate([b_up_[:, H:], b_down_[:, H:]], axis=1)
    q_left, q_right = finish(qkv_part)
    g_qkv = jnp.concatenate([q_left, q_right], axis=1)
    g_q, g_k, g_v = g_qkv[:, :D], g_qkv[:, D : 2 * D], g_qkv[:, 2 * D :]
    return (
        out, gin, g_table, vg[0], vg[1], g_q, vg[2], g_k, g_v, vg[3], g_out, vg[4], vg[5], vg[6], g_up, g_bup, g_down, vg[7],
    )


def solution(mesh):
    rep, shard = mesh.shape["rep"], mesh.shape["shard"]
    fine = Mesh(mesh.devices.reshape(rep // 2, 2, shard), ("xrep", "core", "shard"))
    seqs = ("xrep", "core", "shard")
    mat, vec = P("shard", None), P("shard")
    rows3, rows2 = P(seqs, None, None), P(seqs, None)
    weights = (mat, vec, vec, mat, vec, mat, mat, vec, mat, vec, vec, vec, mat, vec, mat, vec)
    return jax.shard_map(
        on_device,
        mesh=fine,
        in_specs=(rows3, rows3, rows2, rows3, P(seqs)) + weights,
        out_specs=(rows3, rows3) + weights,
        check_vma=False,
    )
```
